256 devices in a mesh: users: 32 (over y, z), items: 8 (over x, core).
Axes of the slice: x: 4, y: 4, z: 8, core: 2. Of those that a mesh axis runs over, the one named last changes fastest.
Arguments:
- item_ids: int32 [2048, 8, 128], P(('users', 'items')), may hold values from 0 to 65535, as said below
- clicks: int32 [2048, 8, 128], P(('users', 'items')), may hold values from 1 to 8
- block_counts: int32 [2048], P(('users', 'items')), may hold values from 1 to 8, as said below
- user_shape0: float32 [2048, 128], P(('users', 'items')), may hold values from 0.5 to 5
- user_rate0: float32 [2048, 128], P(('users', 'items')), may hold values from 0.5 to 5
- item_shape: float32 [65536, 128], P('users'), may hold values from 0.1 to 3
- item_rate: float32 [65536, 128], P('users'), may hold values from 0.5 to 5
- beta_totals: float32 [128], replicated, may hold values from 5 to 50
- covariates: float32 [512, 65536], P('items', 'users'), may hold values from -6 to 6
- cov_weight: float32 [512, 128], P('items'), may hold values from -0.125 to 0.125
Outputs:
- user_shape: float32 [2048, 128], P(('users', 'items'))
- user_rate: float32 [2048, 128], P(('users', 'items'))
- activity_rate: float32 [2048], P(('users', 'items'))
- item_shape_new: float32 [65536, 128], P(('users', 'items'))
- cov_grad: float32 [512, 128], P('items')
The draws below stay inside these ranges and needn't reach their ends.
Inputs may be any that keep to these rules, and one draw needn't show every extreme that they name: `item_ids`: item i belongs to owner i // 2048. In each aligned block of 8 users (one device's users), the slots name items of every owner exactly 256 times; items may repeat. `block_counts`: some user in every draw has 8 live blocks; blocks at or after a user's count are padding. Counts are skewed; about half of all block slots are live.
All inputs are finite; a program needn't handle non-finite values.
Results may differ from the reference program's by a relative error of at most 0.0001.
Values sent between devices are 32-bit elements; how exact they have to be, the bound alone decides.
No kernel may reach another device: no remote copies, remote signals or barrier semaphores. Data moves between devices by JAX's collectives and lax.ppermute only.
A program may use at most 64 MiB of HBM per device.

```python
import math
import jax
import jax.numpy as jnp
from jax import lax

FACTORS = 128
COVARS = 512
BLOCK = 128
MAX_BLOCKS = 8
USER_DEV = 8
ITEM_DEV = 2048
ITERS = 3
USER_RATIO = 4
USERS = 2048
OWNERS = 32
ITEMS = 65536


def draw_item_ids(key, part):
    slot_count = USER_DEV * MAX_BLOCKS * BLOCK
    device_count = USERS // USER_DEV
    per_owner = slot_count // OWNERS
    owner_key, row_key = jax.random.split(jax.random.fold_in(key, 11))
    base_owners = jnp.tile(jnp.arange(OWNERS, dtype=jnp.int32), per_owner)
    device_keys = jax.random.split(owner_key, device_count)
    owner_table = jax.vmap(lambda single: jax.random.permutation(single, base_owners))(device_keys)
    row_table = jax.random.randint(row_key, (device_count, slot_count), 0, ITEM_DEV, dtype=jnp.int32)
    return (owner_table * ITEM_DEV + row_table).reshape(USERS, MAX_BLOCKS, BLOCK).astype(jnp.int32)


def draw_block_counts(key, part):
    first_key, second_key, pick_key = jax.random.split(jax.random.fold_in(key, 23), 3)
    first_draw = jax.random.randint(first_key, (USERS,), 0, MAX_BLOCKS, dtype=jnp.int32)
    second_draw = jax.random.randint(second_key, (USERS,), 0, MAX_BLOCKS, dtype=jnp.int32)
    counts = MAX_BLOCKS // 4 + 1 + first_draw * second_draw // (MAX_BLOCKS + 2)
    counts = jnp.minimum(counts, MAX_BLOCKS)
    chosen = jax.random.randint(pick_key, (), 0, USERS, dtype=jnp.int32)
    counts = jnp.where(jnp.arange(USERS, dtype=jnp.int32) == chosen, MAX_BLOCKS, counts)
    return counts.astype(jnp.int32)


def place_ends(drawn, own_key, low, high):
    longest = drawn.shape.index(max(drawn.shape))
    spots = []
    for shift in (0, 1):
        where = [jax.random.randint(jax.random.fold_in(own_key, axis), (), 0, length) for axis, length in enumerate(drawn.shape)]
        where[longest] = (where[longest] + shift) % drawn.shape[longest]
        spots.append(tuple(where))
    return drawn.at[spots[0]].set(low).at[spots[1]].set(high)


def shard_levels(own_key, shape, cuts, least, top_value):
    def one(dim, parts):
        heights = jax.random.uniform(jax.random.fold_in(jax.random.fold_in(own_key, 6), dim), (parts,), jnp.float32, least / len(cuts), top_value / len(cuts))
        return jnp.repeat(jnp.exp(heights), shape[dim] // parts).reshape((-1,) + (1,) * (len(shape) - dim - 1))

    factor_of = one(*cuts[0])
    for cut in cuts[1:]:
        factor_of = factor_of * one(*cut)
    return factor_of


def scatter_about(key, dims, scale, reach, shards=(), kind=jnp.bfloat16):
    array = scale * jax.random.normal(key, dims, jnp.float32)
    if shards:
        array = array * shard_levels(key, dims, shards, -0.22, 0.18)
    return jnp.clip(array, -reach, reach).astype(kind)


def setup_inputs(seed: int = 0) -> dict:
    key_of = jax.random.split(jax.random.key(seed), 11)
    item_ids = draw_item_ids(jax.random.fold_in(key_of[10], 71), 0)
    clicks = place_ends(jax.random.randint(key_of[1], (USERS, MAX_BLOCKS, BLOCK), 1, 9), jax.random.fold_in(key_of[1], 1), 1, 8).astype(jnp.int32)
    block_counts = draw_block_counts(jax.random.fold_in(key_of[10], 71), 0)
    user_shape0 = jnp.clip(jnp.exp(math.log(5.0) - 2.3025851 * jax.random.uniform(key_of[3], (USERS, FACTORS), jnp.float32) ** shard_levels(key_of[3], (USERS, FACTORS), ((0, 256),), -0.2, 0.2)), 0.5, 5.0)
    user_rate0 = jnp.clip(jnp.exp(math.log(5.0) - 2.3025851 * jax.random.uniform(key_of[4], (USERS, FACTORS), jnp.float32) ** shard_levels(key_of[4], (USERS, FACTORS), ((0, 256),), -0.2, 0.2)), 0.5, 5.0)
    item_shape = jnp.clip(jnp.exp(math.log(3.0) - 3.4011974 * jax.random.uniform(key_of[5], (ITEMS, FACTORS), jnp.float32) ** shard_levels(key_of[5], (ITEMS, FACTORS), ((0, 32),), -0.2, 0.2)), 0.1, 3.0)
    item_rate = jnp.clip(jnp.exp(math.log(5.0) - 2.3025851 * jax.random.uniform(key_of[6], (ITEMS, FACTORS), jnp.float32) ** shard_levels(key_of[6], (ITEMS, FACTORS), ((0, 32),), -0.2, 0.2)), 0.5, 5.0)
    beta_totals = jnp.clip(jnp.exp(jax.random.uniform(key_of[7], (FACTORS,), jnp.float32, math.log(5.0), math.log(50.0))), 5.0, 50.0)
    covariates = scatter_about(key_of[8], (COVARS, ITEMS), 1.0, 6.0, ((0, 8), (1, 32)), jnp.float32)
    cov_weight = scatter_about(key_of[9], (COVARS, FACTORS), (4 * COVARS) ** -0.5, 0.125, ((0, 8),), jnp.float32)
    return dict(item_ids=item_ids, clicks=clicks, block_counts=block_counts, user_shape0=user_shape0, user_rate0=user_rate0, item_shape=item_shape, item_rate=item_rate, beta_totals=beta_totals, covariates=covariates, cov_weight=cov_weight)


user_prior = 0.3
activity_prior = 0.3
activity_base = 1.0
item_prior = 0.3
step_weight = 0.5

def expect_log(shapes, rates):
    return lax.digamma(shapes) - jnp.log(rates)

def ascend(shape_start, rate_start, blocks_log, weights, totals):
    factors = shape_start.shape[1]
    activity_shape = activity_prior + factors * user_prior
    activity = activity_base + lax.optimization_barrier(jnp.sum(shape_start / rate_start, axis=-1))
    shapes, rates = (shape_start, rate_start)
    alloc = None
    for iteration in range(ITERS):
        log_terms = expect_log(shapes, rates)[:, None, :] + blocks_log
        exp_terms = jnp.exp(log_terms)
        alloc = exp_terms / lax.optimization_barrier(jnp.sum(exp_terms, axis=-1, keepdims=True))
        shapes = user_prior + lax.optimization_barrier(jnp.sum(weights[:, :, None] * alloc, axis=1))
        rates = (activity_shape / activity)[:, None] + totals[None, :]
        activity = activity_base + lax.optimization_barrier(jnp.sum(shapes / rates, axis=-1))
    return (shapes, rates, activity, weights[:, :, None] * alloc)

def reference(item_ids, clicks, block_counts, user_shape0, user_rate0, item_shape, item_rate, beta_totals, covariates, cov_weight):
    elog_items = expect_log(item_shape, item_rate)
    live_mask = (jnp.arange(MAX_BLOCKS, dtype=jnp.int32)[None, :] < block_counts[:, None]).astype(jnp.float32)
    weights = (clicks.astype(jnp.float32) * live_mask[:, :, None]).reshape(USERS, MAX_BLOCKS * BLOCK)
    flat_ids = item_ids.reshape(USERS, MAX_BLOCKS * BLOCK)
    groups = USERS // USER_DEV
    group_ids = flat_ids.reshape(groups, USER_DEV, MAX_BLOCKS * BLOCK)
    group_weights = weights.reshape(groups, USER_DEV, MAX_BLOCKS * BLOCK)
    group_shape = user_shape0.reshape(groups, USER_DEV, FACTORS)
    group_rate = user_rate0.reshape(groups, USER_DEV, FACTORS)

    def one_group(stats, inputs):
        ids_here, weights_here, shape_here, rate_here = inputs
        blocks_log = elog_items[ids_here]
        shapes, rates, activity, item_stats = ascend(shape_here, rate_here, blocks_log, weights_here, beta_totals)
        stats = stats.at[ids_here.reshape(-1)].add(item_stats.reshape(-1, FACTORS))
        return (stats, (shapes, rates, activity))
    start_stats = jnp.zeros((ITEMS, FACTORS), jnp.float32)
    stats, (shapes, rates, activity) = lax.scan(one_group, start_stats, (group_ids, group_weights, group_shape, group_rate))
    user_shape = shapes.reshape(USERS, FACTORS)
    user_rate = rates.reshape(USERS, FACTORS)
    activity_rate = activity.reshape(USERS)
    item_shape_new = (1.0 - step_weight) * item_shape + step_weight * (item_prior + USER_RATIO * stats)
    prior_log = lax.dot_general(covariates, cov_weight, (((0,), (0,)), ((), ())), precision=lax.Precision.HIGHEST, preferred_element_type=jnp.float32)
    item_score = item_prior - jnp.exp(prior_log) * item_shape_new / item_rate
    cov_grad = jnp.dot(covariates, item_score, precision=lax.Precision.HIGHEST, preferred_element_type=jnp.float32) / jnp.sqrt(jnp.float32(ITEMS))
    return (user_shape, user_rate, activity_rate, item_shape_new, cov_grad)
```

```python
import functools

import jax
import jax.numpy as jnp
from jax import lax
from jax.experimental import pallas as pl
from jax.experimental.pallas import tpu as pltpu
from jax.sharding import Mesh
from jax.sharding import PartitionSpec as P

ITERS = 3
USER_RATIO = 4

user_prior = 0.3
activity_prior = 0.3
activity_base = 1.0
item_prior = 0.3
step_weight = 0.5

F32 = jnp.float32
BF16 = jnp.bfloat16
HIGHEST = lax.Precision.HIGHEST
NT = (((1,), (1,)), ((), ()))
NN = (((1,), (0,)), ((), ()))
TN = (((0,), (0,)), ((), ()))
LANES = 128
VMEM_LIMIT = 48 * 1024 * 1024


def exp_digamma_over(x, rate):
    pair = x * (x + 5.0)
    low = pair + 4.0
    high = pair + 6.0
    steps = (2.0 * x + 5.0) * (low * high + pair * (low + high)) / (pair * low * high)
    y = x + 6.0
    inv = 1.0 / y
    sq = inv * inv
    tail = 0.5 * inv + sq * (1.0 / 12.0 - sq * (1.0 / 120.0 - sq * (1.0 / 252.0)))
    return y * jnp.exp(-steps - tail) / rate


def kernel_call(kernel, out_shape, **specs):
    return pl.pallas_call(
        kernel,
        out_shape=out_shape,
        compiler_params=pltpu.CompilerParams(vmem_limit_bytes=VMEM_LIMIT),
        **specs,
    )


def shape_of(*dims):
    return jax.ShapeDtypeStruct(dims, F32)


def prep_kernel(owners, counts_ref, ids_ref, clicks_ref, shape_ref, rate_ref, send_ref, theta_ref):
    rows = ids_ref.shape[0]
    blocks = 8
    width = 2 * LANES
    capacity = rows * LANES // owners
    before = (
        lax.broadcasted_iota(jnp.int32, (width, width), 0)
        < lax.broadcasted_iota(jnp.int32, (width, width), 1)
    )
    before = jnp.where(before, 1.0, 0.0).astype(BF16)
    owner_iota = lax.broadcasted_iota(jnp.int32, (owners, width), 0)
    rank_iota = lax.broadcasted_iota(jnp.int32, (capacity, width), 0).astype(F32)
    carry = jnp.zeros((owners, 1), F32)
    lists = jnp.zeros((3 * owners, capacity), F32)
    for chunk in range(rows // 2):
        user = 2 * chunk // blocks
        ids = jnp.concatenate(
            [ids_ref[2 * chunk : 2 * chunk + 1, :], ids_ref[2 * chunk + 1 : 2 * chunk + 2, :]], axis=1
        )
        weights = []
        for row in (2 * chunk, 2 * chunk + 1):
            live = jnp.where(row % blocks < counts_ref[user], 1.0, 0.0)
            weights.append(clicks_ref[row : row + 1, :].astype(F32) * live)
        weight = jnp.concatenate(weights, axis=1)
        marks = jnp.where(owner_iota == (ids >> 11), 1.0, 0.0)
        earlier = lax.dot_general(marks.astype(BF16), before, NN, preferred_element_type=F32)
        rank = jnp.sum(marks * (earlier + carry), axis=0, keepdims=True)
        carry = carry + jnp.sum(marks, axis=1, keepdims=True)
        place = jnp.where(rank_iota == rank, 1.0, 0.0).astype(BF16)
        high = (((ids >> 7) & 15) * 8 + user).astype(F32)
        low = (ids & 127).astype(F32)
        payload = jnp.concatenate([marks * high, marks * low, marks * weight], axis=0).astype(BF16)
        lists = lists + lax.dot_general(payload, place, NT, preferred_element_type=F32)
    theta = exp_digamma_over(shape_ref[...], rate_ref[...])
    theta_ref[...] = theta
    zeros = jnp.zeros((2, LANES), F32)
    for owner in range(owners):
        for part in range(3):
            line = lists[part * owners + owner : part * owners + owner + 1, :]
            send_ref[owner, 2 * part : 2 * part + 1, :] = line[:, :LANES]
            send_ref[owner, 2 * part + 1 : 2 * part + 2, :] = line[:, LANES:]
        send_ref[owner, 6:8, :] = zeros
        send_ref[owner, 8:16, :] = theta


def table_kernel(shape_ref, rate_ref, table_ref):
    table_ref[...] = exp_digamma_over(shape_ref[...], rate_ref[...])


def ascend_block(theta, marks, table):
    share = lax.dot_general(theta, table, NT, precision=HIGHEST, preferred_element_type=F32)
    ratio = marks / share
    return ratio, lax.dot_general(ratio, table, NN, precision=HIGHEST, preferred_element_type=F32)


def build_kernel(recv_ref, table_ref, marks_ref, partial_ref):
    owners = recv_ref.shape[0]
    highs = marks_ref.shape[0]
    line_iota = lax.broadcasted_iota(jnp.int32, (LANES, 2 * LANES), 0).astype(F32)

    def wide(source, part):
        return jnp.concatenate(
            [recv_ref[source, 2 * part : 2 * part + 1, :], recv_ref[source, 2 * part + 1 : 2 * part + 2, :]],
            axis=1,
        )

    for source in range(owners):
        left = jnp.where(line_iota == wide(source, 0), wide(source, 2), 0.0).astype(BF16)
        right = jnp.where(line_iota == wide(source, 1), 1.0, 0.0).astype(BF16)
        tile = lax.dot_general(left, right, NT, preferred_element_type=F32)
        for high in range(highs):
            marks_ref[high, 8 * source : 8 * source + 8, :] = tile[8 * high : 8 * high + 8, :]
    theta = jnp.concatenate([recv_ref[source, 8:16, :] for source in range(owners)], axis=0)
    total = jnp.zeros(theta.shape, F32)
    for high in range(highs):
        table = table_ref[high * LANES : (high + 1) * LANES, :]
        total = total + ascend_block(theta, marks_ref[high], table)[1]
    partial_ref[...] = total


def ascend_kernel(theta_ref, marks_ref, table_ref, partial_ref):
    theta = theta_ref[...]
    total = jnp.zeros(theta.shape, F32)
    for high in range(marks_ref.shape[0]):
        table = table_ref[high * LANES : (high + 1) * LANES, :]
        total = total + ascend_block(theta, marks_ref[high], table)[1]
    partial_ref[...] = total


def last_kernel(theta_ref, marks_ref, table_ref, partial_ref, stats_ref):
    theta = theta_ref[...]
    total = jnp.zeros(theta.shape, F32)
    for high in range(marks_ref.shape[0]):
        table = table_ref[high * LANES : (high + 1) * LANES, :]
        ratio, part = ascend_block(theta, marks_ref[high], table)
        total = total + part
        spread = lax.dot_general(ratio, theta, TN, precision=HIGHEST, preferred_element_type=F32)
        stats_ref[high * LANES : (high + 1) * LANES, :] = table * spread
    partial_ref[...] = total


def update_kernel(
    activity_shape, recv_ref, theta_ref, activity_ref, totals_ref, shapes_ref, rates_ref, active_ref, next_ref, send_ref
):
    total = jnp.sum(recv_ref[...], axis=0)
    shapes = user_prior + theta_ref[...] * total
    rates = activity_shape / activity_ref[...] + totals_ref[...]
    shapes_ref[...] = shapes
    rates_ref[...] = rates
    active = activity_base + jnp.sum(shapes / rates, axis=1, keepdims=True)
    active_ref[...] = jnp.broadcast_to(active, shapes.shape)
    theta = exp_digamma_over(shapes, rates)
    next_ref[...] = theta
    send_ref[...] = jnp.broadcast_to(theta[None], send_ref.shape)


def shards(
    item_ids,
    clicks,
    block_counts,
    user_shape0,
    user_rate0,
    item_shape,
    item_rate,
    beta_totals,
    covariates,
    cov_weight,
):
    y_size, z_size = lax.axis_size("y"), lax.axis_size("z")
    owners = y_size * z_size
    item_rows, factors = item_shape.shape
    users_here, blocks, block_width = item_ids.shape
    slot_rows = users_here * blocks
    highs = item_rows // LANES
    split_count = lax.axis_size(("x", "core"))
    share_rows = item_rows // split_count
    first_row = lax.axis_index(("x", "core")) * share_rows
    activity_shape = activity_prior + factors * user_prior
    user_axes = ("y", "z")
    item_axes = ("x", "core")

    def exchange(array, axes):
        return lax.all_to_all(array, axes, split_axis=0, concat_axis=0, tiled=True)

    cov_full = lax.all_gather(covariates, item_axes, axis=0, tiled=True)
    weight_full = lax.all_gather(cov_weight, item_axes, axis=0, tiled=True)

    smem = pl.BlockSpec(memory_space=pltpu.SMEM)
    vmem = pl.BlockSpec(memory_space=pltpu.VMEM)
    send, theta = kernel_call(
        functools.partial(prep_kernel, owners),
        (shape_of(owners, 16, LANES), shape_of(users_here, factors)),
        in_specs=[smem, vmem, vmem, vmem, vmem],
    )(
        block_counts,
        item_ids.reshape(slot_rows, block_width),
        clicks.reshape(slot_rows, block_width),
        user_shape0,
        user_rate0,
    )
    recv = exchange(send, user_axes)
    table = kernel_call(table_kernel, shape_of(item_rows, factors))(item_shape, item_rate)
    marks, partial = kernel_call(
        build_kernel, (shape_of(highs, owners * users_here, LANES), shape_of(owners * users_here, factors))
    )(recv, table)
    active = jnp.broadcast_to(
        activity_base + jnp.sum(user_shape0 / user_rate0, axis=1, keepdims=True), user_shape0.shape
    )
    totals = beta_totals[None, :]
    small = shape_of(users_here, factors)
    for iteration in range(ITERS - 1):
        parts = exchange(partial.reshape(owners, users_here, factors), user_axes)
        _, _, active, theta, spread = kernel_call(
            functools.partial(update_kernel, activity_shape),
            (small, small, small, small, shape_of(owners, users_here, factors)),
        )(parts, theta, active, totals)
        theta_all = exchange(spread, user_axes).reshape(owners * users_here, factors)
        if iteration < ITERS - 2:
            partial = kernel_call(ascend_kernel, shape_of(owners * users_here, factors))(
                theta_all, marks, table
            )
    partial, stats = kernel_call(
        last_kernel, (shape_of(owners * users_here, factors), shape_of(item_rows, factors))
    )(theta_all, marks, table)

    stats_here = jnp.sum(
        exchange(stats, item_axes).reshape(split_count, share_rows, factors), axis=0
    )
    shape_here = lax.dynamic_slice_in_dim(item_shape, first_row, share_rows, 0)
    rate_here = lax.dynamic_slice_in_dim(item_rate, first_row, share_rows, 0)
    cov_here = lax.dynamic_slice_in_dim(cov_full, first_row, share_rows, 1)
    prior_log = lax.dot_general(cov_here, weight_full, TN, precision=HIGHEST, preferred_element_type=F32)
    scale = jnp.exp(prior_log) / rate_here
    new_shape = (1.0 - step_weight) * shape_here + step_weight * (item_prior + USER_RATIO * stats_here)
    item_score = item_prior - scale * new_shape
    grad_part = jnp.dot(cov_here, item_score, precision=HIGHEST, preferred_element_type=F32)
    cov_rows = covariates.shape[0]
    grad_part = jnp.sum(
        exchange(grad_part, item_axes).reshape(split_count, cov_rows, factors), axis=0
    )

    by_z = partial.reshape(y_size, z_size, users_here, factors).transpose(1, 0, 2, 3)
    by_z = by_z.reshape(z_size, y_size * users_here, factors)
    both = jnp.concatenate(
        [by_z, jnp.broadcast_to(grad_part[None], (z_size, cov_rows, factors))], axis=1
    )
    both = jnp.sum(exchange(both, ("z",)), axis=0)
    user_part = both[: y_size * users_here].reshape(y_size, users_here, factors)
    grad_part = both[y_size * users_here :]
    both = jnp.concatenate(
        [user_part, jnp.broadcast_to(grad_part[None], (y_size, cov_rows, factors))], axis=1
    )
    both = jnp.sum(exchange(both, ("y",)), axis=0)
    user_shape = user_prior + theta * both[:users_here]
    user_rate = activity_shape / active + totals
    activity_rate = activity_base + jnp.sum(user_shape / user_rate, axis=1)
    cov_grad = both[users_here:] / jnp.sqrt(jnp.float32(item_rows * owners))
    return (user_shape, user_rate, activity_rate, new_shape, cov_grad)


def solution(mesh):
    fine = Mesh(mesh.devices.reshape(4, 8, 4, 2), ("y", "z", "x", "core"))
    users, items = ("y", "z"), ("x", "core")
    both = users + items
    return jax.shard_map(
        shards,
        mesh=fine,
        in_specs=(
            P(both, None, None),
            P(both, None, None),
            P(both),
            P(both, None),
            P(both, None),
            P(users, None),
            P(users, None),
            P(),
            P(items, users),
            P(items, None),
        ),
        out_specs=(
            P(both, None),
            P(both, None),
            P(both),
            P(both, None),
            P(items, None),
        ),
        check_vma=False,
    )
```

```python
import functools
import math

import jax
import jax.numpy as jnp
from jax import lax
from jax.experimental import pallas as pl
from jax.experimental.pallas import tpu as pltpu
from jax.sharding import Mesh
from jax.sharding import PartitionSpec as P

ITERS = 3
USER_RATIO = 4

user_prior = 0.3
activity_prior = 0.3
activity_base = 1.0
item_prior = 0.3
step_weight = 0.5

F32 = jnp.float32
BF16 = jnp.bfloat16
HIGHEST = lax.Precision.HIGHEST
NT = (((1,), (1,)), ((), ()))
NN = (((1,), (0,)), ((), ()))
TN = (((0,), (0,)), ((), ()))
LANES = 128
VMEM_LIMIT = 48 * 1024 * 1024


def exp_digamma_over(x, rate):
    pair = x * (x + 5.0)
    low = pair + 4.0
    high = pair + 6.0
    steps = (2.0 * x + 5.0) * (low * high + pair * (low + high)) / (pair * low * high)
    y = x + 6.0
    inv = 1.0 / y
    sq = inv * inv
    tail = 0.5 * inv + sq * (1.0 / 12.0 - sq * (1.0 / 120.0 - sq * (1.0 / 252.0)))
    return y * jnp.exp(-steps - tail) / rate


def kernel_call(kernel, out_shape, **specs):
    return pl.pallas_call(
        kernel,
        out_shape=out_shape,
        compiler_params=pltpu.CompilerParams(vmem_limit_bytes=VMEM_LIMIT),
        **specs,
    )


def shape_of(*dims):
    return jax.ShapeDtypeStruct(dims, F32)


def prep_kernel(owners, counts_ref, ids_ref, clicks_ref, shape_ref, rate_ref, send_ref, theta_ref):
    rows = ids_ref.shape[0]
    blocks = 8
    width = 2 * LANES
    capacity = rows * LANES // owners
    before = (
        lax.broadcasted_iota(jnp.int32, (width, width), 0)
        < lax.broadcasted_iota(jnp.int32, (width, width), 1)
    )
    before = jnp.where(before, 1.0, 0.0).astype(BF16)
    owner_iota = lax.broadcasted_iota(jnp.int32, (owners, width), 0)
    rank_iota = lax.broadcasted_iota(jnp.int32, (capacity, width), 0).astype(F32)
    carry = jnp.zeros((owners, 1), F32)
    lists = jnp.zeros((3 * owners, capacity), F32)
    for chunk in range(rows // 2):
        user = 2 * chunk // blocks
        ids = jnp.concatenate(
            [ids_ref[2 * chunk : 2 * chunk + 1, :], ids_ref[2 * chunk + 1 : 2 * chunk + 2, :]], axis=1
        )
        weights = []
        for row in (2 * chunk, 2 * chunk + 1):
            live = jnp.where(row % blocks < counts_ref[user], 1.0, 0.0)
            weights.append(clicks_ref[row : row + 1, :].astype(F32) * live)
        weight = jnp.concatenate(weights, axis=1)
        marks = jnp.where(owner_iota == (ids >> 11), 1.0, 0.0)
        earlier = lax.dot_general(marks.astype(BF16), before, NN, preferred_element_type=F32)
        rank = jnp.sum(marks * (earlier + carry), axis=0, keepdims=True)
        carry = carry + jnp.sum(marks, axis=1, keepdims=True)
        place = jnp.where(rank_iota == rank, 1.0, 0.0).astype(BF16)
        high = (((ids >> 7) & 15) * 8 + user).astype(F32)
        low = (ids & 127).astype(F32)
        payload = jnp.concatenate([marks * high, marks * low, marks * weight], axis=0).astype(BF16)
        lists = lists + lax.dot_general(payload, place, NT, preferred_element_type=F32)
    theta = exp_digamma_over(shape_ref[...], rate_ref[...])
    theta_ref[...] = theta
    zeros = jnp.zeros((2, LANES), F32)
    for owner in range(owners):
        for part in range(3):
            line = lists[part * owners + owner : part * owners + owner + 1, :]
            send_ref[owner, 2 * part : 2 * part + 1, :] = line[:, :LANES]
            send_ref[owner, 2 * part + 1 : 2 * part + 2, :] = line[:, LANES:]
        send_ref[owner, 6:8, :] = zeros
        send_ref[owner, 8:16, :] = theta


def table_kernel(shape_ref, rate_ref, table_ref):
    table_ref[...] = exp_digamma_over(shape_ref[...], rate_ref[...])


def split(x):
    high = x.astype(BF16)
    return high, (x - high.astype(F32)).astype(BF16)


def dot(left, right, dims):
    return lax.dot_general(left, right, dims, preferred_element_type=F32)


def ascend(theta, marks_ref, table_ref, stats_ref=None):
    factors = theta.shape[1]
    theta_high, theta_low = split(theta)
    theta_both = jnp.concatenate([theta_high, theta_low], axis=1)
    total = jnp.zeros(theta.shape, F32)
    width = 2 * LANES
    for pair in range(marks_ref.shape[0] // 2):
        rows = slice(pair * width, (pair + 1) * width)
        table = table_ref[rows, :]
        table_high, table_low = split(table)
        share = dot(theta_both, jnp.concatenate([table_high, table_high], axis=1), NT) + dot(
            theta_high, table_low, NT
        )
        marks = jnp.concatenate([marks_ref[2 * pair], marks_ref[2 * pair + 1]], axis=1)
        ratio = marks / share
        ratio_high, ratio_low = split(ratio)
        wide = dot(ratio_high, jnp.concatenate([table_high, table_low], axis=1), NN)
        total = total + (wide[:, :factors] + wide[:, factors:]) + dot(ratio_low, table_high, NN)
        if stats_ref is not None:
            wide = dot(ratio_high, theta_both, TN)
            spread = wide[:, :factors] + wide[:, factors:] + dot(ratio_low, theta_high, TN)
            stats_ref[rows, :] = table * spread
    return total


def build_kernel(recv_ref, table_ref, marks_ref, partial_ref):
    owners = recv_ref.shape[0]
    highs = marks_ref.shape[0]
    line_iota = lax.broadcasted_iota(jnp.int32, (LANES, 2 * LANES), 0).astype(F32)

    def wide(source, part):
        return jnp.concatenate(
            [recv_ref[source, 2 * part : 2 * part + 1, :], recv_ref[source, 2 * part + 1 : 2 * part + 2, :]],
            axis=1,
        )

    for source in range(owners):
        left = jnp.where(line_iota == wide(source, 0), wide(source, 2), 0.0).astype(BF16)
        right = jnp.where(line_iota == wide(source, 1), 1.0, 0.0).astype(BF16)
        tile = lax.dot_general(left, right, NT, preferred_element_type=F32)
        for high in range(highs):
            marks_ref[high, 8 * source : 8 * source + 8, :] = tile[8 * high : 8 * high + 8, :]
    theta = jnp.concatenate([recv_ref[source, 8:16, :] for source in range(owners)], axis=0)
    partial_ref[...] = ascend(theta, marks_ref, table_ref)


def ascend_kernel(theta_ref, marks_ref, table_ref, partial_ref):
    partial_ref[...] = ascend(theta_ref[...], marks_ref, table_ref)


def last_kernel(theta_ref, marks_ref, table_ref, partial_ref, stats_ref):
    partial_ref[...] = ascend(theta_ref[...], marks_ref, table_ref, stats_ref)


def update_kernel(
    activity_shape, recv_ref, theta_ref, activity_ref, totals_ref, shapes_ref, rates_ref, active_ref, next_ref, send_ref
):
    total = jnp.sum(recv_ref[...], axis=0)
    shapes = user_prior + theta_ref[...] * total
    rates = activity_shape / activity_ref[...] + totals_ref[...]
    shapes_ref[...] = shapes
    rates_ref[...] = rates
    active = activity_base + jnp.sum(shapes / rates, axis=1, keepdims=True)
    active_ref[...] = jnp.broadcast_to(active, shapes.shape)
    theta = exp_digamma_over(shapes, rates)
    next_ref[...] = theta
    send_ref[...] = jnp.broadcast_to(theta[None], send_ref.shape)


def score_kernel(stats_ref, shape_ref, scale_ref, cov_ref, new_ref, grad_ref):
    stats = jnp.sum(stats_ref[...], axis=0)
    new_shape = (1.0 - step_weight) * shape_ref[...] + step_weight * (item_prior + USER_RATIO * stats)
    new_ref[...] = new_shape
    score = item_prior - scale_ref[...] * new_shape
    parts, rows, _ = grad_ref.shape
    share = score.shape[0]
    for part in range(parts):
        grad_ref[part] = lax.dot_general(
            cov_ref[part, :, :share], score, NN, precision=HIGHEST, preferred_element_type=F32
        )


def join_kernel(grad_ref, partial_ref, send_ref):
    parts, rows, _ = send_ref.shape
    half = rows // 2
    grad = jnp.sum(grad_ref[...], axis=0)
    for part in range(parts):
        send_ref[part, :half, :] = partial_ref[part * half : (part + 1) * half, :]
        send_ref[part, half:, :] = grad


def fan_kernel(recv_ref, send_ref):
    parts, rows, _ = send_ref.shape
    total = jnp.sum(recv_ref[...], axis=0)
    half = total.shape[0] // 2
    users = half // parts
    for part in range(parts):
        send_ref[part, :users, :] = total[part * users : (part + 1) * users, :]
        send_ref[part, users:, :] = total[half:, :]


def finish_kernel(
    activity_shape, root, recv_ref, theta_ref, activity_ref, totals_ref, shapes_ref, rates_ref, active_ref, grad_ref
):
    total = jnp.sum(recv_ref[...], axis=0)
    users = theta_ref.shape[0]
    shapes = user_prior + theta_ref[...] * total[:users]
    rates = activity_shape / activity_ref[...] + totals_ref[...]
    shapes_ref[...] = shapes
    rates_ref[...] = rates
    active = activity_base + jnp.sum(shapes / rates, axis=1, keepdims=True)
    active_ref[...] = jnp.broadcast_to(active, shapes.shape)
    grad_ref[...] = total[users:] / root


def shards(
    item_ids,
    clicks,
    block_counts,
    user_shape0,
    user_rate0,
    item_shape,
    item_rate,
    beta_totals,
    covariates,
    cov_weight,
):
    y_size, z_size = lax.axis_size("y"), lax.axis_size("z")
    owners = y_size * z_size
    item_rows, factors = item_shape.shape
    users_here, blocks, block_width = item_ids.shape
    slot_rows = users_here * blocks
    highs = item_rows // LANES
    split_count = lax.axis_size(("x", "core"))
    share_rows = item_rows // split_count
    first_row = lax.axis_index(("x", "core")) * share_rows
    activity_shape = activity_prior + factors * user_prior
    user_axes = ("y", "z")
    item_axes = ("x", "core")

    def exchange(array, axes):
        return lax.all_to_all(array, axes, split_axis=0, concat_axis=0, tiled=True)

    cov_rows = covariates.shape[0]
    cov_send = jnp.concatenate(
        [
            covariates.reshape(cov_rows, split_count, share_rows).transpose(1, 0, 2),
            jnp.broadcast_to(cov_weight[None], (split_count, cov_rows, factors)),
        ],
        axis=2,
    )
    cov_recv = exchange(cov_send, item_axes)
    shape_here = lax.dynamic_slice_in_dim(item_shape, first_row, share_rows, 0)
    rate_here = lax.dynamic_slice_in_dim(item_rate, first_row, share_rows, 0)
    flat = cov_recv.reshape(split_count * cov_rows, share_rows + factors)
    prior_log = lax.dot_general(
        flat[:, :share_rows], flat[:, share_rows:], TN, precision=HIGHEST, preferred_element_type=F32
    )
    scale = jnp.exp(prior_log) / rate_here

    smem = pl.BlockSpec(memory_space=pltpu.SMEM)
    vmem = pl.BlockSpec(memory_space=pltpu.VMEM)
    send, theta = kernel_call(
        functools.partial(prep_kernel, owners),
        (shape_of(owners, 16, LANES), shape_of(users_here, factors)),
        in_specs=[smem, vmem, vmem, vmem, vmem],
    )(
        block_counts,
        item_ids.reshape(slot_rows, block_width),
        clicks.reshape(slot_rows, block_width),
        user_shape0,
        user_rate0,
    )
    recv = exchange(send, user_axes)
    table = kernel_call(table_kernel, shape_of(item_rows, factors))(item_shape, item_rate)
    marks, partial = kernel_call(
        build_kernel, (shape_of(highs, owners * users_here, LANES), shape_of(owners * users_here, factors))
    )(recv, table)
    active = jnp.broadcast_to(
        activity_base + jnp.sum(user_shape0 / user_rate0, axis=1, keepdims=True), user_shape0.shape
    )
    totals = beta_totals[None, :]
    small = shape_of(users_here, factors)
    for iteration in range(ITERS - 1):
        parts = exchange(partial.reshape(owners, users_here, factors), user_axes)
        _, _, active, theta, spread = kernel_call(
            functools.partial(update_kernel, activity_shape),
            (small, small, small, small, shape_of(owners, users_here, factors)),
        )(parts, theta, active, totals)
        theta_all = exchange(spread, user_axes).reshape(owners * users_here, factors)
        if iteration < ITERS - 2:
            partial = kernel_call(ascend_kernel, shape_of(owners * users_here, factors))(
                theta_all, marks, table
            )
    partial, stats = kernel_call(
        last_kernel, (shape_of(owners * users_here, factors), shape_of(item_rows, factors))
    )(theta_all, marks, table)

    parts = exchange(stats, item_axes).reshape(split_count, share_rows, factors)
    new_shape, grad = kernel_call(
        score_kernel, (shape_of(share_rows, factors), shape_of(split_count, cov_rows, factors))
    )(parts, shape_here, scale, cov_recv)
    grad = exchange(grad, item_axes)
    lines = z_size * users_here + cov_rows
    both = kernel_call(join_kernel, shape_of(y_size, lines, factors))(grad, partial)
    both = exchange(both, ("y",))
    both = kernel_call(fan_kernel, shape_of(z_size, users_here + cov_rows, factors))(both)
    both = exchange(both, ("z",))
    user_shape, user_rate, active, cov_grad = kernel_call(
        functools.partial(finish_kernel, activity_shape, math.sqrt(item_rows * owners)),
        (small, small, small, shape_of(cov_rows, factors)),
    )(both, theta, active, totals)
    return (user_shape, user_rate, active[:, 0], new_shape, cov_grad)


def solution(mesh):
    fine = Mesh(mesh.devices.reshape(4, 8, 4, 2), ("y", "z", "x", "core"))
    users, items = ("y", "z"), ("x", "core")
    both = users + items
    return jax.shard_map(
        shards,
        mesh=fine,
        in_specs=(
            P(both, None, None),
            P(both, None, None),
            P(both),
            P(both, None),
            P(both, None),
            P(users, None),
            P(users, None),
            P(),
            P(items, users),
            P(items, None),
        ),
        out_specs=(
            P(both, None),
            P(both, None),
            P(both),
            P(both, None),
            P(items, None),
        ),
        check_vma=False,
    )
```

```python
import functools
import math

import jax
import jax.numpy as jnp
from jax import lax
from jax.experimental import pallas as pl
from jax.experimental.pallas import tpu as pltpu
from jax.sharding import Mesh
from jax.sharding import PartitionSpec as P

ITERS = 3
USER_RATIO = 4

user_prior = 0.3
activity_prior = 0.3
activity_base = 1.0
item_prior = 0.3
step_weight = 0.5

F32 = jnp.float32
BF16 = jnp.bfloat16
HIGHEST = lax.Precision.HIGHEST
NT = (((1,), (1,)), ((), ()))
NN = (((1,), (0,)), ((), ()))
TN = (((0,), (0,)), ((), ()))
LANES = 128
VMEM_LIMIT = 48 * 1024 * 1024


def exp_digamma_over(x, rate):
    pair = x * (x + 5.0)
    low = pair + 4.0
    high = pair + 6.0
    steps = (2.0 * x + 5.0) * (low * high + pair * (low + high)) / (pair * low * high)
    y = x + 6.0
    inv = 1.0 / y
    sq = inv * inv
    tail = 0.5 * inv + sq * (1.0 / 12.0 - sq * (1.0 / 120.0 - sq * (1.0 / 252.0)))
    return y * jnp.exp(-steps - tail) / rate


def kernel_call(kernel, out_shape, **specs):
    return pl.pallas_call(
        kernel,
        out_shape=out_shape,
        compiler_params=pltpu.CompilerParams(vmem_limit_bytes=VMEM_LIMIT),
        **specs,
    )


def shape_of(*dims):
    return jax.ShapeDtypeStruct(dims, F32)


def prep_kernel(
    owners,
    counts_hbm,
    ids_hbm,
    clicks_hbm,
    shape_hbm,
    rate_hbm,
    send_ref,
    counts_ref,
    ids_ref,
    clicks_ref,
    shape_ref,
    rate_ref,
    sems,
):
    copies = [
        pltpu.make_async_copy(source, target, sems.at[place])
        for place, (source, target) in enumerate(
            (
                (counts_hbm, counts_ref),
                (ids_hbm, ids_ref),
                (clicks_hbm, clicks_ref),
                (shape_hbm, shape_ref),
                (rate_hbm, rate_ref),
            )
        )
    ]
    for copy in copies:
        copy.start()
    for copy in copies:
        copy.wait()
    rows = ids_ref.shape[0]
    blocks = 8
    width = 2 * LANES
    capacity = rows * LANES // owners
    before = (
        lax.broadcasted_iota(jnp.int32, (width, width), 0)
        < lax.broadcasted_iota(jnp.int32, (width, width), 1)
    )
    before = jnp.where(before, 1.0, 0.0).astype(BF16)
    owner_iota = lax.broadcasted_iota(jnp.int32, (owners, width), 0)
    rank_iota = lax.broadcasted_iota(jnp.int32, (capacity, width), 0).astype(F32)
    carry = jnp.zeros((owners, 1), F32)
    lists = jnp.zeros((4 * owners, capacity), F32)
    for chunk in range(rows // 2):
        user = 2 * chunk // blocks
        ids = jnp.concatenate(
            [ids_ref[2 * chunk : 2 * chunk + 1, :], ids_ref[2 * chunk + 1 : 2 * chunk + 2, :]], axis=1
        )
        weights = []
        for row in (2 * chunk, 2 * chunk + 1):
            live = jnp.where(row % blocks < counts_ref[user], 1.0, 0.0)
            weights.append(clicks_ref[row : row + 1, :].astype(F32) * live)
        weight = jnp.concatenate(weights, axis=1)
        marks = jnp.where(owner_iota == (ids >> 11), 1.0, 0.0)
        earlier = lax.dot_general(marks.astype(BF16), before, NN, preferred_element_type=F32)
        rank = jnp.sum(marks * (earlier + carry), axis=0, keepdims=True)
        carry = carry + jnp.sum(marks, axis=1, keepdims=True)
        place = jnp.where(rank_iota == rank, 1.0, 0.0).astype(BF16)
        high = ((ids >> 7) & 15).astype(F32)
        low = (ids & 127).astype(F32)
        payload = jnp.concatenate(
            [marks * high, marks * low, marks * float(user), marks * weight], axis=0
        ).astype(BF16)
        lists = lists + lax.dot_general(payload, place, NT, preferred_element_type=F32)
    theta = exp_digamma_over(shape_ref[...], rate_ref[...])
    active = activity_base + jnp.sum(shape_ref[...] / rate_ref[...], axis=1, keepdims=True)
    eye = lax.broadcasted_iota(jnp.int32, theta.shape, 0) == lax.broadcasted_iota(jnp.int32, theta.shape, 1)
    active = jnp.sum(jnp.where(eye, active, 0.0), axis=0, keepdims=True)
    item_line = lists[:owners] * float(LANES) + lists[owners : 2 * owners]
    lines = (item_line, lists[2 * owners : 3 * owners], lists[3 * owners :])
    for owner in range(owners):
        for part in range(3):
            line = lines[part][owner : owner + 1, :]
            send_ref[owner, 2 * part : 2 * part + 1, :] = line[:, :LANES]
            send_ref[owner, 2 * part + 1 : 2 * part + 2, :] = line[:, LANES:]
        send_ref[owner, 6:7, :] = active
        send_ref[owner, 7:8, :] = jnp.zeros((1, LANES), F32)
        send_ref[owner, 8:16, :] = theta


def table_kernel(spot_ref, shape_ref, rate_ref, table_ref, shape_here_ref, rate_here_ref):
    table_ref[...] = exp_digamma_over(shape_ref[...], rate_ref[...])
    share = shape_here_ref.shape[0]
    here = pl.ds(pl.multiple_of(spot_ref[2] * share, share), share)
    shape_here_ref[...] = shape_ref[here, :]
    rate_here_ref[...] = rate_ref[here, :]


def split(x):
    high = x.astype(BF16)
    return high, (x - high.astype(F32)).astype(BF16)


def dot(left, right, dims):
    return lax.dot_general(left, right, dims, preferred_element_type=F32)


def ascend(theta, marks_ref, table_ref, stats_ref=None):
    factors = theta.shape[1]
    theta_high, theta_low = split(theta)
    theta_both = jnp.concatenate([theta_high, theta_low], axis=1)
    total = jnp.zeros(theta.shape, F32)
    width = 2 * LANES
    for pair in range(marks_ref.shape[0] // 2):
        rows = slice(pair * width, (pair + 1) * width)
        table = table_ref[rows, :]
        table_high, table_low = split(table)
        share = dot(theta_both, jnp.concatenate([table_high, table_high], axis=1), NT) + dot(
            theta_high, table_low, NT
        )
        marks = jnp.concatenate([marks_ref[2 * pair], marks_ref[2 * pair + 1]], axis=1)
        ratio = marks / share
        ratio_high, ratio_low = split(ratio)
        wide = dot(ratio_high, jnp.concatenate([table_high, table_low], axis=1), NN)
        total = total + (wide[:, :factors] + wide[:, factors:]) + dot(ratio_low, table_high, NN)
        if stats_ref is not None:
            wide = dot(ratio_high, theta_both, TN)
            spread = wide[:, :factors] + wide[:, factors:] + dot(ratio_low, theta_high, TN)
            stats_ref[pair, :width, :] = table * spread
    return total


def build_kernel(y_size, spot_ref, recv_ref, table_ref, marks_ref, partial_ref, theta_ref, active_ref):
    owners = recv_ref.shape[0]
    z_size = owners // y_size
    highs = marks_ref.shape[0]
    line_iota = lax.broadcasted_iota(jnp.int32, (LANES, 2 * LANES), 0).astype(F32)

    def wide(source, part):
        return jnp.concatenate(
            [recv_ref[source, 2 * part : 2 * part + 1, :], recv_ref[source, 2 * part + 1 : 2 * part + 2, :]],
            axis=1,
        )

    order = [y * z_size + z for z in range(z_size) for y in range(y_size)]
    for place, source in enumerate(order):
        item = wide(source, 0).astype(jnp.int32)
        low = (item & (LANES - 1)).astype(F32)
        high = (item >> 7).astype(F32) * 8.0 + wide(source, 1)
        left = jnp.where(line_iota == high, wide(source, 2), 0.0).astype(BF16)
        right = jnp.where(line_iota == low, 1.0, 0.0).astype(BF16)
        tile = dot(left, right, NT)
        for high in range(highs):
            marks_ref[high, 8 * place : 8 * place + 8, :] = tile[8 * high : 8 * high + 8, :]
    theta = jnp.concatenate([recv_ref[source, 8:16, :] for source in order], axis=0)
    partial_ref[...] = ascend(theta, marks_ref, table_ref)
    eye = lax.broadcasted_iota(jnp.int32, (8, LANES), 0) == lax.broadcasted_iota(jnp.int32, (8, LANES), 1)
    for y in range(y_size):
        source = y * z_size + spot_ref[1]
        theta_ref[8 * y : 8 * y + 8, :] = recv_ref[source, 8:16, :]
        active = jnp.sum(jnp.where(eye, recv_ref[source, 6:7, :], 0.0), axis=1, keepdims=True)
        active_ref[8 * y : 8 * y + 8, :] = jnp.broadcast_to(active, (8, LANES))


def ascend_kernel(theta_ref, marks_ref, table_ref, partial_ref):
    partial_ref[...] = ascend(theta_ref[...], marks_ref, table_ref)


def last_kernel(theta_ref, marks_ref, table_ref, cov_ref, weight_ref, partial_ref, send_ref):
    width = 2 * LANES
    rows = weight_ref.shape[0]
    for part in range(send_ref.shape[0]):
        for half in range(2):
            start = part * width + half * LANES
            send_ref[part, width + half * rows : width + (half + 1) * rows, :] = cov_ref[:, start : start + LANES]
        send_ref[part, width + 2 * rows :, :] = weight_ref[...]
    partial_ref[...] = ascend(theta_ref[...], marks_ref, table_ref, send_ref)


def sum_kernel(recv_ref, send_ref):
    total = jnp.sum(recv_ref[...], axis=0)
    send_ref[...] = jnp.broadcast_to(total[None], send_ref.shape)


def update_kernel(activity_shape, recv_ref, theta_ref, activity_ref, totals_ref, active_ref, next_ref, send_ref):
    total = jnp.sum(recv_ref[...], axis=0)
    shapes = user_prior + theta_ref[...] * total
    rates = activity_shape / activity_ref[...] + totals_ref[...]
    active = activity_base + jnp.sum(shapes / rates, axis=1, keepdims=True)
    active_ref[...] = jnp.broadcast_to(active, shapes.shape)
    theta = exp_digamma_over(shapes, rates)
    next_ref[...] = theta
    send_ref[...] = jnp.broadcast_to(theta[None], send_ref.shape)


def score_kernel(recv_ref, shape_ref, rate_ref, new_ref, grad_ref):
    share = shape_ref.shape[0]
    parts, rows, _ = grad_ref.shape
    stats = jnp.sum(recv_ref[:, :share, :], axis=0)
    new_shape = (1.0 - step_weight) * shape_ref[...] + step_weight * (item_prior + USER_RATIO * stats)
    new_ref[...] = new_shape
    cov = jnp.concatenate(
        [
            jnp.concatenate(
                [recv_ref[part, share : share + rows, :], recv_ref[part, share + rows : share + 2 * rows, :]],
                axis=1,
            )
            for part in range(parts)
        ],
        axis=0,
    )
    weight = jnp.concatenate([recv_ref[part, share + 2 * rows :, :] for part in range(parts)], axis=0)
    prior_log = lax.dot_general(cov, weight, TN, precision=HIGHEST, preferred_element_type=F32)
    score = item_prior - jnp.exp(prior_log) * new_shape / rate_ref[...]
    grad = lax.dot_general(cov, score, NN, precision=HIGHEST, preferred_element_type=F32)
    for part in range(parts):
        grad_ref[part] = grad[part * rows : (part + 1) * rows]


def join_kernel(users, grad_ref, partial_ref, send_ref):
    y_size, rows, _ = send_ref.shape
    grad = jnp.sum(grad_ref[...], axis=0)
    z_size = partial_ref.shape[0] // (y_size * users)
    for y in range(y_size):
        for z in range(z_size):
            place = (z * y_size + y) * users
            send_ref[y, z * users : (z + 1) * users, :] = partial_ref[place : place + users, :]
        send_ref[y, z_size * users :, :] = grad


def fan_kernel(users, recv_ref, send_ref):
    z_size, rows, _ = send_ref.shape
    total = jnp.sum(recv_ref[...], axis=0)
    for z in range(z_size):
        send_ref[z, :users, :] = total[z * users : (z + 1) * users, :]
        send_ref[z, users:, :] = total[z_size * users :, :]


def finish_kernel(
    activity_shape, root, spot_ref, recv_ref, theta_ref, activity_ref, totals_ref, shapes_ref, rates_ref, active_ref, grad_ref
):
    total = jnp.sum(recv_ref[...], axis=0)
    users = shapes_ref.shape[0]
    here = pl.ds(pl.multiple_of(spot_ref[0] * users, users), users)
    shapes = user_prior + theta_ref[here, :] * total[:users]
    rates = activity_shape / activity_ref[here, :] + totals_ref[...]
    shapes_ref[...] = shapes
    rates_ref[...] = rates
    active = activity_base + jnp.sum(shapes / rates, axis=1, keepdims=True)
    active_ref[...] = jnp.broadcast_to(active, shapes.shape)
    grad_ref[...] = total[users:] / root


def shards(
    item_ids,
    clicks,
    block_counts,
    user_shape0,
    user_rate0,
    item_shape,
    item_rate,
    beta_totals,
    covariates,
    cov_weight,
):
    y_size, z_size = lax.axis_size("y"), lax.axis_size("z")
    owners = y_size * z_size
    item_rows, factors = item_shape.shape
    users_here, blocks, block_width = item_ids.shape
    cov_rows = covariates.shape[0]
    slot_rows = users_here * blocks
    highs = item_rows // LANES
    user_axes, item_axes = ("y", "z"), ("x", "core")
    split_count = lax.axis_size(item_axes)
    share_rows = item_rows // split_count
    group = y_size * users_here
    everyone = owners * users_here
    activity_shape = activity_prior + factors * user_prior

    def exchange(array, axes):
        return lax.all_to_all(array, axes, split_axis=0, concat_axis=0, tiled=True)

    spot = jnp.stack([lax.axis_index("y"), lax.axis_index("z"), lax.axis_index(item_axes)]).astype(jnp.int32)
    totals = beta_totals[None, :]
    smem = pl.BlockSpec(memory_space=pltpu.SMEM)
    vmem = pl.BlockSpec(memory_space=pltpu.VMEM)
    hbm = pl.BlockSpec(memory_space=pltpu.HBM)
    send = kernel_call(
        functools.partial(prep_kernel, owners),
        shape_of(owners, 16, LANES),
        in_specs=[hbm] * 5,
        scratch_shapes=[
            pltpu.SMEM((users_here,), jnp.int32),
            pltpu.VMEM((slot_rows, block_width), jnp.int32),
            pltpu.VMEM((slot_rows, block_width), jnp.int32),
            pltpu.VMEM((users_here, factors), F32),
            pltpu.VMEM((users_here, factors), F32),
            pltpu.SemaphoreType.DMA((5,)),
        ],
    )(
        block_counts,
        item_ids.reshape(slot_rows, block_width),
        clicks.reshape(slot_rows, block_width),
        user_shape0,
        user_rate0,
    )
    recv = exchange(send, user_axes)
    share = shape_of(share_rows, factors)
    table, shape_here, rate_here = kernel_call(
        table_kernel, (shape_of(item_rows, factors), share, share), in_specs=[smem, vmem, vmem]
    )(spot, item_shape, item_rate)
    local = shape_of(group, factors)
    marks, partial, theta, active = kernel_call(
        functools.partial(build_kernel, y_size),
        (shape_of(highs, everyone, LANES), shape_of(everyone, factors), local, local),
        in_specs=[smem, vmem, vmem],
    )(spot, recv, table)
    for iteration in range(ITERS - 1):
        parts = exchange(partial.reshape(z_size, group, factors), ("z",))
        parts = kernel_call(sum_kernel, shape_of(y_size, group, factors))(parts)
        parts = exchange(parts, ("y",))
        active, theta, spread = kernel_call(
            functools.partial(update_kernel, activity_shape),
            (local, local, shape_of(z_size, group, factors)),
        )(parts, theta, active, totals)
        theta_all = exchange(spread, ("z",)).reshape(everyone, factors)
        if iteration < ITERS - 2:
            partial = kernel_call(ascend_kernel, shape_of(everyone, factors))(theta_all, marks, table)
    partial, send = kernel_call(
        last_kernel, (shape_of(everyone, factors), shape_of(split_count, share_rows + 3 * cov_rows, factors))
    )(theta_all, marks, table, covariates, cov_weight)
    recv = exchange(send, item_axes)
    new_shape, grad = kernel_call(score_kernel, (share, shape_of(split_count, cov_rows, factors)))(
        recv, shape_here, rate_here
    )
    grad = exchange(grad, item_axes)
    both = kernel_call(
        functools.partial(join_kernel, users_here), shape_of(y_size, z_size * users_here + cov_rows, factors)
    )(grad, partial)
    both = exchange(both, ("y",))
    both = kernel_call(
        functools.partial(fan_kernel, users_here), shape_of(z_size, users_here + cov_rows, factors)
    )(both)
    both = exchange(both, ("z",))
    small = shape_of(users_here, factors)
    user_shape, user_rate, active, cov_grad = kernel_call(
        functools.partial(finish_kernel, activity_shape, math.sqrt(item_rows * owners)),
        (small, small, small, shape_of(cov_rows, factors)),
        in_specs=[smem, vmem, vmem, vmem, vmem],
    )(spot, both, theta, active, totals)
    return (user_shape, user_rate, active[:, 0], new_shape, cov_grad)


def solution(mesh):
    fine = Mesh(mesh.devices.reshape(4, 8, 4, 2), ("y", "z", "x", "core"))
    users, items = ("y", "z"), ("x", "core")
    both = users + items
    return jax.shard_map(
        shards,
        mesh=fine,
        in_specs=(
            P(both, None, None),
            P(both, None, None),
            P(both),
            P(both, None),
            P(both, None),
            P(users, None),
            P(users, None),
            P(),
            P(items, users),
            P(items, None),
        ),
        out_specs=(
            P(both, None),
            P(both, None),
            P(both),
            P(both, None),
            P(items, None),
        ),
        check_vma=False,
    )
```

```python
import functools
import math

import jax
import jax.numpy as jnp
from jax import lax
from jax.experimental import pallas as pl
from jax.experimental.pallas import tpu as pltpu
from jax.sharding import Mesh
from jax.sharding import PartitionSpec as P

ITERS = 3
USER_RATIO = 4

user_prior = 0.3
activity_prior = 0.3
activity_base = 1.0
item_prior = 0.3
step_weight = 0.5

F32 = jnp.float32
BF16 = jnp.bfloat16
HIGHEST = lax.Precision.HIGHEST
NT = (((1,), (1,)), ((), ()))
NN = (((1,), (0,)), ((), ()))
TN = (((0,), (0,)), ((), ()))
LANES = 128
VMEM_LIMIT = 48 * 1024 * 1024


def exp_digamma_over(x, rate):
    pair = x * (x + 5.0)
    low = pair + 4.0
    high = pair + 6.0
    steps = (2.0 * x + 5.0) * (low * high + pair * (low + high)) / (pair * low * high)
    y = x + 6.0
    inv = 1.0 / y
    sq = inv * inv
    tail = 0.5 * inv + sq * (1.0 / 12.0 - sq * (1.0 / 120.0 - sq * (1.0 / 252.0)))
    return y * jnp.exp(-steps - tail) / rate


def kernel_call(kernel, out_shape, **specs):
    return pl.pallas_call(
        kernel,
        out_shape=out_shape,
        compiler_params=pltpu.CompilerParams(vmem_limit_bytes=VMEM_LIMIT),
        **specs,
    )


def behind(kernel, inputs):
    def wrapped(*refs):
        kernel(*refs[:inputs], *refs[inputs + 1 :])

    return wrapped


def shape_of(*dims):
    return jax.ShapeDtypeStruct(dims, F32)


def prep_kernel(
    owners,
    counts_hbm,
    ids_hbm,
    clicks_hbm,
    shape_hbm,
    rate_hbm,
    send_ref,
    theta_ref,
    active_ref,
    counts_ref,
    ids_ref,
    clicks_ref,
    shape_ref,
    rate_ref,
    sems,
):
    copies = [
        pltpu.make_async_copy(source, target, sems.at[place])
        for place, (source, target) in enumerate(
            (
                (counts_hbm, counts_ref),
                (ids_hbm, ids_ref),
                (clicks_hbm, clicks_ref),
                (shape_hbm, shape_ref),
                (rate_hbm, rate_ref),
            )
        )
    ]
    for copy in copies:
        copy.start()
    for copy in copies:
        copy.wait()
    rows = ids_ref.shape[0]
    blocks = 8
    width = 2 * LANES
    capacity = rows * LANES // owners
    before = (
        lax.broadcasted_iota(jnp.int32, (width, width), 0)
        < lax.broadcasted_iota(jnp.int32, (width, width), 1)
    )
    before = jnp.where(before, 1.0, 0.0).astype(BF16)
    owner_iota = lax.broadcasted_iota(jnp.int32, (owners, width), 0)
    rank_iota = lax.broadcasted_iota(jnp.int32, (capacity, width), 0).astype(F32)
    carry = jnp.zeros((owners, 1), F32)
    lists = jnp.zeros((4 * owners, capacity), F32)
    for chunk in range(rows // 2):
        user = 2 * chunk // blocks
        ids = jnp.concatenate(
            [ids_ref[2 * chunk : 2 * chunk + 1, :], ids_ref[2 * chunk + 1 : 2 * chunk + 2, :]], axis=1
        )
        weights = []
        for row in (2 * chunk, 2 * chunk + 1):
            live = jnp.where(row % blocks < counts_ref[user], 1.0, 0.0)
            weights.append(clicks_ref[row : row + 1, :].astype(F32) * live)
        weight = jnp.concatenate(weights, axis=1)
        marks = jnp.where(owner_iota == (ids >> 11), 1.0, 0.0)
        earlier = lax.dot_general(marks.astype(BF16), before, NN, preferred_element_type=F32)
        rank = jnp.sum(marks * (earlier + carry), axis=0, keepdims=True)
        carry = carry + jnp.sum(marks, axis=1, keepdims=True)
        place = jnp.where(rank_iota == rank, 1.0, 0.0).astype(BF16)
        high = ((ids >> 7) & 15).astype(F32)
        low = (ids & 127).astype(F32)
        payload = jnp.concatenate(
            [marks * high, marks * low, marks * float(user), marks * weight], axis=0
        ).astype(BF16)
        lists = lists + lax.dot_general(payload, place, NT, preferred_element_type=F32)
    theta = exp_digamma_over(shape_ref[...], rate_ref[...])
    active = activity_base + jnp.sum(shape_ref[...] / rate_ref[...], axis=1, keepdims=True)
    theta_ref[...] = theta
    active_ref[...] = jnp.broadcast_to(active, theta.shape)
    item_line = lists[:owners] * float(LANES) + lists[owners : 2 * owners]
    lines = (item_line, lists[2 * owners : 3 * owners], lists[3 * owners :])
    for owner in range(owners):
        for part in range(3):
            line = lines[part][owner : owner + 1, :]
            send_ref[owner, 2 * part : 2 * part + 1, :] = line[:, :LANES]
            send_ref[owner, 2 * part + 1 : 2 * part + 2, :] = line[:, LANES:]
        send_ref[owner, 6:8, :] = jnp.zeros((2, LANES), F32)
        send_ref[owner, 8:16, :] = theta


def table_kernel(spot_ref, shape_ref, rate_ref, table_ref, shape_here_ref, rate_here_ref):
    table_ref[...] = exp_digamma_over(shape_ref[...], rate_ref[...])
    share = shape_here_ref.shape[0]
    here = pl.ds(pl.multiple_of(spot_ref[2] * share, share), share)
    shape_here_ref[...] = shape_ref[here, :]
    rate_here_ref[...] = rate_ref[here, :]


def split(x):
    high = x.astype(BF16)
    return high, (x - high.astype(F32)).astype(BF16)


def dot(left, right, dims):
    return lax.dot_general(left, right, dims, preferred_element_type=F32)


def ascend(theta, marks_ref, table_ref, stats_ref=None):
    factors = theta.shape[1]
    theta_high, theta_low = split(theta)
    theta_both = jnp.concatenate([theta_high, theta_low], axis=1)
    total = jnp.zeros(theta.shape, F32)
    width = 2 * LANES
    for pair in range(marks_ref.shape[0] // 2):
        rows = slice(pair * width, (pair + 1) * width)
        table = table_ref[rows, :]
        table_high, table_low = split(table)
        share = dot(theta_both, jnp.concatenate([table_high, table_high], axis=1), NT) + dot(
            theta_high, table_low, NT
        )
        marks = jnp.concatenate([marks_ref[2 * pair], marks_ref[2 * pair + 1]], axis=1)
        ratio = marks / share
        ratio_high, ratio_low = split(ratio)
        wide = dot(ratio_high, jnp.concatenate([table_high, table_low], axis=1), NN)
        total = total + (wide[:, :factors] + wide[:, factors:]) + dot(ratio_low, table_high, NN)
        if stats_ref is not None:
            wide = dot(ratio_high, theta_both, TN)
            spread = wide[:, :factors] + wide[:, factors:] + dot(ratio_low, theta_high, TN)
            stats_ref[pair, :width, :] = table * spread
    return total


def build_kernel(recv_ref, table_ref, marks_ref, partial_ref):
    owners = recv_ref.shape[0]
    highs = marks_ref.shape[0]
    line_iota = lax.broadcasted_iota(jnp.int32, (LANES, 2 * LANES), 0).astype(F32)

    def wide(source, part):
        return jnp.concatenate(
            [recv_ref[source, 2 * part : 2 * part + 1, :], recv_ref[source, 2 * part + 1 : 2 * part + 2, :]],
            axis=1,
        )

    for source in range(owners):
        item = wide(source, 0).astype(jnp.int32)
        low = (item & (LANES - 1)).astype(F32)
        high = (item >> 7).astype(F32) * 8.0 + wide(source, 1)
        left = jnp.where(line_iota == high, wide(source, 2), 0.0).astype(BF16)
        right = jnp.where(line_iota == low, 1.0, 0.0).astype(BF16)
        tile = dot(left, right, NT)
        for high in range(highs):
            marks_ref[high, 8 * source : 8 * source + 8, :] = tile[8 * high : 8 * high + 8, :]
    theta = jnp.concatenate([recv_ref[source, 8:16, :] for source in range(owners)], axis=0)
    partial_ref[...] = ascend(theta, marks_ref, table_ref)


def ascend_kernel(theta_ref, marks_ref, table_ref, partial_ref):
    partial_ref[...] = ascend(theta_ref[...], marks_ref, table_ref)


def last_kernel(theta_ref, marks_ref, table_ref, partial_ref, stats_ref):
    partial_ref[...] = ascend(theta_ref[...], marks_ref, table_ref, stats_ref)


def core_kernel(spot_ref, cov_ref, weight_ref, send_ref, keep_ref):
    pairs, _, width = keep_ref.shape
    core = spot_ref[2] & 1
    for pair in range(pairs):
        other = pl.multiple_of((2 * pair + 1 - core) * width, width)
        own = pl.multiple_of((2 * pair + core) * width, width)
        send_ref[pair] = cov_ref[:, pl.ds(other, width)]
        keep_ref[pair] = cov_ref[:, pl.ds(own, width)]
    send_ref[pairs, :, :LANES] = weight_ref[...]
    send_ref[pairs, :, LANES:] = weight_ref[...]


def near_kernel(spot_ref, recv_ref, held_ref, weight_ref, send_ref, keep_ref):
    low = (spot_ref[2] >> 1) & 1
    for high in range(2):
        other = 2 * high + 1 - low
        own = 2 * high + low
        send_ref[2 * high] = held_ref[other]
        send_ref[2 * high + 1] = recv_ref[other]
        keep_ref[2 * high] = held_ref[own]
        keep_ref[2 * high + 1] = recv_ref[own]
    for target in (send_ref, keep_ref):
        target[4, :, :LANES] = weight_ref[...]
        target[4, :, LANES:] = recv_ref[4, :, :LANES]


def far_kernel(spot_ref, recv_ref, held_ref, send_ref, keep_ref):
    high = spot_ref[2] >> 2
    for core in range(2):
        other = 2 * (1 - high) + core
        own = 2 * high + core
        send_ref[core] = held_ref[other]
        send_ref[2 + core] = recv_ref[other]
        keep_ref[core] = held_ref[own]
        keep_ref[2 + core] = recv_ref[own]
    for target in (send_ref, keep_ref):
        target[4] = held_ref[4]
        target[5] = recv_ref[4]


def scale_kernel(held_ref, recv_ref, rate_ref, scale_ref):
    total = jnp.zeros(rate_ref.shape, F32)
    for source in (held_ref, recv_ref):
        cov = jnp.concatenate([source[place] for place in range(4)], axis=0)
        weight = jnp.concatenate(
            [source[4 + place // 2, :, (place % 2) * LANES : (place % 2 + 1) * LANES] for place in range(4)], axis=0
        )
        total = total + lax.dot_general(cov, weight, TN, precision=HIGHEST, preferred_element_type=F32)
    scale_ref[...] = jnp.exp(total) / rate_ref[...]


def update_kernel(activity_shape, recv_ref, theta_ref, activity_ref, totals_ref, active_ref, next_ref, send_ref):
    total = jnp.sum(recv_ref[...], axis=0)
    shapes = user_prior + theta_ref[...] * total
    rates = activity_shape / activity_ref[...] + totals_ref[...]
    active = activity_base + jnp.sum(shapes / rates, axis=1, keepdims=True)
    active_ref[...] = jnp.broadcast_to(active, shapes.shape)
    theta = exp_digamma_over(shapes, rates)
    next_ref[...] = theta
    send_ref[...] = jnp.broadcast_to(theta[None], send_ref.shape)


def score_kernel(spot_ref, stats_ref, shape_ref, scale_ref, held_ref, recv_ref, new_ref, grad_ref):
    stats = jnp.sum(stats_ref[...], axis=0)
    new_shape = (1.0 - step_weight) * shape_ref[...] + step_weight * (item_prior + USER_RATIO * stats)
    new_ref[...] = new_shape
    score = item_prior - scale_ref[...] * new_shape
    rows = grad_ref.shape[1]
    for part, source in enumerate((held_ref, recv_ref)):
        cov = jnp.concatenate([source[place] for place in range(4)], axis=0)
        grad = lax.dot_general(cov, score, NN, precision=HIGHEST, preferred_element_type=F32)
        for place in range(4):
            grad_ref[spot_ref[2] ^ (4 * part + place)] = grad[place * rows : (place + 1) * rows]


def join_kernel(grad_ref, partial_ref, send_ref):
    y_size, rows, _ = send_ref.shape
    grad = jnp.sum(grad_ref[...], axis=0)
    users = partial_ref.shape[0] // y_size
    for y in range(y_size):
        send_ref[y, :users, :] = partial_ref[y * users : (y + 1) * users, :]
        send_ref[y, users:, :] = grad


def fan_kernel(users, recv_ref, send_ref):
    z_size, rows, _ = send_ref.shape
    total = jnp.sum(recv_ref[...], axis=0)
    for z in range(z_size):
        send_ref[z, :users, :] = total[z * users : (z + 1) * users, :]
        send_ref[z, users:, :] = total[z_size * users :, :]


def finish_kernel(
    activity_shape, root, recv_ref, theta_ref, activity_ref, totals_ref, shapes_ref, rates_ref, active_ref, grad_ref
):
    total = jnp.sum(recv_ref[...], axis=0)
    users = shapes_ref.shape[0]
    shapes = user_prior + theta_ref[...] * total[:users]
    rates = activity_shape / activity_ref[...] + totals_ref[...]
    shapes_ref[...] = shapes
    rates_ref[...] = rates
    active = activity_base + jnp.sum(shapes / rates, axis=1, keepdims=True)
    active_ref[...] = jnp.broadcast_to(active, shapes.shape)
    grad_ref[...] = total[users:] / root


def shards(
    item_ids,
    clicks,
    block_counts,
    user_shape0,
    user_rate0,
    item_shape,
    item_rate,
    beta_totals,
    covariates,
    cov_weight,
):
    y_size, z_size = lax.axis_size("y"), lax.axis_size("z")
    owners = y_size * z_size
    item_rows, factors = item_shape.shape
    users_here, blocks, block_width = item_ids.shape
    cov_rows = covariates.shape[0]
    slot_rows = users_here * blocks
    highs = item_rows // LANES
    user_axes, item_axes = ("y", "z"), ("x", "core")
    split_count = lax.axis_size(item_axes)
    share_rows = item_rows // split_count
    everyone = owners * users_here
    activity_shape = activity_prior + factors * user_prior

    def exchange(array, axes):
        return lax.all_to_all(array, axes, split_axis=0, concat_axis=0, tiled=True)

    spot = jnp.stack([lax.axis_index("y"), lax.axis_index("z"), lax.axis_index(item_axes)]).astype(jnp.int32)
    totals = beta_totals[None, :]
    smem = pl.BlockSpec(memory_space=pltpu.SMEM)
    vmem = pl.BlockSpec(memory_space=pltpu.VMEM)
    hbm = pl.BlockSpec(memory_space=pl.ANY)
    small = shape_of(users_here, factors)
    share = shape_of(share_rows, factors)
    send, theta, active = kernel_call(
        functools.partial(prep_kernel, owners),
        (shape_of(owners, 16, LANES), small, small),
        in_specs=[hbm] * 5,
        scratch_shapes=[
            pltpu.SMEM((users_here,), jnp.int32),
            pltpu.VMEM((slot_rows, block_width), jnp.int32),
            pltpu.VMEM((slot_rows, block_width), jnp.int32),
            pltpu.VMEM((users_here, factors), F32),
            pltpu.VMEM((users_here, factors), F32),
            pltpu.SemaphoreType.DMA((5,)),
        ],
    )(
        block_counts,
        item_ids.reshape(slot_rows, block_width),
        clicks.reshape(slot_rows, block_width),
        user_shape0,
        user_rate0,
    )
    recv = exchange(send, user_axes)
    table, shape_here, rate_here = kernel_call(
        table_kernel, (shape_of(item_rows, factors), share, share), in_specs=[smem, vmem, vmem]
    )(spot, item_shape, item_rate)

    swap_core = [(place, place ^ 1) for place in range(lax.axis_size("core"))]
    swap_near = [(place, place ^ 1) for place in range(lax.axis_size("x"))]
    swap_far = [(place, place ^ 2) for place in range(lax.axis_size("x"))]
    block = (cov_rows, share_rows)
    moved, held = kernel_call(
        behind(core_kernel, 3), (shape_of(5, *block), shape_of(4, *block)), in_specs=[smem, vmem, vmem, hbm]
    )(spot, covariates, cov_weight, send)
    moved = lax.ppermute(moved, "core", swap_core)
    marks, partial = kernel_call(build_kernel, (shape_of(highs, everyone, LANES), shape_of(everyone, factors)))(
        recv, table
    )
    moved, held = kernel_call(
        behind(near_kernel, 4), (shape_of(5, *block), shape_of(5, *block)), in_specs=[smem, vmem, vmem, vmem, hbm]
    )(spot, moved, held, cov_weight, partial)
    moved = lax.ppermute(moved, "x", swap_near)
    for iteration in range(ITERS - 1):
        parts = exchange(partial.reshape(owners, users_here, factors), user_axes)
        active, theta, spread = kernel_call(
            functools.partial(update_kernel, activity_shape),
            (small, small, shape_of(owners, users_here, factors)),
        )(parts, theta, active, totals)
        theta_all = exchange(spread, user_axes).reshape(everyone, factors)
        if iteration == 0:
            moved, held = kernel_call(
                behind(far_kernel, 3), (shape_of(6, *block), shape_of(6, *block)), in_specs=[smem, vmem, vmem, hbm]
            )(spot, moved, held, spread)
            moved = lax.ppermute(moved, "x", swap_far)
        else:
            scale = kernel_call(behind(scale_kernel, 3), share, in_specs=[vmem, vmem, vmem, hbm])(
                held, moved, rate_here, spread
            )
        if iteration < ITERS - 2:
            partial = kernel_call(ascend_kernel, shape_of(everyone, factors))(theta_all, marks, table)
    partial, stats = kernel_call(
        last_kernel, (shape_of(everyone, factors), shape_of(split_count, share_rows, factors))
    )(theta_all, marks, table)
    stats = exchange(stats, item_axes)
    new_shape, grad = kernel_call(
        score_kernel, (share, shape_of(split_count, cov_rows, factors)), in_specs=[smem] + [vmem] * 5
    )(spot, stats, shape_here, scale, held, moved)
    grad = exchange(grad, item_axes)
    both = kernel_call(join_kernel, shape_of(y_size, z_size * users_here + cov_rows, factors))(grad, partial)
    both = exchange(both, ("y",))
    both = kernel_call(
        functools.partial(fan_kernel, users_here), shape_of(z_size, users_here + cov_rows, factors)
    )(both)
    both = exchange(both, ("z",))
    user_shape, user_rate, active, cov_grad = kernel_call(
        functools.partial(finish_kernel, activity_shape, math.sqrt(item_rows * owners)),
        (small, small, small, shape_of(cov_rows, factors)),
    )(both, theta, active, totals)
    return (user_shape, user_rate, active[:, 0], new_shape, cov_grad)


def solution(mesh):
    fine = Mesh(mesh.devices.reshape(4, 8, 4, 2), ("y", "z", "x", "core"))
    users, items = ("y", "z"), ("x", "core")
    both = users + items
    return jax.shard_map(
        shards,
        mesh=fine,
        in_specs=(
            P(both, None, None),
            P(both, None, None),
            P(both),
            P(both, None),
            P(both, None),
            P(users, None),
            P(users, None),
            P(),
            P(items, users),
            P(items, None),
        ),
        out_specs=(
            P(both, None),
            P(both, None),
            P(both),
            P(both, None),
            P(items, None),
        ),
        check_vma=False,
    )
```

```python
import functools
import math

import jax
import jax.numpy as jnp
from jax import lax
from jax.experimental import pallas as pl
from jax.experimental.pallas import tpu as pltpu
from jax.sharding import Mesh
from jax.sharding import PartitionSpec as P

ITERS = 3
USER_RATIO = 4

user_prior = 0.3
activity_prior = 0.3
activity_base = 1.0
item_prior = 0.3
step_weight = 0.5

F32 = jnp.float32
BF16 = jnp.bfloat16
HIGHEST = lax.Precision.HIGHEST
NT = (((1,), (1,)), ((), ()))
NN = (((1,), (0,)), ((), ()))
TN = (((0,), (0,)), ((), ()))
LANES = 128
VMEM_LIMIT = 48 * 1024 * 1024
WHOLE_VMEM = 60 * 1024 * 1024


def exp_digamma_over(x, rate):
    pair = x * (x + 5.0)
    low = pair + 4.0
    high = pair + 6.0
    steps = (2.0 * x + 5.0) * (low * high + pair * (low + high)) / (pair * low * high)
    y = x + 6.0
    inv = 1.0 / y
    sq = inv * inv
    tail = 0.5 * inv + sq * (1.0 / 12.0 - sq * (1.0 / 120.0 - sq * (1.0 / 252.0)))
    return y * jnp.exp(-steps - tail) / rate


def kernel_call(kernel, out_shape, vmem=VMEM_LIMIT, **specs):
    return pl.pallas_call(
        kernel,
        out_shape=out_shape,
        compiler_params=pltpu.CompilerParams(vmem_limit_bytes=vmem),
        **specs,
    )


def behind(kernel, inputs, awaited=1):
    def wrapped(*refs):
        kernel(*refs[:inputs], *refs[inputs + awaited :])

    return wrapped


def shape_of(*dims):
    return jax.ShapeDtypeStruct(dims, F32)


def prep_kernel(
    owners,
    counts_hbm,
    ids_hbm,
    clicks_hbm,
    shape_hbm,
    rate_hbm,
    send_ref,
    theta_ref,
    active_ref,
    counts_ref,
    ids_ref,
    clicks_ref,
    shape_ref,
    rate_ref,
    sems,
):
    copies = [
        pltpu.make_async_copy(source, target, sems.at[place])
        for place, (source, target) in enumerate(
            (
                (counts_hbm, counts_ref),
                (ids_hbm, ids_ref),
                (clicks_hbm, clicks_ref),
                (shape_hbm, shape_ref),
                (rate_hbm, rate_ref),
            )
        )
    ]
    for copy in copies:
        copy.start()
    for copy in copies:
        copy.wait()
    rows = ids_ref.shape[0]
    blocks = 8
    width = 2 * LANES
    capacity = rows * LANES // owners
    before = (
        lax.broadcasted_iota(jnp.int32, (width, width), 0)
        < lax.broadcasted_iota(jnp.int32, (width, width), 1)
    )
    before = jnp.where(before, 1.0, 0.0).astype(BF16)
    owner_iota = lax.broadcasted_iota(jnp.int32, (owners, width), 0)
    rank_iota = lax.broadcasted_iota(jnp.int32, (capacity, width), 0).astype(F32)
    carry = jnp.zeros((owners, 1), F32)
    lists = jnp.zeros((4 * owners, capacity), F32)
    for chunk in range(rows // 2):
        user = 2 * chunk // blocks
        ids = jnp.concatenate(
            [ids_ref[2 * chunk : 2 * chunk + 1, :], ids_ref[2 * chunk + 1 : 2 * chunk + 2, :]], axis=1
        )
        weights = []
        for row in (2 * chunk, 2 * chunk + 1):
            live = jnp.where(row % blocks < counts_ref[user], 1.0, 0.0)
            weights.append(clicks_ref[row : row + 1, :].astype(F32) * live)
        weight = jnp.concatenate(weights, axis=1)
        marks = jnp.where(owner_iota == (ids >> 11), 1.0, 0.0)
        earlier = lax.dot_general(marks.astype(BF16), before, NN, preferred_element_type=F32)
        rank = jnp.sum(marks * (earlier + carry), axis=0, keepdims=True)
        carry = carry + jnp.sum(marks, axis=1, keepdims=True)
        place = jnp.where(rank_iota == rank, 1.0, 0.0).astype(BF16)
        high = ((ids >> 7) & 15).astype(F32)
        low = (ids & 127).astype(F32)
        payload = jnp.concatenate(
            [marks * high, marks * low, marks * float(user), marks * weight], axis=0
        ).astype(BF16)
        lists = lists + lax.dot_general(payload, place, NT, preferred_element_type=F32)
    theta = exp_digamma_over(shape_ref[...], rate_ref[...])
    active = activity_base + jnp.sum(shape_ref[...] / rate_ref[...], axis=1, keepdims=True)
    theta_ref[...] = theta
    active_ref[...] = jnp.broadcast_to(active, theta.shape)
    item_line = lists[:owners] * float(LANES) + lists[owners : 2 * owners]
    lines = (item_line, lists[2 * owners : 3 * owners], lists[3 * owners :])
    for owner in range(owners):
        for part in range(3):
            line = lines[part][owner : owner + 1, :]
            send_ref[owner, 2 * part : 2 * part + 1, :] = line[:, :LANES]
            send_ref[owner, 2 * part + 1 : 2 * part + 2, :] = line[:, LANES:]
        send_ref[owner, 6:8, :] = jnp.zeros((2, LANES), F32)
        send_ref[owner, 8:16, :] = theta


def table_kernel(spot_ref, shape_ref, rate_ref, table_ref, shape_here_ref, rate_here_ref):
    table_ref[...] = exp_digamma_over(shape_ref[...], rate_ref[...])
    share = shape_here_ref.shape[0]
    here = pl.ds(pl.multiple_of(spot_ref[2] * share, share), share)
    shape_here_ref[...] = shape_ref[here, :]
    rate_here_ref[...] = rate_ref[here, :]


def split(x):
    high = x.astype(BF16)
    return high, (x - high.astype(F32)).astype(BF16)


def dot(left, right, dims):
    return lax.dot_general(left, right, dims, preferred_element_type=F32)


def ascend(theta, marks_ref, table_ref, stats_ref=None):
    factors = theta.shape[1]
    theta_high, theta_low = split(theta)
    theta_both = jnp.concatenate([theta_high, theta_low], axis=1)
    total = jnp.zeros(theta.shape, F32)
    width = 2 * LANES
    for pair in range(marks_ref.shape[0] // 2):
        rows = slice(pair * width, (pair + 1) * width)
        table = table_ref[rows, :]
        table_high, table_low = split(table)
        share = dot(theta_both, jnp.concatenate([table_high, table_high], axis=1), NT) + dot(
            theta_high, table_low, NT
        )
        marks = jnp.concatenate([marks_ref[2 * pair], marks_ref[2 * pair + 1]], axis=1)
        ratio = marks / share
        ratio_high, ratio_low = split(ratio)
        wide = dot(ratio_high, jnp.concatenate([table_high, table_low], axis=1), NN)
        total = total + (wide[:, :factors] + wide[:, factors:]) + dot(ratio_low, table_high, NN)
        if stats_ref is not None:
            wide = dot(ratio_high, theta_both, TN)
            spread = wide[:, :factors] + wide[:, factors:] + dot(ratio_low, theta_high, TN)
            stats_ref[pair, :width, :] = table * spread
    return total


def build_kernel(recv_ref, table_ref, marks_ref, partial_ref):
    owners = recv_ref.shape[0]
    highs = marks_ref.shape[0]
    line_iota = lax.broadcasted_iota(jnp.int32, (LANES, 2 * LANES), 0).astype(F32)

    def wide(source, part):
        return jnp.concatenate(
            [recv_ref[source, 2 * part : 2 * part + 1, :], recv_ref[source, 2 * part + 1 : 2 * part + 2, :]],
            axis=1,
        )

    for source in range(owners):
        item = wide(source, 0).astype(jnp.int32)
        low = (item & (LANES - 1)).astype(F32)
        high = (item >> 7).astype(F32) * 8.0 + wide(source, 1)
        left = jnp.where(line_iota == high, wide(source, 2), 0.0).astype(BF16)
        right = jnp.where(line_iota == low, 1.0, 0.0).astype(BF16)
        tile = dot(left, right, NT)
        for high in range(highs):
            marks_ref[high, 8 * source : 8 * source + 8, :] = tile[8 * high : 8 * high + 8, :]
    theta = jnp.concatenate([recv_ref[source, 8:16, :] for source in range(owners)], axis=0)
    partial_ref[...] = ascend(theta, marks_ref, table_ref)


def ascend_kernel(theta_ref, marks_ref, table_ref, partial_ref):
    partial_ref[...] = ascend(theta_ref[...], marks_ref, table_ref)


def last_kernel(theta_ref, marks_ref, table_ref, partial_ref, stats_ref):
    partial_ref[...] = ascend(theta_ref[...], marks_ref, table_ref, stats_ref)


def core_kernel(spot_ref, cov_ref, weight_ref, send_ref, keep_ref):
    pairs, _, width = keep_ref.shape
    core = spot_ref[2] & 1
    for pair in range(pairs):
        other = pl.multiple_of((2 * pair + 1 - core) * width, width)
        own = pl.multiple_of((2 * pair + core) * width, width)
        send_ref[pair] = cov_ref[:, pl.ds(other, width)]
        keep_ref[pair] = cov_ref[:, pl.ds(own, width)]
    send_ref[pairs, :, :LANES] = weight_ref[...]
    send_ref[pairs, :, LANES:] = weight_ref[...]


def near_kernel(spot_ref, recv_ref, held_ref, weight_ref, send_ref, keep_ref):
    low = (spot_ref[2] >> 1) & 1
    for high in range(2):
        other = 2 * high + 1 - low
        own = 2 * high + low
        send_ref[2 * high] = held_ref[other]
        send_ref[2 * high + 1] = recv_ref[other]
        keep_ref[2 * high] = held_ref[own]
        keep_ref[2 * high + 1] = recv_ref[own]
    for target in (send_ref, keep_ref):
        target[4, :, :LANES] = weight_ref[...]
        target[4, :, LANES:] = recv_ref[4, :, :LANES]


def far_kernel(spot_ref, recv_ref, held_ref, send_ref, keep_ref):
    high = spot_ref[2] >> 2
    for core in range(2):
        other = 2 * (1 - high) + core
        own = 2 * high + core
        send_ref[core] = held_ref[other]
        send_ref[2 + core] = recv_ref[other]
        keep_ref[core] = held_ref[own]
        keep_ref[2 + core] = recv_ref[own]
    for target in (send_ref, keep_ref):
        target[4] = held_ref[4]
        target[5] = recv_ref[4]


def scale_kernel(held_ref, recv_ref, rate_ref, scale_ref):
    total = jnp.zeros(rate_ref.shape, F32)
    for source in (held_ref, recv_ref):
        cov = jnp.concatenate([source[place] for place in range(4)], axis=0)
        weight = jnp.concatenate(
            [source[4 + place // 2, :, (place % 2) * LANES : (place % 2 + 1) * LANES] for place in range(4)], axis=0
        )
        total = total + lax.dot_general(cov, weight, TN, precision=HIGHEST, preferred_element_type=F32)
    scale_ref[...] = jnp.exp(total) / rate_ref[...]


def update_kernel(activity_shape, recv_ref, theta_ref, activity_ref, totals_ref, active_ref, next_ref, send_ref):
    total = jnp.sum(recv_ref[...], axis=0)
    shapes = user_prior + theta_ref[...] * total
    rates = activity_shape / activity_ref[...] + totals_ref[...]
    active = activity_base + jnp.sum(shapes / rates, axis=1, keepdims=True)
    active_ref[...] = jnp.broadcast_to(active, shapes.shape)
    theta = exp_digamma_over(shapes, rates)
    next_ref[...] = theta
    send_ref[...] = jnp.broadcast_to(theta[None], send_ref.shape)


def score_kernel(spot_ref, stats_ref, shape_ref, scale_ref, held_ref, recv_ref, new_ref, grad_ref):
    stats = jnp.sum(stats_ref[...], axis=0)
    new_shape = (1.0 - step_weight) * shape_ref[...] + step_weight * (item_prior + USER_RATIO * stats)
    new_ref[...] = new_shape
    score = item_prior - scale_ref[...] * new_shape
    rows = grad_ref.shape[1]
    for part, source in enumerate((held_ref, recv_ref)):
        cov = jnp.concatenate([source[place] for place in range(4)], axis=0)
        grad = lax.dot_general(cov, score, NN, precision=HIGHEST, preferred_element_type=F32)
        for place in range(4):
            grad_ref[spot_ref[2] ^ (4 * part + place)] = grad[place * rows : (place + 1) * rows]


def join_kernel(grad_ref, partial_ref, send_ref):
    y_size, rows, _ = send_ref.shape
    grad = jnp.sum(grad_ref[...], axis=0)
    users = partial_ref.shape[0] // y_size
    for y in range(y_size):
        send_ref[y, :users, :] = partial_ref[y * users : (y + 1) * users, :]
        send_ref[y, users:, :] = grad


def fan_kernel(users, recv_ref, send_ref):
    z_size, rows, _ = send_ref.shape
    total = jnp.sum(recv_ref[...], axis=0)
    for z in range(z_size):
        send_ref[z, :users, :] = total[z * users : (z + 1) * users, :]
        send_ref[z, users:, :] = total[z_size * users :, :]


def finish_kernel(
    activity_shape, root, recv_ref, theta_ref, activity_ref, totals_ref, shapes_ref, rates_ref, active_ref, grad_ref
):
    total = jnp.sum(recv_ref[...], axis=0)
    users = shapes_ref.shape[0]
    shapes = user_prior + theta_ref[...] * total[:users]
    rates = activity_shape / activity_ref[...] + totals_ref[...]
    shapes_ref[...] = shapes
    rates_ref[...] = rates
    active = activity_base + jnp.sum(shapes / rates, axis=1, keepdims=True)
    eye = lax.broadcasted_iota(jnp.int32, shapes.shape, 0) == lax.broadcasted_iota(jnp.int32, shapes.shape, 1)
    row = jnp.sum(jnp.where(eye, active, 0.0), axis=0, keepdims=True)
    active_ref[...] = row[:, :users]
    grad_ref[...] = total[users:] / root


def shards(
    item_ids,
    clicks,
    block_counts,
    user_shape0,
    user_rate0,
    item_shape,
    item_rate,
    beta_totals,
    covariates,
    cov_weight,
):
    y_size, z_size = lax.axis_size("y"), lax.axis_size("z")
    owners = y_size * z_size
    item_rows, factors = item_shape.shape
    users_here, blocks, block_width = item_ids.shape
    cov_rows = covariates.shape[0]
    slot_rows = users_here * blocks
    highs = item_rows // LANES
    user_axes, item_axes = ("y", "z"), ("x", "core")
    split_count = lax.axis_size(item_axes)
    share_rows = item_rows // split_count
    everyone = owners * users_here
    activity_shape = activity_prior + factors * user_prior

    def exchange(array, axes):
        return lax.all_to_all(array, axes, split_axis=0, concat_axis=0, tiled=True)

    spot = jnp.stack([lax.axis_index("y"), lax.axis_index("z"), lax.axis_index(item_axes)]).astype(jnp.int32)
    totals = beta_totals[None, :]
    smem = pl.BlockSpec(memory_space=pltpu.SMEM)
    vmem = pl.BlockSpec(memory_space=pltpu.VMEM)
    hbm = pl.BlockSpec(memory_space=pl.ANY)
    small = shape_of(users_here, factors)
    share = shape_of(share_rows, factors)
    send, theta, active = kernel_call(
        functools.partial(prep_kernel, owners),
        (shape_of(owners, 16, LANES), small, small),
        vmem=WHOLE_VMEM,
        in_specs=[hbm] * 5,
        scratch_shapes=[
            pltpu.SMEM((users_here,), jnp.int32),
            pltpu.VMEM((slot_rows, block_width), jnp.int32),
            pltpu.VMEM((slot_rows, block_width), jnp.int32),
            pltpu.VMEM((users_here, factors), F32),
            pltpu.VMEM((users_here, factors), F32),
            pltpu.SemaphoreType.DMA((5,)),
        ],
    )(
        block_counts,
        item_ids.reshape(slot_rows, block_width),
        clicks.reshape(slot_rows, block_width),
        user_shape0,
        user_rate0,
    )
    recv = exchange(send, user_axes)
    table, shape_here, rate_here = kernel_call(
        table_kernel, (shape_of(item_rows, factors), share, share), in_specs=[smem, vmem, vmem]
    )(spot, item_shape, item_rate)

    swap_core = [(place, place ^ 1) for place in range(lax.axis_size("core"))]
    swap_near = [(place, place ^ 1) for place in range(lax.axis_size("x"))]
    swap_far = [(place, place ^ 2) for place in range(lax.axis_size("x"))]
    block = (cov_rows, share_rows)
    moved, held = kernel_call(
        behind(core_kernel, 3), (shape_of(5, *block), shape_of(4, *block)), in_specs=[smem, vmem, vmem, hbm]
    )(spot, covariates, cov_weight, send)
    marks, partial = kernel_call(
        behind(build_kernel, 2),
        (shape_of(highs, everyone, LANES), shape_of(everyone, factors)),
        in_specs=[vmem, vmem, hbm],
    )(recv, table, moved)
    for iteration in range(ITERS - 1):
        first = iteration == 0
        if first:
            moved = lax.ppermute(moved, "core", swap_core)
            moved, held = kernel_call(
                behind(near_kernel, 4), (shape_of(5, *block), shape_of(5, *block)), in_specs=[smem, vmem, vmem, vmem, hbm]
            )(spot, moved, held, cov_weight, partial)
        else:
            moved = lax.ppermute(moved, "x", swap_far)
            scale = kernel_call(behind(scale_kernel, 3), share, in_specs=[vmem, vmem, vmem, hbm])(
                held, moved, rate_here, partial
            )
        parts = exchange(partial.reshape(owners, users_here, factors), user_axes)
        active, theta, spread = kernel_call(
            behind(functools.partial(update_kernel, activity_shape), 4),
            (small, small, shape_of(owners, users_here, factors)),
            in_specs=[vmem] * 4 + [hbm],
        )(parts, theta, active, totals, moved if first else scale)
        theta_all = exchange(spread, user_axes).reshape(everyone, factors)
        if first:
            moved = lax.ppermute(moved, "x", swap_near)
            moved, held = kernel_call(
                behind(far_kernel, 3), (shape_of(6, *block), shape_of(6, *block)), in_specs=[smem, vmem, vmem, hbm]
            )(spot, moved, held, spread)
            partial = kernel_call(
                behind(ascend_kernel, 3), shape_of(everyone, factors), in_specs=[vmem, vmem, vmem, hbm]
            )(theta_all, marks, table, moved)
    partial, stats = kernel_call(
        last_kernel, (shape_of(everyone, factors), shape_of(split_count, share_rows, factors))
    )(theta_all, marks, table)
    stats = exchange(stats, item_axes)
    new_shape, grad = kernel_call(
        score_kernel, (share, shape_of(split_count, cov_rows, factors)), in_specs=[smem] + [vmem] * 5
    )(spot, stats, shape_here, scale, held, moved)
    grad = exchange(grad, item_axes)
    both = kernel_call(join_kernel, shape_of(y_size, z_size * users_here + cov_rows, factors))(grad, partial)
    both = exchange(both, ("y",))
    both = kernel_call(
        functools.partial(fan_kernel, users_here), shape_of(z_size, users_here + cov_rows, factors)
    )(both)
    both = exchange(both, ("z",))
    user_shape, user_rate, active, cov_grad = kernel_call(
        functools.partial(finish_kernel, activity_shape, math.sqrt(item_rows * owners)),
        (small, small, shape_of(1, users_here), shape_of(cov_rows, factors)),
    )(both, theta, active, totals)
    return (user_shape, user_rate, active.reshape(users_here), new_shape, cov_grad)


def solution(mesh):
    fine = Mesh(mesh.devices.reshape(4, 8, 4, 2), ("y", "z", "x", "core"))
    users, items = ("y", "z"), ("x", "core")
    both = users + items
    return jax.shard_map(
        shards,
        mesh=fine,
        in_specs=(
            P(both, None, None),
            P(both, None, None),
            P(both),
            P(both, None),
            P(both, None),
            P(users, None),
            P(users, None),
            P(),
            P(items, users),
            P(items, None),
        ),
        out_specs=(
            P(both, None),
            P(both, None),
            P(both),
            P(both, None),
            P(items, None),
        ),
        check_vma=False,
    )
```

```python
import functools
import math

import jax
import jax.numpy as jnp
from jax import lax
from jax.experimental import pallas as pl
from jax.experimental.pallas import tpu as pltpu
from jax.sharding import Mesh
from jax.sharding import PartitionSpec as P

ITERS = 3
USER_RATIO = 4

user_prior = 0.3
activity_prior = 0.3
activity_base = 1.0
item_prior = 0.3
step_weight = 0.5

F32 = jnp.float32
BF16 = jnp.bfloat16
HIGHEST = lax.Precision.HIGHEST
NT = (((1,), (1,)), ((), ()))
NN = (((1,), (0,)), ((), ()))
TN = (((0,), (0,)), ((), ()))
LANES = 128
VMEM_LIMIT = 48 * 1024 * 1024
WHOLE_VMEM = 60 * 1024 * 1024


def exp_digamma_over(x, rate):
    pair = x * (x + 5.0)
    low = pair + 4.0
    high = pair + 6.0
    steps = (2.0 * x + 5.0) * (low * high + pair * (low + high)) / (pair * low * high)
    y = x + 6.0
    inv = 1.0 / y
    sq = inv * inv
    tail = 0.5 * inv + sq * (1.0 / 12.0 - sq * (1.0 / 120.0 - sq * (1.0 / 252.0)))
    return y * jnp.exp(-steps - tail) / rate


def kernel_call(kernel, out_shape, vmem=VMEM_LIMIT, **specs):
    return pl.pallas_call(
        kernel,
        out_shape=out_shape,
        compiler_params=pltpu.CompilerParams(vmem_limit_bytes=vmem),
        **specs,
    )


def behind(kernel, inputs, awaited=1):
    def wrapped(*refs):
        kernel(*refs[:inputs], *refs[inputs + awaited :])

    return wrapped


def shape_of(*dims):
    return jax.ShapeDtypeStruct(dims, F32)


def split(x):
    high = x.astype(BF16)
    return high, (x - high.astype(F32)).astype(BF16)


def dot(left, right, dims):
    return lax.dot_general(left, right, dims, preferred_element_type=F32)


def prep_kernel(
    owners,
    counts_hbm,
    ids_hbm,
    clicks_hbm,
    shape_hbm,
    rate_hbm,
    send_ref,
    theta_ref,
    active_ref,
    counts_ref,
    ids_ref,
    clicks_ref,
    shape_ref,
    rate_ref,
    sems,
):
    copies = [
        pltpu.make_async_copy(source, target, sems.at[place])
        for place, (source, target) in enumerate(
            (
                (counts_hbm, counts_ref),
                (ids_hbm, ids_ref),
                (clicks_hbm, clicks_ref),
                (shape_hbm, shape_ref),
                (rate_hbm, rate_ref),
            )
        )
    ]
    for copy in copies:
        copy.start()
    for copy in copies:
        copy.wait()
    rows = ids_ref.shape[0]
    blocks = 8
    width = 2 * LANES
    capacity = rows * LANES // owners
    before = (
        lax.broadcasted_iota(jnp.int32, (width, width), 0)
        < lax.broadcasted_iota(jnp.int32, (width, width), 1)
    )
    before = jnp.where(before, 1.0, 0.0).astype(BF16)
    owner_iota = lax.broadcasted_iota(jnp.int32, (owners, width), 0)
    rank_iota = lax.broadcasted_iota(jnp.int32, (capacity, width), 0).astype(F32)
    chunks = rows // 2
    ids_of, marks_of = [], []
    for chunk in range(chunks):
        ids = jnp.concatenate(
            [ids_ref[2 * chunk : 2 * chunk + 1, :], ids_ref[2 * chunk + 1 : 2 * chunk + 2, :]], axis=1
        )
        ids_of.append(ids)
        marks_of.append(jnp.where(owner_iota == (ids >> 11), 1.0, 0.0))
    earlier_of = dot(jnp.concatenate([marks.astype(BF16) for marks in marks_of], axis=0), before, NN)
    carry = jnp.zeros((owners, 1), F32)
    lists = jnp.zeros((4 * owners, capacity), F32)
    for chunk in range(chunks):
        user = 2 * chunk // blocks
        ids, marks = ids_of[chunk], marks_of[chunk]
        weights = []
        for row in (2 * chunk, 2 * chunk + 1):
            live = jnp.where(row % blocks < counts_ref[user], 1.0, 0.0)
            weights.append(clicks_ref[row : row + 1, :].astype(F32) * live)
        weight = jnp.concatenate(weights, axis=1)
        earlier = earlier_of[chunk * owners : (chunk + 1) * owners]
        rank = jnp.sum(marks * (earlier + carry), axis=0, keepdims=True)
        carry = carry + (earlier[:, width - 1 :] + marks[:, width - 1 :])
        place = jnp.where(rank_iota == rank, 1.0, 0.0).astype(BF16)
        high = ((ids >> 7) & 15).astype(F32)
        low = (ids & 127).astype(F32)
        payload = jnp.concatenate(
            [marks * high, marks * low, marks * float(user), marks * weight], axis=0
        ).astype(BF16)
        lists = lists + lax.dot_general(payload, place, NT, preferred_element_type=F32)
    theta = exp_digamma_over(shape_ref[...], rate_ref[...])
    active = activity_base + jnp.sum(shape_ref[...] / rate_ref[...], axis=1, keepdims=True)
    theta_ref[...] = theta
    active_ref[...] = jnp.broadcast_to(active, theta.shape)
    item_line = lists[:owners] * float(LANES) + lists[owners : 2 * owners]
    lines = (item_line, lists[2 * owners : 3 * owners], lists[3 * owners :])
    for owner in range(owners):
        for part in range(3):
            line = lines[part][owner : owner + 1, :]
            send_ref[owner, 2 * part : 2 * part + 1, :] = line[:, :LANES]
            send_ref[owner, 2 * part + 1 : 2 * part + 2, :] = line[:, LANES:]
        send_ref[owner, 6:8, :] = jnp.zeros((2, LANES), F32)
        send_ref[owner, 8:16, :] = theta


def table_kernel(shape_ref, rate_ref, table_ref):
    table_ref[...] = exp_digamma_over(shape_ref[...], rate_ref[...])


def widen(table):
    table_high, table_low = split(table)
    twice = jnp.concatenate([table_high, table_high], axis=1)
    return table_high, table_low, twice, jnp.concatenate([table_high, table_low], axis=1)


def ascend_block(theta_high, theta_both, marks, table):
    factors = table.shape[1]
    table_high, table_low, twice, both = widen(table)
    share = dot(theta_both, twice, NT) + dot(theta_high, table_low, NT)
    ratio_high, ratio_low = split(marks / share)
    wide = dot(ratio_high, both, NN)
    part = wide[:, :factors] + wide[:, factors:] + dot(ratio_low, table_high, NN)
    return ratio_high, ratio_low, part


def split_theta(theta):
    theta_high, theta_low = split(theta)
    return theta_high, jnp.concatenate([theta_high, theta_low], axis=1)


def ascend(theta, marks_ref, table_ref):
    theta_high, theta_both = split_theta(theta)
    total = jnp.zeros(theta.shape, F32)
    width = 2 * LANES
    for pair in range(marks_ref.shape[0] // 2):
        marks = jnp.concatenate([marks_ref[2 * pair], marks_ref[2 * pair + 1]], axis=1)
        table = table_ref[pair * width : (pair + 1) * width, :]
        total = total + ascend_block(theta_high, theta_both, marks, table)[2]
    return total


def build_kernel(recv_ref, table_ref, marks_ref, partial_ref):
    owners = recv_ref.shape[0]
    highs = marks_ref.shape[0]
    line_iota = lax.broadcasted_iota(jnp.int32, (LANES, 2 * LANES), 0).astype(F32)

    def wide(source, part):
        return jnp.concatenate(
            [recv_ref[source, 2 * part : 2 * part + 1, :], recv_ref[source, 2 * part + 1 : 2 * part + 2, :]],
            axis=1,
        )

    for source in range(owners):
        item = wide(source, 0).astype(jnp.int32)
        low = (item & (LANES - 1)).astype(F32)
        high = (item >> 7).astype(F32) * 8.0 + wide(source, 1)
        left = jnp.where(line_iota == high, wide(source, 2), 0.0).astype(BF16)
        right = jnp.where(line_iota == low, 1.0, 0.0).astype(BF16)
        tile = dot(left, right, NT)
        for high in range(highs):
            marks_ref[high, 8 * source : 8 * source + 8, :] = tile[8 * high : 8 * high + 8, :]
    theta = jnp.concatenate([recv_ref[source, 8:16, :] for source in range(owners)], axis=0)
    partial_ref[...] = ascend(theta, marks_ref, table_ref)


def ascend_kernel(theta_ref, marks_ref, table_ref, partial_ref, token_ref):
    total = ascend(theta_ref[...], marks_ref, table_ref)
    partial_ref[...] = total
    token_ref[...] = total[: token_ref.shape[0]]


def pack_kernel(cov_ref, weight_ref, own_ref):
    items = cov_ref.shape[1]
    own_ref[:, :items] = cov_ref[...]
    own_ref[:, items:] = weight_ref[...]


def prior_kernel(shards, *refs):
    shard_refs, refs = refs[:shards], refs[shards:]
    sum_ref, token_ref = refs[-2:]
    items = sum_ref.shape[1]
    width = 2 * LANES
    weight = jnp.concatenate([shard[:, items:] for shard in shard_refs], axis=0)
    for start in range(0, items, width):
        cov = jnp.concatenate([shard[:, start : start + width] for shard in shard_refs], axis=0)
        part = lax.dot_general(weight, cov, TN, precision=HIGHEST, preferred_element_type=F32)
        if len(refs) > 2:
            part = part + refs[0][:, start : start + width]
        sum_ref[:, start : start + width] = part
    token_ref[...] = weight[: token_ref.shape[0]]


def scale_kernel(shard_ref, sum_ref, rate_ref, scale_ref):
    items = scale_ref.shape[0]
    width = 2 * LANES
    weight = shard_ref[:, items:]
    for start in range(0, items, width):
        part = lax.dot_general(
            weight, shard_ref[:, start : start + width], TN, precision=HIGHEST, preferred_element_type=F32
        )
        prior_log = (part + sum_ref[:, start : start + width]).T
        scale_ref[start : start + width, :] = jnp.exp(prior_log) / rate_ref[start : start + width, :]


def last_kernel(shards, spot_ref, theta_ref, marks_ref, table_ref, scale_ref, shape_ref, *refs):
    shard_refs = refs[:shards]
    partial_ref, base_ref, keep_ref, send_ref, grad_ref = refs[shards:]
    spot = spot_ref[2]
    theta = theta_ref[...]
    factors = theta.shape[1]
    theta_high, theta_both = split_theta(theta)
    total = jnp.zeros(theta.shape, F32)
    rows = grad_ref.shape[1]
    grad = jnp.zeros((shards * rows, factors), F32)
    width = 2 * LANES
    for place in range(shards):
        block = spot ^ place
        here = pl.ds(pl.multiple_of(block * width, width), width)
        table = table_ref[here, :]
        marks = jnp.concatenate([marks_ref[2 * block], marks_ref[2 * block + 1]], axis=1)
        ratio_high, ratio_low, part = ascend_block(theta_high, theta_both, marks, table)
        total = total + part
        wide = dot(ratio_high, theta_both, TN)
        stats = table * (wide[:, :factors] + wide[:, factors:] + dot(ratio_low, theta_high, TN))
        target = send_ref if place % 2 else keep_ref
        target[place // 2] = stats
        base = (1.0 - step_weight) * shape_ref[here, :] + step_weight * item_prior
        if place == 0:
            base_ref[...] = base
        score = item_prior / shards - scale_ref[here, :] * (base / shards + step_weight * USER_RATIO * stats)
        score_high, score_low = split(score)
        cov_high, cov_low = split(jnp.concatenate([shard[:, here] for shard in shard_refs], axis=0))
        wide = dot(cov_high, jnp.concatenate([score_high, score_low], axis=1), NN)
        grad = grad + (wide[:, :factors] + wide[:, factors:] + dot(cov_low, score_high, NN))
    partial_ref[...] = total
    for place in range(shards):
        grad_ref[spot ^ place] = grad[place * rows : (place + 1) * rows]


def halve_kernel(held_ref, recv_ref, keep_ref, send_ref):
    for place in range(held_ref.shape[0]):
        target = send_ref if place % 2 else keep_ref
        target[place // 2] = held_ref[place] + recv_ref[place]


def close_kernel(held_ref, recv_ref, base_ref, new_ref):
    new_ref[...] = base_ref[...] + step_weight * USER_RATIO * (held_ref[0] + recv_ref[0])


def update_kernel(activity_shape, recv_ref, theta_ref, activity_ref, totals_ref, active_ref, next_ref, send_ref):
    total = jnp.sum(recv_ref[...], axis=0)
    shapes = user_prior + theta_ref[...] * total
    rates = activity_shape / activity_ref[...] + totals_ref[...]
    active = activity_base + jnp.sum(shapes / rates, axis=1, keepdims=True)
    active_ref[...] = jnp.broadcast_to(active, shapes.shape)
    theta = exp_digamma_over(shapes, rates)
    next_ref[...] = theta
    send_ref[...] = jnp.broadcast_to(theta[None], send_ref.shape)


def join_kernel(grad_ref, partial_ref, send_ref):
    y_size, rows, _ = send_ref.shape
    grad = jnp.sum(grad_ref[...], axis=0)
    users = partial_ref.shape[0] // y_size
    for y in range(y_size):
        send_ref[y, :users, :] = partial_ref[y * users : (y + 1) * users, :]
        send_ref[y, users:, :] = grad


def fan_kernel(users, recv_ref, send_ref):
    z_size, rows, _ = send_ref.shape
    total = jnp.sum(recv_ref[...], axis=0)
    for z in range(z_size):
        send_ref[z, :users, :] = total[z * users : (z + 1) * users, :]
        send_ref[z, users:, :] = total[z_size * users :, :]


def finish_kernel(
    activity_shape, root, recv_ref, theta_ref, activity_ref, totals_ref, shapes_ref, rates_ref, active_ref, grad_ref
):
    total = jnp.sum(recv_ref[...], axis=0)
    users = shapes_ref.shape[0]
    shapes = user_prior + theta_ref[...] * total[:users]
    rates = activity_shape / activity_ref[...] + totals_ref[...]
    shapes_ref[...] = shapes
    rates_ref[...] = rates
    active = activity_base + jnp.sum(shapes / rates, axis=1, keepdims=True)
    eye = lax.broadcasted_iota(jnp.int32, shapes.shape, 0) == lax.broadcasted_iota(jnp.int32, shapes.shape, 1)
    row = jnp.sum(jnp.where(eye, active, 0.0), axis=0, keepdims=True)
    active_ref[...] = row[:, :users]
    grad_ref[...] = total[users:] / root


def shards(
    item_ids,
    clicks,
    block_counts,
    user_shape0,
    user_rate0,
    item_shape,
    item_rate,
    beta_totals,
    covariates,
    cov_weight,
):
    y_size, z_size = lax.axis_size("y"), lax.axis_size("z")
    owners = y_size * z_size
    item_rows, factors = item_shape.shape
    users_here, blocks, block_width = item_ids.shape
    cov_rows = covariates.shape[0]
    slot_rows = users_here * blocks
    highs = item_rows // LANES
    user_axes, item_axes = ("y", "z"), ("x", "core")
    split_count = lax.axis_size(item_axes)
    share_rows = item_rows // split_count
    everyone = owners * users_here
    activity_shape = activity_prior + factors * user_prior

    def exchange(array, axes):
        return lax.all_to_all(array, axes, split_axis=0, concat_axis=0, tiled=True)

    spot = jnp.stack([lax.axis_index("y"), lax.axis_index("z"), lax.axis_index(item_axes)]).astype(jnp.int32)
    totals = beta_totals[None, :]
    smem = pl.BlockSpec(memory_space=pltpu.SMEM)
    vmem = pl.BlockSpec(memory_space=pltpu.VMEM)
    hbm = pl.BlockSpec(memory_space=pl.ANY)
    small = shape_of(users_here, factors)
    share = shape_of(share_rows, factors)
    send, theta, active = kernel_call(
        functools.partial(prep_kernel, owners),
        (shape_of(owners, 16, LANES), small, small),
        vmem=WHOLE_VMEM,
        in_specs=[hbm] * 5,
        scratch_shapes=[
            pltpu.SMEM((users_here,), jnp.int32),
            pltpu.VMEM((slot_rows, block_width), jnp.int32),
            pltpu.VMEM((slot_rows, block_width), jnp.int32),
            pltpu.VMEM((users_here, factors), F32),
            pltpu.VMEM((users_here, factors), F32),
            pltpu.SemaphoreType.DMA((5,)),
        ],
    )(
        block_counts,
        item_ids.reshape(slot_rows, block_width),
        clicks.reshape(slot_rows, block_width),
        user_shape0,
        user_rate0,
    )
    recv = exchange(send, user_axes)
    table = kernel_call(table_kernel, shape_of(item_rows, factors))(item_shape, item_rate)

    def swap(array, distance):
        axis, bit = ("core", 1) if distance == 1 else ("x", distance // 2)
        return lax.ppermute(array, axis, [(place, place ^ bit) for place in range(lax.axis_size(axis))])

    shards = [None] * split_count
    own = kernel_call(
        behind(pack_kernel, 2), shape_of(cov_rows, item_rows + factors), in_specs=[vmem, vmem, hbm]
    )(covariates, cov_weight, theta)
    shards[0] = own
    for distance in (1, 2, 6, 4):
        shards[distance] = swap(own, distance)
    for distance in (2, 6, 4):
        shards[distance + 1] = swap(shards[distance], 1)

    def add_prior(places, total, awaited):
        inputs = [shards[place] for place in places] + ([] if total is None else [total])
        return kernel_call(
            behind(functools.partial(prior_kernel, len(places)), len(inputs)),
            (shape_of(factors, item_rows), small),
            in_specs=[vmem] * len(inputs) + [hbm],
        )(*inputs, awaited)

    marks, partial = kernel_call(
        behind(build_kernel, 2),
        (shape_of(highs, everyone, LANES), shape_of(everyone, factors)),
        in_specs=[vmem, vmem, hbm],
    )(recv, table, own)
    prior, token = add_prior((0, 1), None, partial)
    for iteration in range(ITERS - 1):
        parts = exchange(partial.reshape(owners, users_here, factors), user_axes)
        active, theta, spread = kernel_call(
            behind(functools.partial(update_kernel, activity_shape), 4),
            (small, small, shape_of(owners, users_here, factors)),
            in_specs=[vmem] * 4 + [hbm],
        )(parts, theta, active, totals, token)
        theta_all = exchange(spread, user_axes).reshape(everyone, factors)
        if iteration == 0:
            prior, token = add_prior((2, 6), prior, spread)
            partial, token = kernel_call(
                behind(ascend_kernel, 3),
                (shape_of(everyone, factors), small),
                in_specs=[vmem, vmem, vmem, hbm],
            )(theta_all, marks, table, token)
            prior, token = add_prior((3, 7, 4), prior, token)
        else:
            scale = kernel_call(
                behind(scale_kernel, 3), shape_of(item_rows, factors), in_specs=[vmem, vmem, vmem, hbm]
            )(shards[5], prior, item_rate, spread)
    half = split_count // 2
    partial, base, held, moved, grad = kernel_call(
        functools.partial(last_kernel, split_count),
        (
            shape_of(everyone, factors),
            share,
            shape_of(half, share_rows, factors),
            shape_of(half, share_rows, factors),
            shape_of(split_count, cov_rows, factors),
        ),
        in_specs=[smem] + [vmem] * (5 + split_count),
    )(spot, theta_all, marks, table, scale, item_shape, *shards)

    def halve(held, moved, distance):
        half = held.shape[0] // 2
        return kernel_call(halve_kernel, (shape_of(half, share_rows, factors),) * 2)(held, swap(moved, distance))

    grad = exchange(grad, item_axes)
    held, moved = halve(held, moved, 1)
    both = kernel_call(
        behind(join_kernel, 2), shape_of(y_size, z_size * users_here + cov_rows, factors), in_specs=[vmem, vmem, hbm]
    )(grad, partial, moved)
    both = exchange(both, ("y",))
    held, moved = halve(held, moved, 2)
    both = kernel_call(
        behind(functools.partial(fan_kernel, users_here), 1),
        shape_of(z_size, users_here + cov_rows, factors),
        in_specs=[vmem, hbm],
    )(both, moved)
    both = exchange(both, ("z",))
    new_shape = kernel_call(close_kernel, share)(held, swap(moved, 4), base)
    user_shape, user_rate, active, cov_grad = kernel_call(
        functools.partial(finish_kernel, activity_shape, math.sqrt(item_rows * owners)),
        (small, small, shape_of(1, users_here), shape_of(cov_rows, factors)),
    )(both, theta, active, totals)
    return (user_shape, user_rate, active.reshape(users_here), new_shape, cov_grad)


def solution(mesh):
    fine = Mesh(mesh.devices.reshape(4, 8, 4, 2), ("y", "z", "x", "core"))
    users, items = ("y", "z"), ("x", "core")
    both = users + items
    return jax.shard_map(
        shards,
        mesh=fine,
        in_specs=(
            P(both, None, None),
            P(both, None, None),
            P(both),
            P(both, None),
            P(both, None),
            P(users, None),
            P(users, None),
            P(),
            P(items, users),
            P(items, None),
        ),
        out_specs=(
            P(both, None),
            P(both, None),
            P(both),
            P(both, None),
            P(items, None),
        ),
        check_vma=False,
    )
```

```python
import functools
import math

import jax
import jax.numpy as jnp
from jax import lax
from jax.experimental import pallas as pl
from jax.experimental.pallas import tpu as pltpu
from jax.sharding import Mesh
from jax.sharding import PartitionSpec as P

ITERS = 3
USER_RATIO = 4

user_prior = 0.3
activity_prior = 0.3
activity_base = 1.0
item_prior = 0.3
step_weight = 0.5

F32 = jnp.float32
BF16 = jnp.bfloat16
HIGHEST = lax.Precision.HIGHEST
NT = (((1,), (1,)), ((), ()))
NN = (((1,), (0,)), ((), ()))
TN = (((0,), (0,)), ((), ()))
LANES = 128
VMEM_LIMIT = 24 * 1024 * 1024
WHOLE_VMEM = 60 * 1024 * 1024


def exp_digamma_over(x, rate):
    pair = x * (x + 5.0)
    low = pair + 4.0
    high = pair + 6.0
    steps = (2.0 * x + 5.0) * (low * high + pair * (low + high)) / (pair * low * high)
    y = x + 6.0
    inv = 1.0 / y
    sq = inv * inv
    tail = 0.5 * inv + sq * (1.0 / 12.0 - sq * (1.0 / 120.0 - sq * (1.0 / 252.0)))
    return y * jnp.exp(-steps - tail) / rate


def kernel_call(kernel, out_shape, vmem=VMEM_LIMIT, **specs):
    return pl.pallas_call(
        kernel,
        out_shape=out_shape,
        compiler_params=pltpu.CompilerParams(vmem_limit_bytes=vmem),
        **specs,
    )


def behind(kernel, inputs, awaited=1):
    def wrapped(*refs):
        kernel(*refs[:inputs], *refs[inputs + awaited :])

    return wrapped


def shape_of(*dims):
    return jax.ShapeDtypeStruct(dims, F32)


def split(x):
    high = x.astype(BF16)
    return high, (x - high.astype(F32)).astype(BF16)


def dot(left, right, dims):
    return lax.dot_general(left, right, dims, preferred_element_type=F32)


def prep_kernel(
    owners,
    counts_hbm,
    ids_hbm,
    clicks_hbm,
    shape_hbm,
    rate_hbm,
    send_ref,
    theta_ref,
    active_ref,
    counts_ref,
    ids_ref,
    clicks_ref,
    shape_ref,
    rate_ref,
    sems,
):
    copies = [
        pltpu.make_async_copy(source, target, sems.at[place])
        for place, (source, target) in enumerate(
            (
                (counts_hbm, counts_ref),
                (ids_hbm, ids_ref),
                (clicks_hbm, clicks_ref),
                (shape_hbm, shape_ref),
                (rate_hbm, rate_ref),
            )
        )
    ]
    for copy in copies:
        copy.start()
    for copy in copies:
        copy.wait()
    rows = ids_ref.shape[0]
    blocks = 8
    width = 2 * LANES
    capacity = rows * LANES // owners
    before = (
        lax.broadcasted_iota(jnp.int32, (width, width), 0)
        < lax.broadcasted_iota(jnp.int32, (width, width), 1)
    )
    before = jnp.where(before, 1.0, 0.0).astype(BF16)
    owner_iota = lax.broadcasted_iota(jnp.int32, (owners, width), 0)
    rank_iota = lax.broadcasted_iota(jnp.int32, (capacity, width), 0).astype(F32)
    chunks = rows // 2
    ids_of, marks_of = [], []
    for chunk in range(chunks):
        ids = jnp.concatenate(
            [ids_ref[2 * chunk : 2 * chunk + 1, :], ids_ref[2 * chunk + 1 : 2 * chunk + 2, :]], axis=1
        )
        ids_of.append(ids)
        marks_of.append(jnp.where(owner_iota == (ids >> 11), 1.0, 0.0))
    earlier_of = dot(jnp.concatenate([marks.astype(BF16) for marks in marks_of], axis=0), before, NN)
    carry = jnp.zeros((owners, 1), F32)
    lists = jnp.zeros((4 * owners, capacity), F32)
    for chunk in range(chunks):
        user = 2 * chunk // blocks
        ids, marks = ids_of[chunk], marks_of[chunk]
        weights = []
        for row in (2 * chunk, 2 * chunk + 1):
            live = jnp.where(row % blocks < counts_ref[user], 1.0, 0.0)
            weights.append(clicks_ref[row : row + 1, :].astype(F32) * live)
        weight = jnp.concatenate(weights, axis=1)
        earlier = earlier_of[chunk * owners : (chunk + 1) * owners]
        rank = jnp.sum(marks * (earlier + carry), axis=0, keepdims=True)
        carry = carry + (earlier[:, width - 1 :] + marks[:, width - 1 :])
        place = jnp.where(rank_iota == rank, 1.0, 0.0).astype(BF16)
        high = ((ids >> 7) & 15).astype(F32)
        low = (ids & 127).astype(F32)
        payload = jnp.concatenate(
            [marks * high, marks * low, marks * float(user), marks * weight], axis=0
        ).astype(BF16)
        lists = lists + lax.dot_general(payload, place, NT, preferred_element_type=F32)
    theta = exp_digamma_over(shape_ref[...], rate_ref[...])
    active = activity_base + jnp.sum(shape_ref[...] / rate_ref[...], axis=1, keepdims=True)
    theta_ref[...] = theta
    active_ref[...] = jnp.broadcast_to(active, theta.shape)
    item_line = lists[:owners] * float(LANES) + lists[owners : 2 * owners]
    lines = (item_line, lists[2 * owners : 3 * owners], lists[3 * owners :])
    for owner in range(owners):
        for part in range(3):
            line = lines[part][owner : owner + 1, :]
            send_ref[owner, 2 * part : 2 * part + 1, :] = line[:, :LANES]
            send_ref[owner, 2 * part + 1 : 2 * part + 2, :] = line[:, LANES:]
        send_ref[owner, 6:8, :] = jnp.zeros((2, LANES), F32)
        send_ref[owner, 8:16, :] = theta


def table_kernel(shape_ref, rate_ref, table_ref):
    table_ref[...] = exp_digamma_over(shape_ref[...], rate_ref[...])


def widen(table):
    table_high, table_low = split(table)
    twice = jnp.concatenate([table_high, table_high], axis=1)
    return table_high, table_low, twice, jnp.concatenate([table_high, table_low], axis=1)


def ascend_block(theta_high, theta_both, marks, table):
    factors = table.shape[1]
    table_high, table_low, twice, both = widen(table)
    share = dot(theta_both, twice, NT) + dot(theta_high, table_low, NT)
    ratio_high, ratio_low = split(marks / share)
    wide = dot(ratio_high, both, NN)
    part = wide[:, :factors] + wide[:, factors:] + dot(ratio_low, table_high, NN)
    return ratio_high, ratio_low, part


def split_theta(theta):
    theta_high, theta_low = split(theta)
    return theta_high, jnp.concatenate([theta_high, theta_low], axis=1)


def ascend(theta, marks_ref, table_ref):
    theta_high, theta_both = split_theta(theta)
    total = jnp.zeros(theta.shape, F32)
    width = 2 * LANES
    for pair in range(marks_ref.shape[0] // 2):
        marks = jnp.concatenate([marks_ref[2 * pair], marks_ref[2 * pair + 1]], axis=1)
        table = table_ref[pair * width : (pair + 1) * width, :]
        total = total + ascend_block(theta_high, theta_both, marks, table)[2]
    return total


def build_kernel(recv_ref, table_ref, marks_ref, partial_ref):
    owners = recv_ref.shape[0]
    highs = marks_ref.shape[0]
    line_iota = lax.broadcasted_iota(jnp.int32, (LANES, 2 * LANES), 0).astype(F32)

    def wide(source, part):
        return jnp.concatenate(
            [recv_ref[source, 2 * part : 2 * part + 1, :], recv_ref[source, 2 * part + 1 : 2 * part + 2, :]],
            axis=1,
        )

    for source in range(owners):
        item = wide(source, 0).astype(jnp.int32)
        low = (item & (LANES - 1)).astype(F32)
        high = (item >> 7).astype(F32) * 8.0 + wide(source, 1)
        left = jnp.where(line_iota == high, wide(source, 2), 0.0).astype(BF16)
        right = jnp.where(line_iota == low, 1.0, 0.0).astype(BF16)
        tile = dot(left, right, NT)
        for high in range(highs):
            marks_ref[high, 8 * source : 8 * source + 8, :] = tile[8 * high : 8 * high + 8, :]
    theta = jnp.concatenate([recv_ref[source, 8:16, :] for source in range(owners)], axis=0)
    partial_ref[...] = ascend(theta, marks_ref, table_ref)


def ascend_kernel(theta_ref, marks_ref, table_ref, partial_ref, token_ref):
    total = ascend(theta_ref[...], marks_ref, table_ref)
    partial_ref[...] = total
    token_ref[...] = total[: token_ref.shape[0]]


def pack_kernel(cov_ref, weight_ref, own_ref):
    items = cov_ref.shape[1]
    own_ref[:, :items] = cov_ref[...]
    own_ref[:, items:] = weight_ref[...]


def prior_kernel(shards, *refs):
    shard_refs, refs = refs[:shards], refs[shards:]
    sum_ref, token_ref = refs[-2:]
    items = sum_ref.shape[1]
    width = 2 * LANES
    weight = jnp.concatenate([shard[:, items:] for shard in shard_refs], axis=0)
    for start in range(0, items, width):
        cov = jnp.concatenate([shard[:, start : start + width] for shard in shard_refs], axis=0)
        part = lax.dot_general(weight, cov, TN, precision=HIGHEST, preferred_element_type=F32)
        if len(refs) > 2:
            part = part + refs[0][:, start : start + width]
        sum_ref[:, start : start + width] = part
    token_ref[...] = weight[: token_ref.shape[0]]


def scale_kernel(shard_ref, sum_ref, rate_ref, scale_ref):
    items = scale_ref.shape[0]
    width = 2 * LANES
    weight = shard_ref[:, items:]
    for start in range(0, items, width):
        part = lax.dot_general(
            weight, shard_ref[:, start : start + width], TN, precision=HIGHEST, preferred_element_type=F32
        )
        prior_log = (part + sum_ref[:, start : start + width]).T
        scale_ref[start : start + width, :] = jnp.exp(prior_log) / rate_ref[start : start + width, :]


def last_kernel(shards, spot_ref, theta_ref, marks_ref, table_ref, scale_ref, shape_ref, *refs):
    shard_refs = refs[:shards]
    partial_ref, base_ref, keep_ref, send_ref, grad_ref, score_ref = refs[shards:]
    spot = spot_ref[2]
    theta = theta_ref[...]
    factors = theta.shape[1]
    theta_high, theta_both = split_theta(theta)
    total = jnp.zeros(theta.shape, F32)
    width = 2 * LANES
    for place in range(shards):
        block = spot ^ place
        here = pl.ds(pl.multiple_of(block * width, width), width)
        table = table_ref[here, :]
        marks = jnp.concatenate([marks_ref[2 * block], marks_ref[2 * block + 1]], axis=1)
        ratio_high, ratio_low, part = ascend_block(theta_high, theta_both, marks, table)
        total = total + part
        wide = dot(ratio_high, theta_both, TN)
        stats = table * (wide[:, :factors] + wide[:, factors:] + dot(ratio_low, theta_high, TN))
        target = send_ref if place % 2 else keep_ref
        target[place // 2] = stats
        base = (1.0 - step_weight) * shape_ref[here, :] + step_weight * item_prior
        if place == 0:
            base_ref[...] = base
        score = item_prior / shards - scale_ref[here, :] * (base / shards + step_weight * USER_RATIO * stats)
        score_ref[here, :] = jnp.concatenate(split(score), axis=1)
    partial_ref[...] = total
    rows = grad_ref.shape[1]
    group = 4
    for first in range(0, shards, group):
        cov = jnp.concatenate([shard[:, : score_ref.shape[0]] for shard in shard_refs[first : first + group]], axis=0)
        cov_high, cov_low = split(cov)
        wide = dot(cov_high, score_ref[...], NN)
        grad = wide[:, :factors] + wide[:, factors:] + dot(cov_low, score_ref[:, :factors], NN)
        for place in range(group):
            grad_ref[spot ^ (first + place)] = grad[place * rows : (place + 1) * rows]


def halve_kernel(held_ref, recv_ref, keep_ref, send_ref):
    for place in range(held_ref.shape[0]):
        target = send_ref if place % 2 else keep_ref
        target[place // 2] = held_ref[place] + recv_ref[place]


def close_kernel(held_ref, recv_ref, base_ref, new_ref):
    new_ref[...] = base_ref[...] + step_weight * USER_RATIO * (held_ref[0] + recv_ref[0])


def update_kernel(activity_shape, recv_ref, theta_ref, activity_ref, totals_ref, active_ref, next_ref, send_ref):
    total = jnp.sum(recv_ref[...], axis=0)
    shapes = user_prior + theta_ref[...] * total
    rates = activity_shape / activity_ref[...] + totals_ref[...]
    active = activity_base + jnp.sum(shapes / rates, axis=1, keepdims=True)
    active_ref[...] = jnp.broadcast_to(active, shapes.shape)
    theta = exp_digamma_over(shapes, rates)
    next_ref[...] = theta
    send_ref[...] = jnp.broadcast_to(theta[None], send_ref.shape)


def join_kernel(grad_ref, partial_ref, send_ref):
    y_size, rows, _ = send_ref.shape
    grad = jnp.sum(grad_ref[...], axis=0)
    users = partial_ref.shape[0] // y_size
    for y in range(y_size):
        send_ref[y, :users, :] = partial_ref[y * users : (y + 1) * users, :]
        send_ref[y, users:, :] = grad


def fan_kernel(users, recv_ref, send_ref):
    z_size, rows, _ = send_ref.shape
    total = jnp.sum(recv_ref[...], axis=0)
    for z in range(z_size):
        send_ref[z, :users, :] = total[z * users : (z + 1) * users, :]
        send_ref[z, users:, :] = total[z_size * users :, :]


def finish_kernel(
    activity_shape, root, recv_ref, theta_ref, activity_ref, totals_ref, shapes_ref, rates_ref, active_ref, grad_ref
):
    total = jnp.sum(recv_ref[...], axis=0)
    users = shapes_ref.shape[0]
    shapes = user_prior + theta_ref[...] * total[:users]
    rates = activity_shape / activity_ref[...] + totals_ref[...]
    shapes_ref[...] = shapes
    rates_ref[...] = rates
    active = activity_base + jnp.sum(shapes / rates, axis=1, keepdims=True)
    eye = lax.broadcasted_iota(jnp.int32, shapes.shape, 0) == lax.broadcasted_iota(jnp.int32, shapes.shape, 1)
    row = jnp.sum(jnp.where(eye, active, 0.0), axis=0, keepdims=True)
    active_ref[...] = row[:, :users]
    grad_ref[...] = total[users:] / root


def shards(
    item_ids,
    clicks,
    block_counts,
    user_shape0,
    user_rate0,
    item_shape,
    item_rate,
    beta_totals,
    covariates,
    cov_weight,
):
    y_size, z_size = lax.axis_size("y"), lax.axis_size("z")
    owners = y_size * z_size
    item_rows, factors = item_shape.shape
    users_here, blocks, block_width = item_ids.shape
    cov_rows = covariates.shape[0]
    slot_rows = users_here * blocks
    highs = item_rows // LANES
    user_axes, item_axes = ("y", "z"), ("x", "core")
    split_count = lax.axis_size(item_axes)
    share_rows = item_rows // split_count
    everyone = owners * users_here
    activity_shape = activity_prior + factors * user_prior

    def exchange(array, axes):
        return lax.all_to_all(array, axes, split_axis=0, concat_axis=0, tiled=True)

    spot = jnp.stack([lax.axis_index("y"), lax.axis_index("z"), lax.axis_index(item_axes)]).astype(jnp.int32)
    totals = beta_totals[None, :]
    smem = pl.BlockSpec(memory_space=pltpu.SMEM)
    vmem = pl.BlockSpec(memory_space=pltpu.VMEM)
    hbm = pl.BlockSpec(memory_space=pl.ANY)
    small = shape_of(users_here, factors)
    share = shape_of(share_rows, factors)
    send, theta, active = kernel_call(
        functools.partial(prep_kernel, owners),
        (shape_of(owners, 16, LANES), small, small),
        vmem=WHOLE_VMEM,
        in_specs=[hbm] * 5,
        scratch_shapes=[
            pltpu.SMEM((users_here,), jnp.int32),
            pltpu.VMEM((slot_rows, block_width), jnp.int32),
            pltpu.VMEM((slot_rows, block_width), jnp.int32),
            pltpu.VMEM((users_here, factors), F32),
            pltpu.VMEM((users_here, factors), F32),
            pltpu.SemaphoreType.DMA((5,)),
        ],
    )(
        block_counts,
        item_ids.reshape(slot_rows, block_width),
        clicks.reshape(slot_rows, block_width),
        user_shape0,
        user_rate0,
    )
    recv = exchange(send, user_axes)
    table = kernel_call(table_kernel, shape_of(item_rows, factors))(item_shape, item_rate)

    def swap(array, distance):
        axis, bit = ("core", 1) if distance == 1 else ("x", distance // 2)
        return lax.ppermute(array, axis, [(place, place ^ bit) for place in range(lax.axis_size(axis))])

    shards = [None] * split_count
    own = kernel_call(
        behind(pack_kernel, 2), shape_of(cov_rows, item_rows + factors), in_specs=[vmem, vmem, hbm]
    )(covariates, cov_weight, theta)
    shards[0] = own
    for distance in (1, 2, 6, 4):
        shards[distance] = swap(own, distance)
    for distance in (2, 6, 4):
        shards[distance + 1] = swap(shards[distance], 1)

    def add_prior(places, total, awaited):
        inputs = [shards[place] for place in places] + ([] if total is None else [total])
        return kernel_call(
            behind(functools.partial(prior_kernel, len(places)), len(inputs)),
            (shape_of(factors, item_rows), small),
            in_specs=[vmem] * len(inputs) + [hbm],
        )(*inputs, awaited)

    marks, partial = kernel_call(
        behind(build_kernel, 2),
        (shape_of(highs, everyone, LANES), shape_of(everyone, factors)),
        in_specs=[vmem, vmem, hbm],
    )(recv, table, own)
    prior, token = add_prior((0, 1), None, partial)
    for iteration in range(ITERS - 1):
        parts = exchange(partial.reshape(owners, users_here, factors), user_axes)
        active, theta, spread = kernel_call(
            behind(functools.partial(update_kernel, activity_shape), 4),
            (small, small, shape_of(owners, users_here, factors)),
            in_specs=[vmem] * 4 + [hbm],
        )(parts, theta, active, totals, token)
        theta_all = exchange(spread, user_axes).reshape(everyone, factors)
        if iteration == 0:
            prior, token = add_prior((2, 6), prior, spread)
            partial, token = kernel_call(
                behind(ascend_kernel, 3),
                (shape_of(everyone, factors), small),
                in_specs=[vmem, vmem, vmem, hbm],
            )(theta_all, marks, table, token)
            prior, token = add_prior((3, 7, 4), prior, token)
        else:
            scale = kernel_call(
                behind(scale_kernel, 3), shape_of(item_rows, factors), in_specs=[vmem, vmem, vmem, hbm]
            )(shards[5], prior, item_rate, spread)
    half = split_count // 2
    partial, base, held, moved, grad = kernel_call(
        functools.partial(last_kernel, split_count),
        (
            shape_of(everyone, factors),
            share,
            shape_of(half, share_rows, factors),
            shape_of(half, share_rows, factors),
            shape_of(split_count, cov_rows, factors),
        ),
        in_specs=[smem] + [vmem] * (5 + split_count),
        scratch_shapes=[pltpu.VMEM((item_rows, 2 * factors), BF16)],
    )(spot, theta_all, marks, table, scale, item_shape, *shards)

    def halve(held, moved, distance):
        half = held.shape[0] // 2
        return kernel_call(halve_kernel, (shape_of(half, share_rows, factors),) * 2)(held, swap(moved, distance))

    grad = exchange(grad, item_axes)
    held, moved = halve(held, moved, 1)
    both = kernel_call(
        behind(join_kernel, 2), shape_of(y_size, z_size * users_here + cov_rows, factors), in_specs=[vmem, vmem, hbm]
    )(grad, partial, moved)
    both = exchange(both, ("y",))
    held, moved = halve(held, moved, 2)
    both = kernel_call(
        behind(functools.partial(fan_kernel, users_here), 1),
        shape_of(z_size, users_here + cov_rows, factors),
        in_specs=[vmem, hbm],
    )(both, moved)
    both = exchange(both, ("z",))
    new_shape = kernel_call(close_kernel, share)(held, swap(moved, 4), base)
    user_shape, user_rate, active, cov_grad = kernel_call(
        functools.partial(finish_kernel, activity_shape, math.sqrt(item_rows * owners)),
        (small, small, shape_of(1, users_here), shape_of(cov_rows, factors)),
    )(both, theta, active, totals)
    return (user_shape, user_rate, active.reshape(users_here), new_shape, cov_grad)


def solution(mesh):
    fine = Mesh(mesh.devices.reshape(4, 8, 4, 2), ("y", "z", "x", "core"))
    users, items = ("y", "z"), ("x", "core")
    both = users + items
    return jax.shard_map(
        shards,
        mesh=fine,
        in_specs=(
            P(both, None, None),
            P(both, None, None),
            P(both),
            P(both, None),
            P(both, None),
            P(users, None),
            P(users, None),
            P(),
            P(items, users),
            P(items, None),
        ),
        out_specs=(
            P(both, None),
            P(both, None),
            P(both),
            P(both, None),
            P(items, None),
        ),
        check_vma=False,
    )
```

```python
import functools
import math

import jax
import jax.numpy as jnp
from jax import lax
from jax.experimental import pallas as pl
from jax.experimental.pallas import tpu as pltpu
from jax.sharding import Mesh
from jax.sharding import PartitionSpec as P

ITERS = 3
USER_RATIO = 4

user_prior = 0.3
activity_prior = 0.3
activity_base = 1.0
item_prior = 0.3
step_weight = 0.5

F32 = jnp.float32
BF16 = jnp.bfloat16
HIGHEST = lax.Precision.HIGHEST
NT = (((1,), (1,)), ((), ()))
NN = (((1,), (0,)), ((), ()))
TN = (((0,), (0,)), ((), ()))
LANES = 128
VMEM_LIMIT = 48 * 1024 * 1024
WHOLE_VMEM = 60 * 1024 * 1024


def exp_digamma_over(x, rate):
    pair = x * (x + 5.0)
    low = pair + 4.0
    high = pair + 6.0
    steps = (2.0 * x + 5.0) * (low * high + pair * (low + high)) / (pair * low * high)
    y = x + 6.0
    inv = 1.0 / y
    sq = inv * inv
    tail = 0.5 * inv + sq * (1.0 / 12.0 - sq * (1.0 / 120.0 - sq * (1.0 / 252.0)))
    return y * jnp.exp(-steps - tail) / rate


def kernel_call(kernel, out_shape, vmem=VMEM_LIMIT, **specs):
    return pl.pallas_call(
        kernel,
        out_shape=out_shape,
        compiler_params=pltpu.CompilerParams(vmem_limit_bytes=vmem),
        **specs,
    )


def behind(kernel, inputs, awaited=1):
    def wrapped(*refs):
        kernel(*refs[:inputs], *refs[inputs + awaited :])

    return wrapped


def shape_of(*dims):
    return jax.ShapeDtypeStruct(dims, F32)


def split(x):
    high = x.astype(BF16)
    return high, (x - high.astype(F32)).astype(BF16)


def dot(left, right, dims):
    return lax.dot_general(left, right, dims, preferred_element_type=F32)


def prep_kernel(
    owners,
    counts_hbm,
    ids_hbm,
    clicks_hbm,
    shape_hbm,
    rate_hbm,
    send_ref,
    theta_ref,
    active_ref,
    counts_ref,
    ids_ref,
    clicks_ref,
    shape_ref,
    rate_ref,
    sems,
):
    copies = [
        pltpu.make_async_copy(source, target, sems.at[place])
        for place, (source, target) in enumerate(
            (
                (counts_hbm, counts_ref),
                (ids_hbm, ids_ref),
                (clicks_hbm, clicks_ref),
                (shape_hbm, shape_ref),
                (rate_hbm, rate_ref),
            )
        )
    ]
    for copy in copies:
        copy.start()
    for copy in copies:
        copy.wait()
    rows = ids_ref.shape[0]
    blocks = 8
    width = 2 * LANES
    capacity = rows * LANES // owners
    before = (
        lax.broadcasted_iota(jnp.int32, (width, width), 0)
        < lax.broadcasted_iota(jnp.int32, (width, width), 1)
    )
    before = jnp.where(before, 1.0, 0.0).astype(BF16)
    owner_iota = lax.broadcasted_iota(jnp.int32, (owners, width), 0)
    rank_iota = lax.broadcasted_iota(jnp.int32, (capacity, width), 0).astype(F32)
    chunks = rows // 2
    ids_of, marks_of = [], []
    for chunk in range(chunks):
        ids = jnp.concatenate(
            [ids_ref[2 * chunk : 2 * chunk + 1, :], ids_ref[2 * chunk + 1 : 2 * chunk + 2, :]], axis=1
        )
        ids_of.append(ids)
        marks_of.append(jnp.where(owner_iota == (ids >> 11), 1.0, 0.0))
    earlier_of = dot(jnp.concatenate([marks.astype(BF16) for marks in marks_of], axis=0), before, NN)
    carry = jnp.zeros((owners, 1), F32)
    lists = jnp.zeros((4 * owners, capacity), F32)
    for chunk in range(chunks):
        user = 2 * chunk // blocks
        ids, marks = ids_of[chunk], marks_of[chunk]
        weights = []
        for row in (2 * chunk, 2 * chunk + 1):
            live = jnp.where(row % blocks < counts_ref[user], 1.0, 0.0)
            weights.append(clicks_ref[row : row + 1, :].astype(F32) * live)
        weight = jnp.concatenate(weights, axis=1)
        earlier = earlier_of[chunk * owners : (chunk + 1) * owners]
        rank = jnp.sum(marks * (earlier + carry), axis=0, keepdims=True)
        carry = carry + (earlier[:, width - 1 :] + marks[:, width - 1 :])
        place = jnp.where(rank_iota == rank, 1.0, 0.0).astype(BF16)
        high = ((ids >> 7) & 15).astype(F32)
        low = (ids & 127).astype(F32)
        payload = jnp.concatenate(
            [marks * high, marks * low, marks * float(user), marks * weight], axis=0
        ).astype(BF16)
        lists = lists + lax.dot_general(payload, place, NT, preferred_element_type=F32)
    theta = exp_digamma_over(shape_ref[...], rate_ref[...])
    active = activity_base + jnp.sum(shape_ref[...] / rate_ref[...], axis=1, keepdims=True)
    theta_ref[...] = theta
    active_ref[...] = jnp.broadcast_to(active, theta.shape)
    item_line = lists[:owners] * float(LANES) + lists[owners : 2 * owners]
    lines = (item_line, lists[2 * owners : 3 * owners], lists[3 * owners :])
    for owner in range(owners):
        for part in range(3):
            line = lines[part][owner : owner + 1, :]
            send_ref[owner, 2 * part : 2 * part + 1, :] = line[:, :LANES]
            send_ref[owner, 2 * part + 1 : 2 * part + 2, :] = line[:, LANES:]
        send_ref[owner, 6:8, :] = jnp.zeros((2, LANES), F32)
        send_ref[owner, 8:16, :] = theta


def table_kernel(shape_ref, rate_ref, table_ref):
    table_ref[...] = exp_digamma_over(shape_ref[...], rate_ref[...])


def widen(table):
    table_high, table_low = split(table)
    twice = jnp.concatenate([table_high, table_high], axis=1)
    return table_high, table_low, twice, jnp.concatenate([table_high, table_low], axis=1)


def ascend_block(theta_high, theta_both, marks, table):
    factors = table.shape[1]
    table_high, table_low, twice, both = widen(table)
    share = dot(theta_both, twice, NT) + dot(theta_high, table_low, NT)
    ratio_high, ratio_low = split(marks / share)
    wide = dot(ratio_high, both, NN)
    part = wide[:, :factors] + wide[:, factors:] + dot(ratio_low, table_high, NN)
    return ratio_high, ratio_low, part


def split_theta(theta):
    theta_high, theta_low = split(theta)
    return theta_high, jnp.concatenate([theta_high, theta_low], axis=1)


def ascend(theta, marks_ref, table_ref):
    theta_high, theta_both = split_theta(theta)
    total = jnp.zeros(theta.shape, F32)
    width = 2 * LANES
    for pair in range(marks_ref.shape[0] // 2):
        marks = jnp.concatenate([marks_ref[2 * pair], marks_ref[2 * pair + 1]], axis=1)
        table = table_ref[pair * width : (pair + 1) * width, :]
        total = total + ascend_block(theta_high, theta_both, marks, table)[2]
    return total


def build_kernel(recv_ref, table_ref, marks_ref, partial_ref):
    owners = recv_ref.shape[0]
    highs = marks_ref.shape[0]
    line_iota = lax.broadcasted_iota(jnp.int32, (LANES, 2 * LANES), 0).astype(F32)

    def wide(source, part):
        return jnp.concatenate(
            [recv_ref[source, 2 * part : 2 * part + 1, :], recv_ref[source, 2 * part + 1 : 2 * part + 2, :]],
            axis=1,
        )

    for source in range(owners):
        item = wide(source, 0).astype(jnp.int32)
        low = (item & (LANES - 1)).astype(F32)
        high = (item >> 7).astype(F32) * 8.0 + wide(source, 1)
        left = jnp.where(line_iota == high, wide(source, 2), 0.0).astype(BF16)
        right = jnp.where(line_iota == low, 1.0, 0.0).astype(BF16)
        tile = dot(left, right, NT)
        for high in range(highs):
            marks_ref[high, 8 * source : 8 * source + 8, :] = tile[8 * high : 8 * high + 8, :]
    theta = jnp.concatenate([recv_ref[source, 8:16, :] for source in range(owners)], axis=0)
    partial_ref[...] = ascend(theta, marks_ref, table_ref)


def ascend_kernel(theta_ref, marks_ref, table_ref, partial_ref, token_ref):
    total = ascend(theta_ref[...], marks_ref, table_ref)
    partial_ref[...] = total
    token_ref[...] = total[: token_ref.shape[0]]


def pack_kernel(cov_ref, weight_ref, own_ref):
    items = cov_ref.shape[1]
    own_ref[:, :items] = cov_ref[...]
    own_ref[:, items:] = weight_ref[...]


def touch_kernel(weight_ref, token_ref):
    token_ref[...] = weight_ref[: token_ref.shape[0], :]


def scale_kernel(shards, *refs):
    shard_refs = refs[:shards]
    rate_ref, scale_ref = refs[shards:]
    items = scale_ref.shape[0]
    width = 2 * LANES
    weight = jnp.concatenate([shard[:, items:] for shard in shard_refs], axis=0)
    for start in range(0, items, width):
        cov = jnp.concatenate([shard[:, start : start + width] for shard in shard_refs], axis=0)
        prior_log = lax.dot_general(weight, cov, TN, precision=HIGHEST, preferred_element_type=F32).T
        scale_ref[start : start + width, :] = jnp.exp(prior_log) / rate_ref[start : start + width, :]


def last_kernel(shards, spot_ref, theta_ref, marks_hbm, table_hbm, scale_hbm, shape_hbm, *refs):
    shard_hbm, refs = refs[:shards], refs[shards:]
    partial_ref, base_ref, keep_ref, send_ref, grad_ref = refs[:5]
    marks_ref, table_ref, scale_ref, shape_ref, cov_ref, score_ref, block_sems, shard_sems = refs[5:]
    spot = spot_ref[2]
    width = 2 * LANES
    copies = []
    for place in range(shards):
        block = spot ^ place
        here = pl.ds(pl.multiple_of(block * width, width), width)
        pairs = [(marks_hbm.at[pl.ds(2 * block, 2)], marks_ref.at[place])]
        for source, target in ((table_hbm, table_ref), (scale_hbm, scale_ref), (shape_hbm, shape_ref)):
            pairs.append((source.at[here], target.at[place]))
        copies.append(
            [
                pltpu.make_async_copy(source, target, block_sems.at[place, index])
                for index, (source, target) in enumerate(pairs)
            ]
        )
    shard_copies = [
        pltpu.make_async_copy(source, cov_ref.at[place], shard_sems.at[place])
        for place, source in enumerate(shard_hbm)
    ]
    for copy in [copy for group in copies for copy in group] + shard_copies:
        copy.start()
    theta = theta_ref[...]
    factors = theta.shape[1]
    theta_high, theta_both = split_theta(theta)
    total = jnp.zeros(theta.shape, F32)
    for place in range(shards):
        for copy in copies[place]:
            copy.wait()
        table = table_ref[place]
        marks = jnp.concatenate([marks_ref[place, 0], marks_ref[place, 1]], axis=1)
        ratio_high, ratio_low, part = ascend_block(theta_high, theta_both, marks, table)
        total = total + part
        wide = dot(ratio_high, theta_both, TN)
        stats = table * (wide[:, :factors] + wide[:, factors:] + dot(ratio_low, theta_high, TN))
        target = send_ref if place % 2 else keep_ref
        target[place // 2] = stats
        base = (1.0 - step_weight) * shape_ref[place] + step_weight * item_prior
        if place == 0:
            base_ref[...] = base
        score = item_prior / shards - scale_ref[place] * (base / shards + step_weight * USER_RATIO * stats)
        here = pl.ds(pl.multiple_of((spot ^ place) * width, width), width)
        score_ref[here, :] = jnp.concatenate(split(score), axis=1)
    partial_ref[...] = total
    rows = grad_ref.shape[1]
    group = 4
    items = score_ref.shape[0]
    for first in range(0, shards, group):
        for copy in shard_copies[first : first + group]:
            copy.wait()
        cov = jnp.concatenate([cov_ref[place, :, :items] for place in range(first, first + group)], axis=0)
        cov_high, cov_low = split(cov)
        wide = dot(cov_high, score_ref[...], NN)
        grad = wide[:, :factors] + wide[:, factors:] + dot(cov_low, score_ref[:, :factors], NN)
        for place in range(group):
            grad_ref[spot ^ (first + place)] = grad[place * rows : (place + 1) * rows]


def halve_kernel(held_ref, recv_ref, keep_ref, send_ref):
    for place in range(held_ref.shape[0]):
        target = send_ref if place % 2 else keep_ref
        target[place // 2] = held_ref[place] + recv_ref[place]


def close_kernel(held_ref, recv_ref, base_ref, new_ref):
    new_ref[...] = base_ref[...] + step_weight * USER_RATIO * (held_ref[0] + recv_ref[0])


def update_kernel(activity_shape, recv_ref, theta_ref, activity_ref, totals_ref, active_ref, next_ref, send_ref):
    total = jnp.sum(recv_ref[...], axis=0)
    shapes = user_prior + theta_ref[...] * total
    rates = activity_shape / activity_ref[...] + totals_ref[...]
    active = activity_base + jnp.sum(shapes / rates, axis=1, keepdims=True)
    active_ref[...] = jnp.broadcast_to(active, shapes.shape)
    theta = exp_digamma_over(shapes, rates)
    next_ref[...] = theta
    send_ref[...] = jnp.broadcast_to(theta[None], send_ref.shape)


def join_kernel(grad_ref, partial_ref, send_ref):
    y_size, rows, _ = send_ref.shape
    grad = jnp.sum(grad_ref[...], axis=0)
    users = partial_ref.shape[0] // y_size
    for y in range(y_size):
        send_ref[y, :users, :] = partial_ref[y * users : (y + 1) * users, :]
        send_ref[y, users:, :] = grad


def fan_kernel(users, recv_ref, send_ref):
    z_size, rows, _ = send_ref.shape
    total = jnp.sum(recv_ref[...], axis=0)
    for z in range(z_size):
        send_ref[z, :users, :] = total[z * users : (z + 1) * users, :]
        send_ref[z, users:, :] = total[z_size * users :, :]


def finish_kernel(
    activity_shape, root, recv_ref, theta_ref, activity_ref, totals_ref, shapes_ref, rates_ref, active_ref, grad_ref
):
    total = jnp.sum(recv_ref[...], axis=0)
    users = shapes_ref.shape[0]
    shapes = user_prior + theta_ref[...] * total[:users]
    rates = activity_shape / activity_ref[...] + totals_ref[...]
    shapes_ref[...] = shapes
    rates_ref[...] = rates
    active = activity_base + jnp.sum(shapes / rates, axis=1, keepdims=True)
    eye = lax.broadcasted_iota(jnp.int32, shapes.shape, 0) == lax.broadcasted_iota(jnp.int32, shapes.shape, 1)
    row = jnp.sum(jnp.where(eye, active, 0.0), axis=0, keepdims=True)
    active_ref[...] = row[:, :users]
    grad_ref[...] = total[users:] / root


def shards(
    item_ids,
    clicks,
    block_counts,
    user_shape0,
    user_rate0,
    item_shape,
    item_rate,
    beta_totals,
    covariates,
    cov_weight,
):
    y_size, z_size = lax.axis_size("y"), lax.axis_size("z")
    owners = y_size * z_size
    item_rows, factors = item_shape.shape
    users_here, blocks, block_width = item_ids.shape
    cov_rows = covariates.shape[0]
    slot_rows = users_here * blocks
    highs = item_rows // LANES
    user_axes, item_axes = ("y", "z"), ("x", "core")
    split_count = lax.axis_size(item_axes)
    share_rows = item_rows // split_count
    everyone = owners * users_here
    activity_shape = activity_prior + factors * user_prior

    def exchange(array, axes):
        return lax.all_to_all(array, axes, split_axis=0, concat_axis=0, tiled=True)

    spot = jnp.stack([lax.axis_index("y"), lax.axis_index("z"), lax.axis_index(item_axes)]).astype(jnp.int32)
    totals = beta_totals[None, :]
    smem = pl.BlockSpec(memory_space=pltpu.SMEM)
    vmem = pl.BlockSpec(memory_space=pltpu.VMEM)
    hbm = pl.BlockSpec(memory_space=pl.ANY)
    small = shape_of(users_here, factors)
    share = shape_of(share_rows, factors)
    send, theta, active = kernel_call(
        functools.partial(prep_kernel, owners),
        (shape_of(owners, 16, LANES), small, small),
        vmem=WHOLE_VMEM,
        in_specs=[hbm] * 5,
        scratch_shapes=[
            pltpu.SMEM((users_here,), jnp.int32),
            pltpu.VMEM((slot_rows, block_width), jnp.int32),
            pltpu.VMEM((slot_rows, block_width), jnp.int32),
            pltpu.VMEM((users_here, factors), F32),
            pltpu.VMEM((users_here, factors), F32),
            pltpu.SemaphoreType.DMA((5,)),
        ],
    )(
        block_counts,
        item_ids.reshape(slot_rows, block_width),
        clicks.reshape(slot_rows, block_width),
        user_shape0,
        user_rate0,
    )
    recv = exchange(send, user_axes)
    table = kernel_call(table_kernel, shape_of(item_rows, factors))(item_shape, item_rate)

    def swap(array, distance):
        axis, bit = ("core", 1) if distance == 1 else ("x", distance // 2)
        return lax.ppermute(array, axis, [(place, place ^ bit) for place in range(lax.axis_size(axis))])

    shards = [None] * split_count
    own = kernel_call(
        behind(pack_kernel, 2), shape_of(cov_rows, item_rows + factors), in_specs=[vmem, vmem, hbm]
    )(covariates, cov_weight, theta)
    shards[0] = own
    for distance in (1, 2, 6, 4):
        shards[distance] = swap(own, distance)
    for distance in (2, 6, 4):
        shards[distance + 1] = swap(shards[distance], 1)

    def touch(*awaited):
        return kernel_call(
            behind(touch_kernel, 1, len(awaited)), small, in_specs=[vmem] + [hbm] * len(awaited)
        )(cov_weight, *awaited)

    marks, partial = kernel_call(
        behind(build_kernel, 2),
        (shape_of(highs, everyone, LANES), shape_of(everyone, factors)),
        in_specs=[vmem, vmem, hbm],
    )(recv, table, own)
    token = touch(partial, marks, shards[1])
    for iteration in range(ITERS - 1):
        parts = exchange(partial.reshape(owners, users_here, factors), user_axes)
        active, theta, spread = kernel_call(
            behind(functools.partial(update_kernel, activity_shape), 4, 2),
            (small, small, shape_of(owners, users_here, factors)),
            in_specs=[vmem] * 4 + [hbm] * 2,
        )(parts, theta, active, totals, token, marks)
        theta_all = exchange(spread, user_axes).reshape(everyone, factors)
        if iteration == 0:
            token = touch(spread, marks, shards[2], shards[6])
            partial, token = kernel_call(
                behind(ascend_kernel, 3),
                (shape_of(everyone, factors), small),
                in_specs=[vmem, vmem, vmem, hbm],
            )(theta_all, marks, table, token)
            token = touch(token, marks, shards[3], shards[4], shards[7])
        else:
            scale = kernel_call(
                behind(functools.partial(scale_kernel, split_count), split_count + 1, 2),
                shape_of(item_rows, factors),
                in_specs=[vmem] * (split_count + 1) + [hbm] * 2,
            )(*shards, item_rate, spread, marks)
    half = split_count // 2
    partial, base, held, moved, grad = kernel_call(
        functools.partial(last_kernel, split_count),
        (
            shape_of(everyone, factors),
            share,
            shape_of(half, share_rows, factors),
            shape_of(half, share_rows, factors),
            shape_of(split_count, cov_rows, factors),
        ),
        in_specs=[smem, vmem] + [hbm] * (4 + split_count),
        scratch_shapes=[
            pltpu.VMEM((split_count, highs // split_count, everyone, LANES), F32),
            pltpu.VMEM((split_count, share_rows, factors), F32),
            pltpu.VMEM((split_count, share_rows, factors), F32),
            pltpu.VMEM((split_count, share_rows, factors), F32),
            pltpu.VMEM((split_count, cov_rows, item_rows + factors), F32),
            pltpu.VMEM((item_rows, 2 * factors), BF16),
            pltpu.SemaphoreType.DMA((split_count, 4)),
            pltpu.SemaphoreType.DMA((split_count,)),
        ],
    )(spot, theta_all, marks, table, scale, item_shape, *shards)

    def halve(held, moved, distance):
        half = held.shape[0] // 2
        return kernel_call(halve_kernel, (shape_of(half, share_rows, factors),) * 2)(held, swap(moved, distance))

    grad = exchange(grad, item_axes)
    held, moved = halve(held, moved, 1)
    both = kernel_call(
        behind(join_kernel, 2), shape_of(y_size, z_size * users_here + cov_rows, factors), in_specs=[vmem, vmem, hbm]
    )(grad, partial, moved)
    both = exchange(both, ("y",))
    held, moved = halve(held, moved, 2)
    both = kernel_call(
        behind(functools.partial(fan_kernel, users_here), 1),
        shape_of(z_size, users_here + cov_rows, factors),
        in_specs=[vmem, hbm],
    )(both, moved)
    both = exchange(both, ("z",))
    new_shape = kernel_call(close_kernel, share)(held, swap(moved, 4), base)
    user_shape, user_rate, active, cov_grad = kernel_call(
        functools.partial(finish_kernel, activity_shape, math.sqrt(item_rows * owners)),
        (small, small, shape_of(1, users_here), shape_of(cov_rows, factors)),
    )(both, theta, active, totals)
    return (user_shape, user_rate, active.reshape(users_here), new_shape, cov_grad)


def solution(mesh):
    fine = Mesh(mesh.devices.reshape(4, 8, 4, 2), ("y", "z", "x", "core"))
    users, items = ("y", "z"), ("x", "core")
    both = users + items
    return jax.shard_map(
        shards,
        mesh=fine,
        in_specs=(
            P(both, None, None),
            P(both, None, None),
            P(both),
            P(both, None),
            P(both, None),
            P(users, None),
            P(users, None),
            P(),
            P(items, users),
            P(items, None),
        ),
        out_specs=(
            P(both, None),
            P(both, None),
            P(both),
            P(both, None),
            P(items, None),
        ),
        check_vma=False,
    )
```

```python
import functools
import math

import jax
import jax.numpy as jnp
from jax import lax
from jax.experimental import pallas as pl
from jax.experimental.pallas import tpu as pltpu
from jax.sharding import Mesh
from jax.sharding import PartitionSpec as P

ITERS = 3
USER_RATIO = 4

user_prior = 0.3
activity_prior = 0.3
activity_base = 1.0
item_prior = 0.3
step_weight = 0.5

F32 = jnp.float32
BF16 = jnp.bfloat16
HIGHEST = lax.Precision.HIGHEST
NT = (((1,), (1,)), ((), ()))
NN = (((1,), (0,)), ((), ()))
TN = (((0,), (0,)), ((), ()))
LANES = 128
VMEM_LIMIT = 48 * 1024 * 1024
WHOLE_VMEM = 60 * 1024 * 1024


def exp_digamma_over(x, rate):
    pair = x * (x + 5.0)
    low = pair + 4.0
    high = pair + 6.0
    steps = (2.0 * x + 5.0) * (low * high + pair * (low + high)) / (pair * low * high)
    y = x + 6.0
    inv = 1.0 / y
    sq = inv * inv
    tail = 0.5 * inv + sq * (1.0 / 12.0 - sq * (1.0 / 120.0 - sq * (1.0 / 252.0)))
    return y * jnp.exp(-steps - tail) / rate


def kernel_call(kernel, out_shape, vmem=VMEM_LIMIT, **specs):
    return pl.pallas_call(
        kernel,
        out_shape=out_shape,
        compiler_params=pltpu.CompilerParams(vmem_limit_bytes=vmem),
        **specs,
    )


def behind(kernel, inputs, awaited=1):
    def wrapped(*refs):
        kernel(*refs[:inputs], *refs[inputs + awaited :])

    return wrapped


def shape_of(*dims):
    return jax.ShapeDtypeStruct(dims, F32)


def split(x):
    high = x.astype(BF16)
    return high, (x - high.astype(F32)).astype(BF16)


def dot(left, right, dims):
    return lax.dot_general(left, right, dims, preferred_element_type=F32)


def prep_kernel(
    owners,
    counts_hbm,
    ids_hbm,
    clicks_hbm,
    shape_hbm,
    rate_hbm,
    cov_hbm,
    weight_hbm,
    send_ref,
    theta_ref,
    active_ref,
    own_hbm,
    counts_ref,
    ids_ref,
    clicks_ref,
    shape_ref,
    rate_ref,
    sems,
):
    copies = [
        pltpu.make_async_copy(source, target, sems.at[place])
        for place, (source, target) in enumerate(
            (
                (counts_hbm, counts_ref),
                (ids_hbm, ids_ref),
                (clicks_hbm, clicks_ref),
                (shape_hbm, shape_ref),
                (rate_hbm, rate_ref),
            )
        )
    ]
    items = cov_hbm.shape[1]
    pack = [
        pltpu.make_async_copy(cov_hbm, own_hbm.at[:, pl.ds(0, items)], sems.at[len(copies)]),
        pltpu.make_async_copy(
            weight_hbm, own_hbm.at[:, pl.ds(items, weight_hbm.shape[1])], sems.at[len(copies) + 1]
        ),
    ]
    for copy in copies + pack:
        copy.start()
    for copy in copies:
        copy.wait()
    rows = ids_ref.shape[0]
    blocks = 8
    width = 2 * LANES
    capacity = rows * LANES // owners
    before = (
        lax.broadcasted_iota(jnp.int32, (width, width), 0)
        < lax.broadcasted_iota(jnp.int32, (width, width), 1)
    )
    before = jnp.where(before, 1.0, 0.0).astype(BF16)
    owner_iota = lax.broadcasted_iota(jnp.int32, (owners, width), 0)
    rank_iota = lax.broadcasted_iota(jnp.int32, (capacity, width), 0).astype(F32)
    chunks = rows // 2
    ids_of, marks_of = [], []
    for chunk in range(chunks):
        ids = jnp.concatenate(
            [ids_ref[2 * chunk : 2 * chunk + 1, :], ids_ref[2 * chunk + 1 : 2 * chunk + 2, :]], axis=1
        )
        ids_of.append(ids)
        marks_of.append(jnp.where(owner_iota == (ids >> 11), 1.0, 0.0))
    earlier_of = dot(jnp.concatenate([marks.astype(BF16) for marks in marks_of], axis=0), before, NN)
    carry = jnp.zeros((owners, 1), F32)
    lists = jnp.zeros((4 * owners, capacity), F32)
    for chunk in range(chunks):
        user = 2 * chunk // blocks
        ids, marks = ids_of[chunk], marks_of[chunk]
        weights = []
        for row in (2 * chunk, 2 * chunk + 1):
            live = jnp.where(row % blocks < counts_ref[user], 1.0, 0.0)
            weights.append(clicks_ref[row : row + 1, :].astype(F32) * live)
        weight = jnp.concatenate(weights, axis=1)
        earlier = earlier_of[chunk * owners : (chunk + 1) * owners]
        rank = jnp.sum(marks * (earlier + carry), axis=0, keepdims=True)
        carry = carry + (earlier[:, width - 1 :] + marks[:, width - 1 :])
        place = jnp.where(rank_iota == rank, 1.0, 0.0).astype(BF16)
        high = ((ids >> 7) & 15).astype(F32)
        low = (ids & 127).astype(F32)
        payload = jnp.concatenate(
            [marks * high, marks * low, marks * float(user), marks * weight], axis=0
        ).astype(BF16)
        lists = lists + lax.dot_general(payload, place, NT, preferred_element_type=F32)
    theta = exp_digamma_over(shape_ref[...], rate_ref[...])
    active = activity_base + jnp.sum(shape_ref[...] / rate_ref[...], axis=1, keepdims=True)
    theta_ref[...] = theta
    active_ref[...] = jnp.broadcast_to(active, theta.shape)
    item_line = lists[:owners] * float(LANES) + lists[owners : 2 * owners]
    lines = (item_line, lists[2 * owners : 3 * owners], lists[3 * owners :])
    for owner in range(owners):
        for part in range(3):
            line = lines[part][owner : owner + 1, :]
            send_ref[owner, 2 * part : 2 * part + 1, :] = line[:, :LANES]
            send_ref[owner, 2 * part + 1 : 2 * part + 2, :] = line[:, LANES:]
        send_ref[owner, 6:8, :] = jnp.zeros((2, LANES), F32)
        send_ref[owner, 8:16, :] = theta
    for copy in pack:
        copy.wait()


def table_kernel(shape_ref, rate_ref, table_ref):
    table_ref[...] = exp_digamma_over(shape_ref[...], rate_ref[...])


def widen(table):
    table_high, table_low = split(table)
    twice = jnp.concatenate([table_high, table_high], axis=1)
    return table_high, table_low, twice, jnp.concatenate([table_high, table_low], axis=1)


def ascend_block(theta_high, theta_both, marks, table):
    factors = table.shape[1]
    table_high, table_low, twice, both = widen(table)
    share = dot(theta_both, twice, NT) + dot(theta_high, table_low, NT)
    ratio_high, ratio_low = split(marks / share)
    wide = dot(ratio_high, both, NN)
    part = wide[:, :factors] + wide[:, factors:] + dot(ratio_low, table_high, NN)
    return ratio_high, ratio_low, part


def split_theta(theta):
    theta_high, theta_low = split(theta)
    return theta_high, jnp.concatenate([theta_high, theta_low], axis=1)


def ascend(theta, marks_ref, table_ref):
    theta_high, theta_both = split_theta(theta)
    total = jnp.zeros(theta.shape, F32)
    width = 2 * LANES
    for pair in range(marks_ref.shape[0] // 2):
        marks = jnp.concatenate([marks_ref[2 * pair], marks_ref[2 * pair + 1]], axis=1)
        table = table_ref[pair * width : (pair + 1) * width, :]
        total = total + ascend_block(theta_high, theta_both, marks, table)[2]
    return total


def build_kernel(recv_ref, table_ref, marks_ref, partial_ref):
    owners = recv_ref.shape[0]
    highs = marks_ref.shape[0]
    line_iota = lax.broadcasted_iota(jnp.int32, (LANES, 2 * LANES), 0).astype(F32)

    def wide(source, part):
        return jnp.concatenate(
            [recv_ref[source, 2 * part : 2 * part + 1, :], recv_ref[source, 2 * part + 1 : 2 * part + 2, :]],
            axis=1,
        )

    for source in range(owners):
        item = wide(source, 0).astype(jnp.int32)
        low = (item & (LANES - 1)).astype(F32)
        high = (item >> 7).astype(F32) * 8.0 + wide(source, 1)
        left = jnp.where(line_iota == high, wide(source, 2), 0.0).astype(BF16)
        right = jnp.where(line_iota == low, 1.0, 0.0).astype(BF16)
        tile = dot(left, right, NT)
        for high in range(highs):
            marks_ref[high, 8 * source : 8 * source + 8, :] = tile[8 * high : 8 * high + 8, :]
    theta = jnp.concatenate([recv_ref[source, 8:16, :] for source in range(owners)], axis=0)
    partial_ref[...] = ascend(theta, marks_ref, table_ref)


def ascend_kernel(theta_ref, marks_ref, table_ref, partial_ref, token_ref):
    total = ascend(theta_ref[...], marks_ref, table_ref)
    partial_ref[...] = total
    token_ref[...] = total[: token_ref.shape[0]]


def touch_kernel(weight_ref, token_ref):
    token_ref[...] = weight_ref[: token_ref.shape[0], :]


def scale_kernel(shards, *refs):
    shard_refs = refs[:shards]
    rate_ref, scale_ref = refs[shards:]
    items = scale_ref.shape[0]
    width = 2 * LANES
    weight = jnp.concatenate([shard[:, items:] for shard in shard_refs], axis=0)
    for start in range(0, items, width):
        cov = jnp.concatenate([shard[:, start : start + width] for shard in shard_refs], axis=0)
        prior_log = lax.dot_general(weight, cov, TN, precision=HIGHEST, preferred_element_type=F32).T
        scale_ref[start : start + width, :] = jnp.exp(prior_log) / rate_ref[start : start + width, :]


def last_kernel(shards, spot_ref, theta_ref, marks_hbm, table_hbm, scale_hbm, shape_hbm, *refs):
    shard_hbm, refs = refs[:shards], refs[shards:]
    partial_ref, base_ref, keep_ref, send_ref, grad_ref = refs[:5]
    marks_ref, table_ref, scale_ref, shape_ref, cov_ref, score_ref, block_sems, shard_sems = refs[5:]
    spot = spot_ref[2]
    width = 2 * LANES
    copies = []
    for place in range(shards):
        block = spot ^ place
        here = pl.ds(pl.multiple_of(block * width, width), width)
        pairs = [(marks_hbm.at[pl.ds(2 * block, 2)], marks_ref.at[place])]
        for source, target in ((table_hbm, table_ref), (scale_hbm, scale_ref), (shape_hbm, shape_ref)):
            pairs.append((source.at[here], target.at[place]))
        copies.append(
            [
                pltpu.make_async_copy(source, target, block_sems.at[place, index])
                for index, (source, target) in enumerate(pairs)
            ]
        )
    shard_copies = [
        pltpu.make_async_copy(source, cov_ref.at[place], shard_sems.at[place])
        for place, source in enumerate(shard_hbm)
    ]
    ahead = 2
    for copy in [copy for group in copies[:ahead] for copy in group]:
        copy.start()
    theta = theta_ref[...]
    factors = theta.shape[1]
    theta_high, theta_both = split_theta(theta)
    total = jnp.zeros(theta.shape, F32)
    for place in range(shards):
        for copy in copies[place]:
            copy.wait()
        for copy in (copies[place + ahead] if place + ahead < shards else []) + [shard_copies[place]]:
            copy.start()
        table = table_ref[place]
        marks = jnp.concatenate([marks_ref[place, 0], marks_ref[place, 1]], axis=1)
        ratio_high, ratio_low, part = ascend_block(theta_high, theta_both, marks, table)
        total = total + part
        wide = dot(ratio_high, theta_both, TN)
        stats = table * (wide[:, :factors] + wide[:, factors:] + dot(ratio_low, theta_high, TN))
        target = send_ref if place % 2 else keep_ref
        target[place // 2] = stats
        base = (1.0 - step_weight) * shape_ref[place] + step_weight * item_prior
        if place == 0:
            base_ref[...] = base
        score = item_prior / shards - scale_ref[place] * (base / shards + step_weight * USER_RATIO * stats)
        here = pl.ds(pl.multiple_of((spot ^ place) * width, width), width)
        score_ref[here, :] = jnp.concatenate(split(score), axis=1)
    partial_ref[...] = total
    rows = grad_ref.shape[1]
    group = 4
    items = score_ref.shape[0]
    for first in range(0, shards, group):
        for copy in shard_copies[first : first + group]:
            copy.wait()
        cov = jnp.concatenate([cov_ref[place, :, :items] for place in range(first, first + group)], axis=0)
        cov_high, cov_low = split(cov)
        wide = dot(cov_high, score_ref[...], NN)
        grad = wide[:, :factors] + wide[:, factors:] + dot(cov_low, score_ref[:, :factors], NN)
        for place in range(group):
            grad_ref[spot ^ (first + place)] = grad[place * rows : (place + 1) * rows]


def halve_kernel(held_ref, recv_ref, keep_ref, send_ref):
    for place in range(held_ref.shape[0]):
        target = send_ref if place % 2 else keep_ref
        target[place // 2] = held_ref[place] + recv_ref[place]


def close_kernel(held_ref, recv_ref, base_ref, new_ref):
    new_ref[...] = base_ref[...] + step_weight * USER_RATIO * (held_ref[0] + recv_ref[0])


def update_kernel(activity_shape, recv_ref, theta_ref, activity_ref, totals_ref, active_ref, next_ref, send_ref):
    total = jnp.sum(recv_ref[...], axis=0)
    shapes = user_prior + theta_ref[...] * total
    rates = activity_shape / activity_ref[...] + totals_ref[...]
    active = activity_base + jnp.sum(shapes / rates, axis=1, keepdims=True)
    active_ref[...] = jnp.broadcast_to(active, shapes.shape)
    theta = exp_digamma_over(shapes, rates)
    next_ref[...] = theta
    send_ref[...] = jnp.broadcast_to(theta[None], send_ref.shape)


def join_kernel(grad_ref, partial_ref, send_ref):
    y_size, rows, _ = send_ref.shape
    grad = jnp.sum(grad_ref[...], axis=0)
    users = partial_ref.shape[0] // y_size
    for y in range(y_size):
        send_ref[y, :users, :] = partial_ref[y * users : (y + 1) * users, :]
        send_ref[y, users:, :] = grad


def fan_kernel(users, recv_ref, send_ref):
    z_size, rows, _ = send_ref.shape
    total = jnp.sum(recv_ref[...], axis=0)
    for z in range(z_size):
        send_ref[z, :users, :] = total[z * users : (z + 1) * users, :]
        send_ref[z, users:, :] = total[z_size * users :, :]


def finish_kernel(
    activity_shape, root, recv_ref, theta_ref, activity_ref, totals_ref, shapes_ref, rates_ref, active_ref, grad_ref
):
    total = jnp.sum(recv_ref[...], axis=0)
    users = shapes_ref.shape[0]
    shapes = user_prior + theta_ref[...] * total[:users]
    rates = activity_shape / activity_ref[...] + totals_ref[...]
    shapes_ref[...] = shapes
    rates_ref[...] = rates
    active = activity_base + jnp.sum(shapes / rates, axis=1, keepdims=True)
    eye = lax.broadcasted_iota(jnp.int32, shapes.shape, 0) == lax.broadcasted_iota(jnp.int32, shapes.shape, 1)
    row = jnp.sum(jnp.where(eye, active, 0.0), axis=0, keepdims=True)
    active_ref[...] = row[:, :users]
    grad_ref[...] = total[users:] / root


def shards(
    item_ids,
    clicks,
    block_counts,
    user_shape0,
    user_rate0,
    item_shape,
    item_rate,
    beta_totals,
    covariates,
    cov_weight,
):
    y_size, z_size = lax.axis_size("y"), lax.axis_size("z")
    owners = y_size * z_size
    item_rows, factors = item_shape.shape
    users_here, blocks, block_width = item_ids.shape
    cov_rows = covariates.shape[0]
    slot_rows = users_here * blocks
    highs = item_rows // LANES
    user_axes, item_axes = ("y", "z"), ("x", "core")
    split_count = lax.axis_size(item_axes)
    share_rows = item_rows // split_count
    everyone = owners * users_here
    activity_shape = activity_prior + factors * user_prior

    def exchange(array, axes):
        return lax.all_to_all(array, axes, split_axis=0, concat_axis=0, tiled=True)

    spot = jnp.stack([lax.axis_index("y"), lax.axis_index("z"), lax.axis_index(item_axes)]).astype(jnp.int32)
    totals = beta_totals[None, :]
    smem = pl.BlockSpec(memory_space=pltpu.SMEM)
    vmem = pl.BlockSpec(memory_space=pltpu.VMEM)
    hbm = pl.BlockSpec(memory_space=pl.ANY)
    small = shape_of(users_here, factors)
    share = shape_of(share_rows, factors)
    send, theta, active, own = kernel_call(
        functools.partial(prep_kernel, owners),
        (shape_of(owners, 16, LANES), small, small, shape_of(cov_rows, item_rows + factors)),
        vmem=WHOLE_VMEM,
        in_specs=[hbm] * 7,
        out_specs=(vmem, vmem, vmem, hbm),
        scratch_shapes=[
            pltpu.SMEM((users_here,), jnp.int32),
            pltpu.VMEM((slot_rows, block_width), jnp.int32),
            pltpu.VMEM((slot_rows, block_width), jnp.int32),
            pltpu.VMEM((users_here, factors), F32),
            pltpu.VMEM((users_here, factors), F32),
            pltpu.SemaphoreType.DMA((7,)),
        ],
    )(
        block_counts,
        item_ids.reshape(slot_rows, block_width),
        clicks.reshape(slot_rows, block_width),
        user_shape0,
        user_rate0,
        covariates,
        cov_weight,
    )
    recv = exchange(send, user_axes)
    table = kernel_call(table_kernel, shape_of(item_rows, factors))(item_shape, item_rate)

    def swap(array, distance):
        axis, bit = ("core", 1) if distance == 1 else ("x", distance // 2)
        return lax.ppermute(array, axis, [(place, place ^ bit) for place in range(lax.axis_size(axis))])

    shards = [None] * split_count
    shards[0] = own
    for distance in (1, 2, 6, 4):
        shards[distance] = swap(own, distance)
    for distance in (2, 6, 4):
        shards[distance + 1] = swap(shards[distance], 1)

    def touch(*awaited):
        return kernel_call(
            behind(touch_kernel, 1, len(awaited)), small, in_specs=[vmem] + [hbm] * len(awaited)
        )(cov_weight, *awaited)

    marks, partial = kernel_call(
        build_kernel, (shape_of(highs, everyone, LANES), shape_of(everyone, factors))
    )(recv, table)
    awaited = (marks,)
    for iteration in range(ITERS - 1):
        parts = exchange(partial.reshape(owners, users_here, factors), user_axes)
        active, theta, spread = kernel_call(
            behind(functools.partial(update_kernel, activity_shape), 4, len(awaited)),
            (small, small, shape_of(owners, users_here, factors)),
            in_specs=[vmem] * 4 + [hbm] * len(awaited),
        )(parts, theta, active, totals, *awaited)
        theta_all = exchange(spread, user_axes).reshape(everyone, factors)
        if iteration == 0:
            token = touch(spread, marks, shards[2], shards[6])
            partial, token = kernel_call(
                behind(ascend_kernel, 3),
                (shape_of(everyone, factors), small),
                in_specs=[vmem, vmem, vmem, hbm],
            )(theta_all, marks, table, token)
            awaited = (touch(token, marks, shards[1], shards[3], shards[4], shards[7]), marks)
        else:
            scale = kernel_call(
                behind(functools.partial(scale_kernel, split_count), split_count + 1, 2),
                shape_of(item_rows, factors),
                in_specs=[vmem] * (split_count + 1) + [hbm] * 2,
            )(*shards, item_rate, spread, marks)
    half = split_count // 2
    partial, base, held, moved, grad = kernel_call(
        functools.partial(last_kernel, split_count),
        (
            shape_of(everyone, factors),
            share,
            shape_of(half, share_rows, factors),
            shape_of(half, share_rows, factors),
            shape_of(split_count, cov_rows, factors),
        ),
        in_specs=[smem, vmem] + [hbm] * (4 + split_count),
        scratch_shapes=[
            pltpu.VMEM((split_count, highs // split_count, everyone, LANES), F32),
            pltpu.VMEM((split_count, share_rows, factors), F32),
            pltpu.VMEM((split_count, share_rows, factors), F32),
            pltpu.VMEM((split_count, share_rows, factors), F32),
            pltpu.VMEM((split_count, cov_rows, item_rows + factors), F32),
            pltpu.VMEM((item_rows, 2 * factors), BF16),
            pltpu.SemaphoreType.DMA((split_count, 4)),
            pltpu.SemaphoreType.DMA((split_count,)),
        ],
    )(spot, theta_all, marks, table, scale, item_shape, *shards)

    def halve(held, moved, distance):
        half = held.shape[0] // 2
        return kernel_call(halve_kernel, (shape_of(half, share_rows, factors),) * 2)(held, swap(moved, distance))

    grad = exchange(grad, item_axes)
    held, moved = halve(held, moved, 1)
    both = kernel_call(
        behind(join_kernel, 2), shape_of(y_size, z_size * users_here + cov_rows, factors), in_specs=[vmem, vmem, hbm]
    )(grad, partial, moved)
    both = exchange(both, ("y",))
    held, moved = halve(held, moved, 2)
    both = kernel_call(
        behind(functools.partial(fan_kernel, users_here), 1),
        shape_of(z_size, users_here + cov_rows, factors),
        in_specs=[vmem, hbm],
    )(both, moved)
    both = exchange(both, ("z",))
    new_shape = kernel_call(close_kernel, share)(held, swap(moved, 4), base)
    user_shape, user_rate, active, cov_grad = kernel_call(
        functools.partial(finish_kernel, activity_shape, math.sqrt(item_rows * owners)),
        (small, small, shape_of(1, users_here), shape_of(cov_rows, factors)),
    )(both, theta, active, totals)
    return (user_shape, user_rate, active.reshape(users_here), new_shape, cov_grad)


def solution(mesh):
    fine = Mesh(mesh.devices.reshape(4, 8, 4, 2), ("y", "z", "x", "core"))
    users, items = ("y", "z"), ("x", "core")
    both = users + items
    return jax.shard_map(
        shards,
        mesh=fine,
        in_specs=(
            P(both, None, None),
            P(both, None, None),
            P(both),
            P(both, None),
            P(both, None),
            P(users, None),
            P(users, None),
            P(),
            P(items, users),
            P(items, None),
        ),
        out_specs=(
            P(both, None),
            P(both, None),
            P(both),
            P(both, None),
            P(items, None),
        ),
        check_vma=False,
    )
```

```python
import functools
import math

import jax
import jax.numpy as jnp
from jax import lax
from jax.experimental import pallas as pl
from jax.experimental.pallas import tpu as pltpu
from jax.sharding import Mesh
from jax.sharding import PartitionSpec as P

ITERS = 3
USER_RATIO = 4

user_prior = 0.3
activity_prior = 0.3
activity_base = 1.0
item_prior = 0.3
step_weight = 0.5

F32 = jnp.float32
BF16 = jnp.bfloat16
HIGHEST = lax.Precision.HIGHEST
NT = (((1,), (1,)), ((), ()))
NN = (((1,), (0,)), ((), ()))
TN = (((0,), (0,)), ((), ()))
LANES = 128
VMEM_LIMIT = 32 * 1024 * 1024


def exp_digamma_over(x, rate):
    pair = x * (x + 5.0)
    low = pair + 4.0
    high = pair + 6.0
    steps = (2.0 * x + 5.0) * (low * high + pair * (low + high)) / (pair * low * high)
    y = x + 6.0
    inv = 1.0 / y
    sq = inv * inv
    tail = 0.5 * inv + sq * (1.0 / 12.0 - sq * (1.0 / 120.0 - sq * (1.0 / 252.0)))
    return y * jnp.exp(-steps - tail) / rate


def kernel_call(kernel, out_shape, **specs):
    return pl.pallas_call(
        kernel,
        out_shape=out_shape,
        compiler_params=pltpu.CompilerParams(vmem_limit_bytes=VMEM_LIMIT),
        **specs,
    )


def behind(kernel, inputs, awaited=1):
    def wrapped(*refs):
        kernel(*refs[:inputs], *refs[inputs + awaited :])

    return wrapped


def shape_of(*dims):
    return jax.ShapeDtypeStruct(dims, F32)


def on_chip(*dims):
    return pltpu.VMEM(dims, F32)


def off_chip(*dims):
    return pltpu.HBM(dims, F32)


def stay(array):
    return pltpu.with_memory_space_constraint(array, pltpu.VMEM)


def away(array):
    return pltpu.with_memory_space_constraint(array, pltpu.HBM)


def split(x):
    high = x.astype(BF16)
    return high, (x - high.astype(F32)).astype(BF16)


def dot(left, right, dims):
    return lax.dot_general(left, right, dims, preferred_element_type=F32)


def prep_kernel(
    owners,
    counts_hbm,
    ids_hbm,
    clicks_hbm,
    shape_hbm,
    rate_hbm,
    cov_hbm,
    weight_hbm,
    send_ref,
    theta_ref,
    active_ref,
    own_ref,
    counts_ref,
    ids_ref,
    clicks_ref,
    shape_ref,
    rate_ref,
    sems,
):
    copies = [
        pltpu.make_async_copy(source, target, sems.at[place])
        for place, (source, target) in enumerate(
            (
                (counts_hbm, counts_ref),
                (ids_hbm, ids_ref),
                (clicks_hbm, clicks_ref),
                (shape_hbm, shape_ref),
                (rate_hbm, rate_ref),
            )
        )
    ]
    items = cov_hbm.shape[1]
    pack = [
        pltpu.make_async_copy(cov_hbm, own_ref.at[:, pl.ds(0, items)], sems.at[len(copies)]),
        pltpu.make_async_copy(
            weight_hbm, own_ref.at[:, pl.ds(items, weight_hbm.shape[1])], sems.at[len(copies) + 1]
        ),
    ]
    for copy in copies + pack:
        copy.start()
    for copy in copies:
        copy.wait()
    rows = ids_ref.shape[0]
    blocks = 8
    width = 2 * LANES
    capacity = rows * LANES // owners
    before = (
        lax.broadcasted_iota(jnp.int32, (width, width), 0)
        < lax.broadcasted_iota(jnp.int32, (width, width), 1)
    )
    before = jnp.where(before, 1.0, 0.0).astype(BF16)
    owner_iota = lax.broadcasted_iota(jnp.int32, (owners, width), 0)
    rank_iota = lax.broadcasted_iota(jnp.int32, (capacity, width), 0).astype(F32)
    chunks = rows // 2
    ids_of, marks_of = [], []
    for chunk in range(chunks):
        ids = jnp.concatenate(
            [ids_ref[2 * chunk : 2 * chunk + 1, :], ids_ref[2 * chunk + 1 : 2 * chunk + 2, :]], axis=1
        )
        ids_of.append(ids)
        marks_of.append(jnp.where(owner_iota == (ids >> 11), 1.0, 0.0))
    earlier_of = dot(jnp.concatenate([marks.astype(BF16) for marks in marks_of], axis=0), before, NN)
    carry = jnp.zeros((owners, 1), F32)
    lists = jnp.zeros((4 * owners, capacity), F32)
    for chunk in range(chunks):
        user = 2 * chunk // blocks
        ids, marks = ids_of[chunk], marks_of[chunk]
        weights = []
        for row in (2 * chunk, 2 * chunk + 1):
            live = jnp.where(row % blocks < counts_ref[user], 1.0, 0.0)
            weights.append(clicks_ref[row : row + 1, :].astype(F32) * live)
        weight = jnp.concatenate(weights, axis=1)
        earlier = earlier_of[chunk * owners : (chunk + 1) * owners]
        rank = jnp.sum(marks * (earlier + carry), axis=0, keepdims=True)
        carry = carry + (earlier[:, width - 1 :] + marks[:, width - 1 :])
        place = jnp.where(rank_iota == rank, 1.0, 0.0).astype(BF16)
        high = ((ids >> 7) & 15).astype(F32)
        low = (ids & 127).astype(F32)
        payload = jnp.concatenate(
            [marks * high, marks * low, marks * float(user), marks * weight], axis=0
        ).astype(BF16)
        lists = lists + lax.dot_general(payload, place, NT, preferred_element_type=F32)
    theta = exp_digamma_over(shape_ref[...], rate_ref[...])
    active = activity_base + jnp.sum(shape_ref[...] / rate_ref[...], axis=1, keepdims=True)
    theta_ref[...] = theta
    active_ref[...] = jnp.broadcast_to(active, theta.shape)
    item_line = lists[:owners] * float(LANES) + lists[owners : 2 * owners]
    lines = (item_line, lists[2 * owners : 3 * owners], lists[3 * owners :])
    for owner in range(owners):
        for part in range(3):
            line = lines[part][owner : owner + 1, :]
            send_ref[owner, 2 * part : 2 * part + 1, :] = line[:, :LANES]
            send_ref[owner, 2 * part + 1 : 2 * part + 2, :] = line[:, LANES:]
        send_ref[owner, 6:8, :] = jnp.zeros((2, LANES), F32)
        send_ref[owner, 8:16, :] = theta
    for copy in pack:
        copy.wait()


def table_kernel(shape_ref, rate_ref, table_ref, base_ref):
    shapes = shape_ref[...]
    table_ref[...] = exp_digamma_over(shapes, rate_ref[...])
    base_ref[...] = (1.0 - step_weight) * shapes + step_weight * item_prior


def widen(table):
    table_high, table_low = split(table)
    twice = jnp.concatenate([table_high, table_high], axis=1)
    return table_high, table_low, twice, jnp.concatenate([table_high, table_low], axis=1)


def ascend_block(theta_high, theta_both, marks, table):
    factors = table.shape[1]
    table_high, table_low, twice, both = widen(table)
    share = dot(theta_both, twice, NT) + dot(theta_high, table_low, NT)
    ratio_high, ratio_low = split(marks / share)
    wide = dot(ratio_high, both, NN)
    part = wide[:, :factors] + wide[:, factors:] + dot(ratio_low, table_high, NN)
    return ratio_high, ratio_low, part


def split_theta(theta):
    theta_high, theta_low = split(theta)
    return theta_high, jnp.concatenate([theta_high, theta_low], axis=1)


def ascend(theta, marks_ref, table_ref):
    theta_high, theta_both = split_theta(theta)
    total = jnp.zeros(theta.shape, F32)
    width = 2 * LANES
    for pair in range(marks_ref.shape[0] // 2):
        marks = jnp.concatenate([marks_ref[2 * pair], marks_ref[2 * pair + 1]], axis=1)
        table = table_ref[pair * width : (pair + 1) * width, :]
        total = total + ascend_block(theta_high, theta_both, marks, table)[2]
    return total


def build_kernel(recv_ref, table_ref, marks_ref, partial_ref):
    owners = recv_ref.shape[0]
    highs = marks_ref.shape[0]
    line_iota = lax.broadcasted_iota(jnp.int32, (LANES, 2 * LANES), 0).astype(F32)

    def wide(source, part):
        return jnp.concatenate(
            [recv_ref[source, 2 * part : 2 * part + 1, :], recv_ref[source, 2 * part + 1 : 2 * part + 2, :]],
            axis=1,
        )

    for source in range(owners):
        item = wide(source, 0).astype(jnp.int32)
        low = (item & (LANES - 1)).astype(F32)
        high = (item >> 7).astype(F32) * 8.0 + wide(source, 1)
        left = jnp.where(line_iota == high, wide(source, 2), 0.0).astype(BF16)
        right = jnp.where(line_iota == low, 1.0, 0.0).astype(BF16)
        tile = dot(left, right, NT)
        for high in range(highs):
            marks_ref[high, 8 * source : 8 * source + 8, :] = tile[8 * high : 8 * high + 8, :]
    theta = jnp.concatenate([recv_ref[source, 8:16, :] for source in range(owners)], axis=0)
    partial_ref[...] = ascend(theta, marks_ref, table_ref)


def ascend_kernel(theta_ref, marks_ref, table_ref, partial_ref, token_ref):
    total = ascend(theta_ref[...], marks_ref, table_ref)
    partial_ref[...] = total
    token_ref[...] = total[: token_ref.shape[0]]


def touch_kernel(weight_ref, token_ref):
    token_ref[...] = weight_ref[: token_ref.shape[0], :]


def scale_kernel(shards, *refs):
    shard_refs = refs[:shards]
    rate_ref, scale_ref = refs[shards:]
    items = scale_ref.shape[0]
    width = 2 * LANES
    weight = jnp.concatenate([shard[:, items:] for shard in shard_refs], axis=0)
    for start in range(0, items, width):
        cov = jnp.concatenate([shard[:, start : start + width] for shard in shard_refs], axis=0)
        prior_log = lax.dot_general(weight, cov, TN, precision=HIGHEST, preferred_element_type=F32).T
        scale_ref[start : start + width, :] = jnp.exp(prior_log) / rate_ref[start : start + width, :]


def last_kernel(shards, spot_ref, theta_ref, marks_ref, table_ref, scale_hbm, base_hbm, *refs):
    shard_hbm, refs = refs[:shards], refs[shards:]
    partial_ref, here_ref, keep_hbm, send_hbm, grad_ref = refs[:5]
    scale_ref, base_ref, cov_ref, stats_ref, score_ref, item_sems, shard_sems, stats_sems = refs[5:]
    spot = spot_ref[2]
    item_copies = [
        pltpu.make_async_copy(source, target, item_sems.at[index])
        for index, (source, target) in enumerate(((scale_hbm, scale_ref), (base_hbm, base_ref)))
    ]
    shard_copies = [
        pltpu.make_async_copy(source, cov_ref.at[place], shard_sems.at[place])
        for place, source in enumerate(shard_hbm)
    ]
    stats_copies = [
        pltpu.make_async_copy(
            stats_ref.at[place], (send_hbm if place % 2 else keep_hbm).at[place // 2], stats_sems.at[place]
        )
        for place in range(shards)
    ]
    for copy in item_copies:
        copy.start()
    theta = theta_ref[...]
    factors = theta.shape[1]
    theta_high, theta_both = split_theta(theta)
    total = jnp.zeros(theta.shape, F32)
    width = 2 * LANES
    for place in range(shards):
        block = spot ^ place
        here = pl.ds(pl.multiple_of(block * width, width), width)
        table = table_ref[here, :]
        marks = jnp.concatenate([marks_ref[2 * block], marks_ref[2 * block + 1]], axis=1)
        ratio_high, ratio_low, part = ascend_block(theta_high, theta_both, marks, table)
        total = total + part
        wide = dot(ratio_high, theta_both, TN)
        stats_ref[place] = table * (wide[:, :factors] + wide[:, factors:] + dot(ratio_low, theta_high, TN))
        stats_copies[place].start()
        shard_copies[place].start()
    partial_ref[...] = total
    for copy in item_copies:
        copy.wait()
    for place in range(shards):
        here = pl.ds(pl.multiple_of((spot ^ place) * width, width), width)
        base = base_ref[here, :]
        if place == 0:
            here_ref[...] = base
        score = item_prior / shards - scale_ref[here, :] * (
            base / shards + step_weight * USER_RATIO * stats_ref[place]
        )
        score_ref[here, :] = jnp.concatenate(split(score), axis=1)
    rows = grad_ref.shape[1]
    group = 4
    items = score_ref.shape[0]
    for first in range(0, shards, group):
        for copy in shard_copies[first : first + group]:
            copy.wait()
        cov = jnp.concatenate([cov_ref[place, :, :items] for place in range(first, first + group)], axis=0)
        cov_high, cov_low = split(cov)
        wide = dot(cov_high, score_ref[...], NN)
        grad = wide[:, :factors] + wide[:, factors:] + dot(cov_low, score_ref[:, :factors], NN)
        for place in range(group):
            grad_ref[spot ^ (first + place)] = grad[place * rows : (place + 1) * rows]
    for copy in stats_copies:
        copy.wait()


def halve_kernel(held_ref, recv_ref, keep_ref, send_ref):
    for place in range(held_ref.shape[0]):
        target = send_ref if place % 2 else keep_ref
        target[place // 2] = held_ref[place] + recv_ref[place]


def close_kernel(held_ref, recv_ref, base_ref, new_ref):
    new_ref[...] = base_ref[...] + step_weight * USER_RATIO * (held_ref[0] + recv_ref[0])


def update_kernel(activity_shape, recv_ref, theta_ref, activity_ref, totals_ref, active_ref, next_ref, send_ref):
    total = jnp.sum(recv_ref[...], axis=0)
    shapes = user_prior + theta_ref[...] * total
    rates = activity_shape / activity_ref[...] + totals_ref[...]
    active = activity_base + jnp.sum(shapes / rates, axis=1, keepdims=True)
    active_ref[...] = jnp.broadcast_to(active, shapes.shape)
    theta = exp_digamma_over(shapes, rates)
    next_ref[...] = theta
    send_ref[...] = jnp.broadcast_to(theta[None], send_ref.shape)


def join_kernel(grad_ref, partial_ref, send_ref):
    y_size, rows, _ = send_ref.shape
    grad = jnp.sum(grad_ref[...], axis=0)
    users = partial_ref.shape[0] // y_size
    for y in range(y_size):
        send_ref[y, :users, :] = partial_ref[y * users : (y + 1) * users, :]
        send_ref[y, users:, :] = grad


def fan_kernel(users, recv_ref, send_ref):
    z_size, rows, _ = send_ref.shape
    total = jnp.sum(recv_ref[...], axis=0)
    for z in range(z_size):
        send_ref[z, :users, :] = total[z * users : (z + 1) * users, :]
        send_ref[z, users:, :] = total[z_size * users :, :]


def finish_kernel(
    activity_shape, root, recv_ref, theta_ref, activity_ref, totals_ref, shapes_ref, rates_ref, active_ref, grad_ref
):
    total = jnp.sum(recv_ref[...], axis=0)
    users = shapes_ref.shape[0]
    shapes = user_prior + theta_ref[...] * total[:users]
    rates = activity_shape / activity_ref[...] + totals_ref[...]
    shapes_ref[...] = shapes
    rates_ref[...] = rates
    active = activity_base + jnp.sum(shapes / rates, axis=1, keepdims=True)
    eye = lax.broadcasted_iota(jnp.int32, shapes.shape, 0) == lax.broadcasted_iota(jnp.int32, shapes.shape, 1)
    row = jnp.sum(jnp.where(eye, active, 0.0), axis=0, keepdims=True)
    active_ref[...] = row[:, :users]
    grad_ref[...] = total[users:] / root


def shards(
    item_ids,
    clicks,
    block_counts,
    user_shape0,
    user_rate0,
    item_shape,
    item_rate,
    beta_totals,
    covariates,
    cov_weight,
):
    y_size, z_size = lax.axis_size("y"), lax.axis_size("z")
    owners = y_size * z_size
    item_rows, factors = item_shape.shape
    users_here, blocks, block_width = item_ids.shape
    cov_rows = covariates.shape[0]
    slot_rows = users_here * blocks
    highs = item_rows // LANES
    user_axes, item_axes = ("y", "z"), ("x", "core")
    split_count = lax.axis_size(item_axes)
    share_rows = item_rows // split_count
    everyone = owners * users_here
    activity_shape = activity_prior + factors * user_prior

    def exchange(array, axes):
        return lax.all_to_all(array, axes, split_axis=0, concat_axis=0, tiled=True)

    spot = jnp.stack([lax.axis_index("y"), lax.axis_index("z"), lax.axis_index(item_axes)]).astype(jnp.int32)
    totals = beta_totals[None, :]
    smem = pl.BlockSpec(memory_space=pltpu.SMEM)
    vmem = pl.BlockSpec(memory_space=pltpu.VMEM)
    hbm = pl.BlockSpec(memory_space=pl.ANY)
    small = shape_of(users_here, factors)
    share = shape_of(share_rows, factors)
    send, theta, active, own = kernel_call(
        functools.partial(prep_kernel, owners),
        (off_chip(owners, 16, LANES), small, small, off_chip(cov_rows, item_rows + factors)),
        in_specs=[hbm] * 7,
        scratch_shapes=[
            pltpu.SMEM((users_here,), jnp.int32),
            pltpu.VMEM((slot_rows, block_width), jnp.int32),
            pltpu.VMEM((slot_rows, block_width), jnp.int32),
            pltpu.VMEM((users_here, factors), F32),
            pltpu.VMEM((users_here, factors), F32),
            pltpu.SemaphoreType.DMA((7,)),
        ],
    )(
        away(block_counts),
        away(item_ids.reshape(slot_rows, block_width)),
        away(clicks.reshape(slot_rows, block_width)),
        away(user_shape0),
        away(user_rate0),
        away(covariates),
        away(cov_weight),
    )
    recv = exchange(send, user_axes)
    table, base = kernel_call(table_kernel, (on_chip(item_rows, factors), off_chip(item_rows, factors)))(
        item_shape, item_rate
    )
    table = stay(table)

    def swap(array, distance):
        axis, bit = ("core", 1) if distance == 1 else ("x", distance // 2)
        return lax.ppermute(array, axis, [(place, place ^ bit) for place in range(lax.axis_size(axis))])

    shards = [None] * split_count
    shards[0] = away(own)
    for distance in (1, 2, 6, 4):
        shards[distance] = swap(own, distance)
    for distance in (2, 6, 4):
        shards[distance + 1] = swap(shards[distance], 1)

    def touch(*awaited):
        return kernel_call(
            behind(touch_kernel, 1, len(awaited)), small, in_specs=[vmem] + [hbm] * len(awaited)
        )(cov_weight, *awaited)

    marks, partial = kernel_call(
        build_kernel, (on_chip(highs, everyone, LANES), off_chip(everyone, factors))
    )(recv, table)
    marks = stay(marks)
    awaited = ()
    for iteration in range(ITERS - 1):
        parts = exchange(partial.reshape(owners, users_here, factors), user_axes)
        active, theta, spread = kernel_call(
            behind(functools.partial(update_kernel, activity_shape), 4, len(awaited)),
            (small, small, off_chip(owners, users_here, factors)),
            in_specs=[vmem] * 4 + [hbm] * len(awaited),
        )(parts, theta, active, totals, *awaited)
        theta_all = exchange(spread, user_axes).reshape(everyone, factors)
        if iteration == 0:
            token = touch(away(spread), shards[2], shards[6])
            partial, token = kernel_call(
                behind(ascend_kernel, 3),
                (off_chip(everyone, factors), small),
                in_specs=[vmem, vmem, vmem, hbm],
            )(theta_all, marks, table, token)
            awaited = (touch(token, shards[1], shards[3], shards[4], shards[7]),)
        else:
            scale = kernel_call(
                behind(functools.partial(scale_kernel, split_count), split_count + 1),
                off_chip(item_rows, factors),
                in_specs=[vmem] * (split_count + 1) + [hbm],
            )(*shards, item_rate, away(spread))
    half = split_count // 2
    partial, base, held, moved, grad = kernel_call(
        functools.partial(last_kernel, split_count),
        (
            shape_of(everyone, factors),
            shape_of(share_rows, factors),
            off_chip(half, share_rows, factors),
            off_chip(half, share_rows, factors),
            off_chip(split_count, cov_rows, factors),
        ),
        in_specs=[smem] + [vmem] * 3 + [hbm] * (2 + split_count),
        out_specs=(vmem, vmem, hbm, hbm, vmem),
        scratch_shapes=[
            pltpu.VMEM((item_rows, factors), F32),
            pltpu.VMEM((item_rows, factors), F32),
            pltpu.VMEM((split_count, cov_rows, item_rows + factors), F32),
            pltpu.VMEM((split_count, share_rows, factors), F32),
            pltpu.VMEM((item_rows, 2 * factors), BF16),
            pltpu.SemaphoreType.DMA((2,)),
            pltpu.SemaphoreType.DMA((split_count,)),
            pltpu.SemaphoreType.DMA((split_count,)),
        ],
    )(spot, theta_all, marks, table, away(scale), away(base), *shards)

    def halve(held, moved, distance):
        half = held.shape[0] // 2
        return kernel_call(halve_kernel, (shape_of(half, share_rows, factors),) * 2)(held, swap(moved, distance))

    grad = exchange(grad, item_axes)
    held, moved = halve(held, moved, 1)
    both = kernel_call(
        behind(join_kernel, 2), off_chip(y_size, z_size * users_here + cov_rows, factors), in_specs=[vmem, vmem, hbm]
    )(grad, partial, moved)
    both = exchange(both, ("y",))
    held, moved = halve(held, moved, 2)
    both = kernel_call(
        behind(functools.partial(fan_kernel, users_here), 1),
        off_chip(z_size, users_here + cov_rows, factors),
        in_specs=[vmem, hbm],
    )(both, moved)
    both = exchange(both, ("z",))
    new_shape = kernel_call(close_kernel, share)(held, swap(moved, 4), base)
    user_shape, user_rate, active, cov_grad = kernel_call(
        functools.partial(finish_kernel, activity_shape, math.sqrt(item_rows * owners)),
        (small, small, shape_of(1, users_here), shape_of(cov_rows, factors)),
    )(both, theta, active, totals)
    return (user_shape, user_rate, active.reshape(users_here), new_shape, cov_grad)


def solution(mesh):
    fine = Mesh(mesh.devices.reshape(4, 8, 4, 2), ("y", "z", "x", "core"))
    users, items = ("y", "z"), ("x", "core")
    both = users + items
    return jax.shard_map(
        shards,
        mesh=fine,
        in_specs=(
            P(both, None, None),
            P(both, None, None),
            P(both),
            P(both, None),
            P(both, None),
            P(users, None),
            P(users, None),
            P(),
            P(items, users),
            P(items, None),
        ),
        out_specs=(
            P(both, None),
            P(both, None),
            P(both),
            P(both, None),
            P(items, None),
        ),
        check_vma=False,
    )
```

```python
import functools
import math

import jax
import jax.numpy as jnp
from jax import lax
from jax.experimental import pallas as pl
from jax.experimental.pallas import tpu as pltpu
from jax.sharding import Mesh
from jax.sharding import PartitionSpec as P

ITERS = 3
USER_RATIO = 4

user_prior = 0.3
activity_prior = 0.3
activity_base = 1.0
item_prior = 0.3
step_weight = 0.5

F32 = jnp.float32
BF16 = jnp.bfloat16
HIGHEST = lax.Precision.HIGHEST
NT = (((1,), (1,)), ((), ()))
NN = (((1,), (0,)), ((), ()))
TN = (((0,), (0,)), ((), ()))
LANES = 128
VMEM_LIMIT = 32 * 1024 * 1024


def exp_digamma_over(x, rate):
    pair = x * (x + 5.0)
    low = pair + 4.0
    high = pair + 6.0
    steps = (2.0 * x + 5.0) * (low * high + pair * (low + high)) / (pair * low * high)
    y = x + 6.0
    inv = 1.0 / y
    sq = inv * inv
    tail = 0.5 * inv + sq * (1.0 / 12.0 - sq * (1.0 / 120.0 - sq * (1.0 / 252.0)))
    return y * jnp.exp(-steps - tail) / rate


def kernel_call(kernel, out_shape, **specs):
    return pl.pallas_call(
        kernel,
        out_shape=out_shape,
        compiler_params=pltpu.CompilerParams(vmem_limit_bytes=VMEM_LIMIT),
        **specs,
    )


def behind(kernel, inputs, awaited=1):
    def wrapped(*refs):
        kernel(*refs[:inputs], *refs[inputs + awaited :])

    return wrapped


def shape_of(*dims):
    return jax.ShapeDtypeStruct(dims, F32)


def on_chip(*dims):
    return pltpu.VMEM(dims, F32)


def off_chip(*dims):
    return pltpu.HBM(dims, F32)


def stay(array):
    return pltpu.with_memory_space_constraint(array, pltpu.VMEM)


def away(array):
    return pltpu.with_memory_space_constraint(array, pltpu.HBM)


def split(x):
    high = x.astype(BF16)
    return high, (x - high.astype(F32)).astype(BF16)


def dot(left, right, dims):
    return lax.dot_general(left, right, dims, preferred_element_type=F32)


def prep_kernel(
    owners,
    counts_hbm,
    ids_hbm,
    clicks_hbm,
    shape_hbm,
    rate_hbm,
    cov_hbm,
    weight_hbm,
    send_ref,
    theta_ref,
    active_ref,
    own_ref,
    counts_ref,
    ids_ref,
    clicks_ref,
    shape_ref,
    rate_ref,
    sems,
):
    copies = [
        pltpu.make_async_copy(source, target, sems.at[place])
        for place, (source, target) in enumerate(
            (
                (counts_hbm, counts_ref),
                (ids_hbm, ids_ref),
                (clicks_hbm, clicks_ref),
                (shape_hbm, shape_ref),
                (rate_hbm, rate_ref),
            )
        )
    ]
    items = cov_hbm.shape[1]
    pack = [
        pltpu.make_async_copy(cov_hbm, own_ref.at[:, pl.ds(0, items)], sems.at[len(copies)]),
        pltpu.make_async_copy(
            weight_hbm, own_ref.at[:, pl.ds(items, weight_hbm.shape[1])], sems.at[len(copies) + 1]
        ),
    ]
    for copy in copies + pack:
        copy.start()
    for copy in copies:
        copy.wait()
    rows = ids_ref.shape[0]
    blocks = 8
    width = 2 * LANES
    capacity = rows * LANES // owners
    before = (
        lax.broadcasted_iota(jnp.int32, (width, width), 0)
        < lax.broadcasted_iota(jnp.int32, (width, width), 1)
    )
    before = jnp.where(before, 1.0, 0.0).astype(BF16)
    owner_iota = lax.broadcasted_iota(jnp.int32, (owners, width), 0)
    rank_iota = lax.broadcasted_iota(jnp.int32, (capacity, width), 0).astype(F32)
    chunks = rows // 2
    ids_of, marks_of = [], []
    for chunk in range(chunks):
        ids = jnp.concatenate(
            [ids_ref[2 * chunk : 2 * chunk + 1, :], ids_ref[2 * chunk + 1 : 2 * chunk + 2, :]], axis=1
        )
        ids_of.append(ids)
        marks_of.append(jnp.where(owner_iota == (ids >> 11), 1.0, 0.0))
    earlier_of = dot(jnp.concatenate([marks.astype(BF16) for marks in marks_of], axis=0), before, NN)
    carry = jnp.zeros((owners, 1), F32)
    lists = jnp.zeros((4 * owners, capacity), F32)
    for chunk in range(chunks):
        user = 2 * chunk // blocks
        ids, marks = ids_of[chunk], marks_of[chunk]
        weights = []
        for row in (2 * chunk, 2 * chunk + 1):
            live = jnp.where(row % blocks < counts_ref[user], 1.0, 0.0)
            weights.append(clicks_ref[row : row + 1, :].astype(F32) * live)
        weight = jnp.concatenate(weights, axis=1)
        earlier = earlier_of[chunk * owners : (chunk + 1) * owners]
        rank = jnp.sum(marks * (earlier + carry), axis=0, keepdims=True)
        carry = carry + (earlier[:, width - 1 :] + marks[:, width - 1 :])
        place = jnp.where(rank_iota == rank, 1.0, 0.0).astype(BF16)
        high = ((ids >> 7) & 15).astype(F32)
        low = (ids & 127).astype(F32)
        payload = jnp.concatenate(
            [marks * high, marks * low, marks * float(user), marks * weight], axis=0
        ).astype(BF16)
        lists = lists + lax.dot_general(payload, place, NT, preferred_element_type=F32)
    theta = exp_digamma_over(shape_ref[...], rate_ref[...])
    active = activity_base + jnp.sum(shape_ref[...] / rate_ref[...], axis=1, keepdims=True)
    theta_ref[...] = theta
    active_ref[...] = jnp.broadcast_to(active, theta.shape)
    item_line = lists[:owners] * float(LANES) + lists[owners : 2 * owners]
    lines = (item_line, lists[2 * owners : 3 * owners], lists[3 * owners :])
    for owner in range(owners):
        for part in range(3):
            line = lines[part][owner : owner + 1, :]
            send_ref[owner, 2 * part : 2 * part + 1, :] = line[:, :LANES]
            send_ref[owner, 2 * part + 1 : 2 * part + 2, :] = line[:, LANES:]
        send_ref[owner, 6:8, :] = jnp.zeros((2, LANES), F32)
        send_ref[owner, 8:16, :] = theta
    for copy in pack:
        copy.wait()


def table_kernel(shape_ref, rate_ref, table_ref, base_ref):
    shapes = shape_ref[...]
    table_ref[...] = exp_digamma_over(shapes, rate_ref[...])
    base_ref[...] = (1.0 - step_weight) * shapes + step_weight * item_prior


def widen(table):
    table_high, table_low = split(table)
    twice = jnp.concatenate([table_high, table_high], axis=1)
    return table_high, table_low, twice, jnp.concatenate([table_high, table_low], axis=1)


def ascend_block(theta_high, theta_both, marks, table):
    factors = table.shape[1]
    table_high, table_low, twice, both = widen(table)
    share = dot(theta_both, twice, NT) + dot(theta_high, table_low, NT)
    ratio_high, ratio_low = split(marks / share)
    wide = dot(ratio_high, both, NN)
    part = wide[:, :factors] + wide[:, factors:] + dot(ratio_low, table_high, NN)
    return ratio_high, ratio_low, part


def split_theta(theta):
    theta_high, theta_low = split(theta)
    return theta_high, jnp.concatenate([theta_high, theta_low], axis=1)


def ascend(theta, marks_ref, table_ref):
    theta_high, theta_both = split_theta(theta)
    total = jnp.zeros(theta.shape, F32)
    width = 2 * LANES
    for pair in range(marks_ref.shape[0] // 2):
        marks = jnp.concatenate([marks_ref[2 * pair], marks_ref[2 * pair + 1]], axis=1)
        table = table_ref[pair * width : (pair + 1) * width, :]
        total = total + ascend_block(theta_high, theta_both, marks, table)[2]
    return total


def build_kernel(recv_ref, table_ref, marks_ref, partial_ref):
    owners = recv_ref.shape[0]
    highs = marks_ref.shape[0]
    line_iota = lax.broadcasted_iota(jnp.int32, (LANES, 2 * LANES), 0).astype(F32)

    def wide(source, part):
        return jnp.concatenate(
            [recv_ref[source, 2 * part : 2 * part + 1, :], recv_ref[source, 2 * part + 1 : 2 * part + 2, :]],
            axis=1,
        )

    for source in range(owners):
        item = wide(source, 0).astype(jnp.int32)
        low = (item & (LANES - 1)).astype(F32)
        high = (item >> 7).astype(F32) * 8.0 + wide(source, 1)
        left = jnp.where(line_iota == high, wide(source, 2), 0.0).astype(BF16)
        right = jnp.where(line_iota == low, 1.0, 0.0).astype(BF16)
        tile = dot(left, right, NT)
        for high in range(highs):
            marks_ref[high, 8 * source : 8 * source + 8, :] = tile[8 * high : 8 * high + 8, :]
    theta = jnp.concatenate([recv_ref[source, 8:16, :] for source in range(owners)], axis=0)
    partial_ref[...] = ascend(theta, marks_ref, table_ref)


def ascend_kernel(theta_ref, marks_ref, table_ref, partial_ref):
    partial_ref[...] = ascend(theta_ref[...], marks_ref, table_ref)


def scale_kernel(shards, *refs):
    shard_refs = refs[:shards]
    rate_ref, scale_ref = refs[shards:]
    items = scale_ref.shape[0]
    width = 2 * LANES
    weight = jnp.concatenate([shard[:, items:] for shard in shard_refs], axis=0)
    for start in range(0, items, width):
        cov = jnp.concatenate([shard[:, start : start + width] for shard in shard_refs], axis=0)
        prior_log = lax.dot_general(weight, cov, TN, precision=HIGHEST, preferred_element_type=F32).T
        scale_ref[start : start + width, :] = jnp.exp(prior_log) / rate_ref[start : start + width, :]


def last_kernel(shards, spot_ref, theta_ref, marks_ref, table_ref, scale_ref, base_ref, *refs):
    shard_refs = refs[:shards]
    partial_ref, here_ref, keep_ref, send_ref, grad_ref, score_ref = refs[shards:]
    spot = spot_ref[2]
    theta = theta_ref[...]
    factors = theta.shape[1]
    theta_high, theta_both = split_theta(theta)
    total = jnp.zeros(theta.shape, F32)
    width = 2 * LANES
    for place in range(shards):
        block = spot ^ place
        here = pl.ds(pl.multiple_of(block * width, width), width)
        table = table_ref[here, :]
        marks = jnp.concatenate([marks_ref[2 * block], marks_ref[2 * block + 1]], axis=1)
        ratio_high, ratio_low, part = ascend_block(theta_high, theta_both, marks, table)
        total = total + part
        wide = dot(ratio_high, theta_both, TN)
        stats = table * (wide[:, :factors] + wide[:, factors:] + dot(ratio_low, theta_high, TN))
        (send_ref if place % 2 else keep_ref)[place // 2] = stats
        base = base_ref[here, :]
        if place == 0:
            here_ref[...] = base
        score = item_prior / shards - scale_ref[here, :] * (base / shards + step_weight * USER_RATIO * stats)
        score_ref[here, :] = jnp.concatenate(split(score), axis=1)
    partial_ref[...] = total
    rows = grad_ref.shape[1]
    group = 4
    items = score_ref.shape[0]
    for first in range(0, shards, group):
        cov = jnp.concatenate([shard[:, :items] for shard in shard_refs[first : first + group]], axis=0)
        cov_high, cov_low = split(cov)
        wide = dot(cov_high, score_ref[...], NN)
        grad = wide[:, :factors] + wide[:, factors:] + dot(cov_low, score_ref[:, :factors], NN)
        for place in range(group):
            grad_ref[spot ^ (first + place)] = grad[place * rows : (place + 1) * rows]


def halve_kernel(held_ref, recv_ref, keep_ref, send_ref):
    for place in range(held_ref.shape[0]):
        target = send_ref if place % 2 else keep_ref
        target[place // 2] = held_ref[place] + recv_ref[place]


def close_kernel(held_ref, recv_ref, base_ref, new_ref):
    new_ref[...] = base_ref[...] + step_weight * USER_RATIO * (held_ref[0] + recv_ref[0])


def update_kernel(activity_shape, recv_ref, theta_ref, activity_ref, totals_ref, active_ref, next_ref, send_ref):
    total = jnp.sum(recv_ref[...], axis=0)
    shapes = user_prior + theta_ref[...] * total
    rates = activity_shape / activity_ref[...] + totals_ref[...]
    active = activity_base + jnp.sum(shapes / rates, axis=1, keepdims=True)
    active_ref[...] = jnp.broadcast_to(active, shapes.shape)
    theta = exp_digamma_over(shapes, rates)
    next_ref[...] = theta
    send_ref[...] = jnp.broadcast_to(theta[None], send_ref.shape)


def join_kernel(grad_ref, partial_ref, send_ref):
    y_size, rows, _ = send_ref.shape
    grad = jnp.sum(grad_ref[...], axis=0)
    users = partial_ref.shape[0] // y_size
    for y in range(y_size):
        send_ref[y, :users, :] = partial_ref[y * users : (y + 1) * users, :]
        send_ref[y, users:, :] = grad


def fan_kernel(users, recv_ref, send_ref):
    z_size, rows, _ = send_ref.shape
    total = jnp.sum(recv_ref[...], axis=0)
    for z in range(z_size):
        send_ref[z, :users, :] = total[z * users : (z + 1) * users, :]
        send_ref[z, users:, :] = total[z_size * users :, :]


def finish_kernel(
    activity_shape, root, recv_ref, theta_ref, activity_ref, totals_ref, shapes_ref, rates_ref, active_ref, grad_ref
):
    total = jnp.sum(recv_ref[...], axis=0)
    users = shapes_ref.shape[0]
    shapes = user_prior + theta_ref[...] * total[:users]
    rates = activity_shape / activity_ref[...] + totals_ref[...]
    shapes_ref[...] = shapes
    rates_ref[...] = rates
    active = activity_base + jnp.sum(shapes / rates, axis=1, keepdims=True)
    eye = lax.broadcasted_iota(jnp.int32, shapes.shape, 0) == lax.broadcasted_iota(jnp.int32, shapes.shape, 1)
    row = jnp.sum(jnp.where(eye, active, 0.0), axis=0, keepdims=True)
    active_ref[...] = row[:, :users]
    grad_ref[...] = total[users:] / root


def shards(
    item_ids,
    clicks,
    block_counts,
    user_shape0,
    user_rate0,
    item_shape,
    item_rate,
    beta_totals,
    covariates,
    cov_weight,
):
    y_size, z_size = lax.axis_size("y"), lax.axis_size("z")
    owners = y_size * z_size
    item_rows, factors = item_shape.shape
    users_here, blocks, block_width = item_ids.shape
    cov_rows = covariates.shape[0]
    slot_rows = users_here * blocks
    highs = item_rows // LANES
    user_axes, item_axes = ("y", "z"), ("x", "core")
    split_count = lax.axis_size(item_axes)
    share_rows = item_rows // split_count
    everyone = owners * users_here
    activity_shape = activity_prior + factors * user_prior

    def exchange(array, axes):
        return lax.all_to_all(array, axes, split_axis=0, concat_axis=0, tiled=True)

    spot = jnp.stack([lax.axis_index("y"), lax.axis_index("z"), lax.axis_index(item_axes)]).astype(jnp.int32)
    totals = beta_totals[None, :]
    smem = pl.BlockSpec(memory_space=pltpu.SMEM)
    vmem = pl.BlockSpec(memory_space=pltpu.VMEM)
    hbm = pl.BlockSpec(memory_space=pl.ANY)
    small = shape_of(users_here, factors)
    share = shape_of(share_rows, factors)
    send, theta, active, own = kernel_call(
        functools.partial(prep_kernel, owners),
        (off_chip(owners, 16, LANES), small, small, off_chip(cov_rows, item_rows + factors)),
        in_specs=[hbm] * 7,
        scratch_shapes=[
            pltpu.SMEM((users_here,), jnp.int32),
            pltpu.VMEM((slot_rows, block_width), jnp.int32),
            pltpu.VMEM((slot_rows, block_width), jnp.int32),
            pltpu.VMEM((users_here, factors), F32),
            pltpu.VMEM((users_here, factors), F32),
            pltpu.SemaphoreType.DMA((7,)),
        ],
    )(
        away(block_counts),
        away(item_ids.reshape(slot_rows, block_width)),
        away(clicks.reshape(slot_rows, block_width)),
        away(user_shape0),
        away(user_rate0),
        away(covariates),
        away(cov_weight),
    )
    recv = exchange(send, user_axes)
    table, base = kernel_call(table_kernel, (on_chip(item_rows, factors), off_chip(item_rows, factors)))(
        item_shape, item_rate
    )
    table = stay(table)

    def swap(array, distance):
        axis, bit = ("core", 1) if distance == 1 else ("x", distance // 2)
        return lax.ppermute(array, axis, [(place, place ^ bit) for place in range(lax.axis_size(axis))])

    shards = [None] * split_count
    shards[0] = own
    for distance in (1, 2, 6, 4):
        shards[distance] = swap(own, distance)
    for distance in (2, 6, 4):
        shards[distance + 1] = swap(shards[distance], 1)

    marks, partial = kernel_call(
        build_kernel, (on_chip(highs, everyone, LANES), shape_of(everyone, factors))
    )(recv, table)
    marks = stay(marks)
    awaited = ()
    for iteration in range(ITERS - 1):
        parts = exchange(partial.reshape(owners, users_here, factors), user_axes)
        active, theta, spread = kernel_call(
            behind(functools.partial(update_kernel, activity_shape), 4, len(awaited)),
            (small, small, shape_of(owners, users_here, factors)),
            in_specs=[vmem] * 4 + [hbm] * len(awaited),
        )(parts, theta, active, totals, *awaited)
        theta_all = exchange(spread, user_axes).reshape(everyone, factors)
        if iteration == 0:
            partial = kernel_call(
                behind(ascend_kernel, 3, 2),
                shape_of(everyone, factors),
                in_specs=[vmem, vmem, vmem, hbm, hbm],
            )(theta_all, marks, table, away(shards[2]), away(shards[6]))
            awaited = [away(shards[place]) for place in (1, 3, 4, 7)]
        else:
            scale = kernel_call(
                behind(functools.partial(scale_kernel, split_count), split_count + 1),
                off_chip(item_rows, factors),
                in_specs=[vmem] * (split_count + 1) + [hbm],
            )(*[away(shard) for shard in shards], away(item_rate), away(spread))
    half = split_count // 2
    partial, base, held, moved, grad = kernel_call(
        functools.partial(last_kernel, split_count),
        (
            shape_of(everyone, factors),
            shape_of(share_rows, factors),
            off_chip(half, share_rows, factors),
            off_chip(half, share_rows, factors),
            off_chip(split_count, cov_rows, factors),
        ),
        in_specs=[smem] + [vmem] * (5 + split_count),
        scratch_shapes=[pltpu.VMEM((item_rows, 2 * factors), BF16)],
    )(spot, theta_all, marks, table, away(scale), away(base), *[away(shard) for shard in shards])
    held = away(held)

    def halve(held, moved, distance):
        half = held.shape[0] // 2
        return kernel_call(halve_kernel, (shape_of(half, share_rows, factors),) * 2)(held, swap(moved, distance))

    grad = exchange(grad, item_axes)
    held, moved = halve(held, moved, 1)
    both = kernel_call(
        behind(join_kernel, 2), off_chip(y_size, z_size * users_here + cov_rows, factors), in_specs=[vmem, vmem, hbm]
    )(grad, partial, moved)
    both = exchange(both, ("y",))
    held, moved = halve(held, moved, 2)
    both = kernel_call(
        behind(functools.partial(fan_kernel, users_here), 1),
        off_chip(z_size, users_here + cov_rows, factors),
        in_specs=[vmem, hbm],
    )(both, moved)
    both = exchange(both, ("z",))
    new_shape = kernel_call(close_kernel, share)(held, swap(moved, 4), base)
    user_shape, user_rate, active, cov_grad = kernel_call(
        functools.partial(finish_kernel, activity_shape, math.sqrt(item_rows * owners)),
        (small, small, shape_of(1, users_here), shape_of(cov_rows, factors)),
    )(both, theta, active, totals)
    return (user_shape, user_rate, active.reshape(users_here), new_shape, cov_grad)


def solution(mesh):
    fine = Mesh(mesh.devices.reshape(4, 8, 4, 2), ("y", "z", "x", "core"))
    users, items = ("y", "z"), ("x", "core")
    both = users + items
    return jax.shard_map(
        shards,
        mesh=fine,
        in_specs=(
            P(both, None, None),
            P(both, None, None),
            P(both),
            P(both, None),
            P(both, None),
            P(users, None),
            P(users, None),
            P(),
            P(items, users),
            P(items, None),
        ),
        out_specs=(
            P(both, None),
            P(both, None),
            P(both),
            P(both, None),
            P(items, None),
        ),
        check_vma=False,
    )
```

```python
import functools
import math

import jax
import jax.numpy as jnp
from jax import lax
from jax.experimental import pallas as pl
from jax.experimental.pallas import tpu as pltpu
from jax.sharding import Mesh
from jax.sharding import PartitionSpec as P

ITERS = 3
USER_RATIO = 4

user_prior = 0.3
activity_prior = 0.3
activity_base = 1.0
item_prior = 0.3
step_weight = 0.5

F32 = jnp.float32
BF16 = jnp.bfloat16
HIGHEST = lax.Precision.HIGHEST
NT = (((1,), (1,)), ((), ()))
NN = (((1,), (0,)), ((), ()))
TN = (((0,), (0,)), ((), ()))
LANES = 128
VMEM_LIMIT = 32 * 1024 * 1024


def exp_digamma_over(x, rate):
    pair = x * (x + 5.0)
    low = pair + 4.0
    high = pair + 6.0
    steps = (2.0 * x + 5.0) * (low * high + pair * (low + high)) / (pair * low * high)
    y = x + 6.0
    inv = 1.0 / y
    sq = inv * inv
    tail = 0.5 * inv + sq * (1.0 / 12.0 - sq * (1.0 / 120.0 - sq * (1.0 / 252.0)))
    return y * jnp.exp(-steps - tail) / rate


def kernel_call(kernel, out_shape, **specs):
    return pl.pallas_call(
        kernel,
        out_shape=out_shape,
        compiler_params=pltpu.CompilerParams(vmem_limit_bytes=VMEM_LIMIT),
        **specs,
    )


def behind(kernel, inputs, awaited=1):
    def wrapped(*refs):
        kernel(*refs[:inputs], *refs[inputs + awaited :])

    return wrapped


def shape_of(*dims):
    return jax.ShapeDtypeStruct(dims, F32)


def on_chip(*dims):
    return pltpu.VMEM(dims, F32)


def off_chip(*dims):
    return pltpu.HBM(dims, F32)


def stay(array):
    return pltpu.with_memory_space_constraint(array, pltpu.VMEM)


def away(array):
    return pltpu.with_memory_space_constraint(array, pltpu.HBM)


def split(x):
    high = x.astype(BF16)
    return high, (x - high.astype(F32)).astype(BF16)


def dot(left, right, dims):
    return lax.dot_general(left, right, dims, preferred_element_type=F32)


def prep_kernel(
    owners,
    counts_hbm,
    ids_hbm,
    clicks_hbm,
    shape_hbm,
    rate_hbm,
    cov_hbm,
    weight_hbm,
    send_ref,
    theta_ref,
    active_ref,
    own_ref,
    counts_ref,
    ids_ref,
    clicks_ref,
    shape_ref,
    rate_ref,
    sems,
):
    copies = [
        pltpu.make_async_copy(source, target, sems.at[place])
        for place, (source, target) in enumerate(
            (
                (counts_hbm, counts_ref),
                (ids_hbm, ids_ref),
                (clicks_hbm, clicks_ref),
                (shape_hbm, shape_ref),
                (rate_hbm, rate_ref),
            )
        )
    ]
    items = cov_hbm.shape[1]
    pack = [
        pltpu.make_async_copy(cov_hbm, own_ref.at[:, pl.ds(0, items)], sems.at[len(copies)]),
        pltpu.make_async_copy(
            weight_hbm, own_ref.at[:, pl.ds(items, weight_hbm.shape[1])], sems.at[len(copies) + 1]
        ),
    ]
    for copy in copies + pack:
        copy.start()
    for copy in copies:
        copy.wait()
    rows = ids_ref.shape[0]
    blocks = 8
    width = 2 * LANES
    capacity = rows * LANES // owners
    before = (
        lax.broadcasted_iota(jnp.int32, (width, width), 0)
        < lax.broadcasted_iota(jnp.int32, (width, width), 1)
    )
    before = jnp.where(before, 1.0, 0.0).astype(BF16)
    owner_iota = lax.broadcasted_iota(jnp.int32, (owners, width), 0)
    rank_iota = lax.broadcasted_iota(jnp.int32, (capacity, width), 0).astype(F32)
    chunks = rows // 2
    ids_of, marks_of = [], []
    for chunk in range(chunks):
        ids = jnp.concatenate(
            [ids_ref[2 * chunk : 2 * chunk + 1, :], ids_ref[2 * chunk + 1 : 2 * chunk + 2, :]], axis=1
        )
        ids_of.append(ids)
        marks_of.append(jnp.where(owner_iota == (ids >> 11), 1.0, 0.0))
    earlier_of = dot(jnp.concatenate([marks.astype(BF16) for marks in marks_of], axis=0), before, NN)
    carry = jnp.zeros((owners, 1), F32)
    lists = jnp.zeros((4 * owners, capacity), F32)
    for chunk in range(chunks):
        user = 2 * chunk // blocks
        ids, marks = ids_of[chunk], marks_of[chunk]
        weights = []
        for row in (2 * chunk, 2 * chunk + 1):
            live = jnp.where(row % blocks < counts_ref[user], 1.0, 0.0)
            weights.append(clicks_ref[row : row + 1, :].astype(F32) * live)
        weight = jnp.concatenate(weights, axis=1)
        earlier = earlier_of[chunk * owners : (chunk + 1) * owners]
        rank = jnp.sum(marks * (earlier + carry), axis=0, keepdims=True)
        carry = carry + (earlier[:, width - 1 :] + marks[:, width - 1 :])
        place = jnp.where(rank_iota == rank, 1.0, 0.0).astype(BF16)
        high = ((ids >> 7) & 15).astype(F32)
        low = (ids & 127).astype(F32)
        payload = jnp.concatenate(
            [marks * high, marks * low, marks * float(user), marks * weight], axis=0
        ).astype(BF16)
        lists = lists + lax.dot_general(payload, place, NT, preferred_element_type=F32)
    theta = exp_digamma_over(shape_ref[...], rate_ref[...])
    active = activity_base + jnp.sum(shape_ref[...] / rate_ref[...], axis=1, keepdims=True)
    theta_ref[...] = theta
    active_ref[...] = jnp.broadcast_to(active, theta.shape)
    item_line = lists[:owners] * float(LANES) + lists[owners : 2 * owners]
    lines = (item_line, lists[2 * owners : 3 * owners], lists[3 * owners :])
    for owner in range(owners):
        for part in range(3):
            line = lines[part][owner : owner + 1, :]
            send_ref[owner, 2 * part : 2 * part + 1, :] = line[:, :LANES]
            send_ref[owner, 2 * part + 1 : 2 * part + 2, :] = line[:, LANES:]
        send_ref[owner, 6:8, :] = jnp.zeros((2, LANES), F32)
        send_ref[owner, 8:16, :] = theta
    for copy in pack:
        copy.wait()


def table_kernel(shape_ref, rate_ref, table_ref, base_ref):
    shapes = shape_ref[...]
    table_ref[...] = exp_digamma_over(shapes, rate_ref[...])
    base_ref[...] = (1.0 - step_weight) * shapes + step_weight * item_prior


def widen(table):
    table_high, table_low = split(table)
    twice = jnp.concatenate([table_high, table_high], axis=1)
    return table_high, table_low, twice, jnp.concatenate([table_high, table_low], axis=1)


def ascend_block(theta_high, theta_both, marks, table):
    factors = table.shape[1]
    table_high, table_low, twice, both = widen(table)
    share = dot(theta_both, twice, NT) + dot(theta_high, table_low, NT)
    ratio_high, ratio_low = split(marks / share)
    wide = dot(ratio_high, both, NN)
    part = wide[:, :factors] + wide[:, factors:] + dot(ratio_low, table_high, NN)
    return ratio_high, ratio_low, part


def split_theta(theta):
    theta_high, theta_low = split(theta)
    return theta_high, jnp.concatenate([theta_high, theta_low], axis=1)


def ascend(theta, marks_ref, table_ref):
    theta_high, theta_both = split_theta(theta)
    total = jnp.zeros(theta.shape, F32)
    width = 2 * LANES
    for pair in range(marks_ref.shape[0] // 2):
        marks = jnp.concatenate([marks_ref[2 * pair], marks_ref[2 * pair + 1]], axis=1)
        table = table_ref[pair * width : (pair + 1) * width, :]
        total = total + ascend_block(theta_high, theta_both, marks, table)[2]
    return total


def build_kernel(recv_ref, table_ref, marks_ref, partial_ref):
    owners = recv_ref.shape[0]
    highs = marks_ref.shape[0]
    line_iota = lax.broadcasted_iota(jnp.int32, (LANES, 2 * LANES), 0).astype(F32)

    def wide(source, part):
        return jnp.concatenate(
            [recv_ref[source, 2 * part : 2 * part + 1, :], recv_ref[source, 2 * part + 1 : 2 * part + 2, :]],
            axis=1,
        )

    for source in range(owners):
        item = wide(source, 0).astype(jnp.int32)
        low = (item & (LANES - 1)).astype(F32)
        high = (item >> 7).astype(F32) * 8.0 + wide(source, 1)
        left = jnp.where(line_iota == high, wide(source, 2), 0.0).astype(BF16)
        right = jnp.where(line_iota == low, 1.0, 0.0).astype(BF16)
        tile = dot(left, right, NT)
        for high in range(highs):
            marks_ref[high, 8 * source : 8 * source + 8, :] = tile[8 * high : 8 * high + 8, :]
    theta = jnp.concatenate([recv_ref[source, 8:16, :] for source in range(owners)], axis=0)
    partial_ref[...] = ascend(theta, marks_ref, table_ref)


def ascend_kernel(theta_ref, marks_ref, table_ref, partial_ref):
    partial_ref[...] = ascend(theta_ref[...], marks_ref, table_ref)


def scale_kernel(shards, *refs):
    shard_refs = refs[:shards]
    rate_ref, scale_ref = refs[shards:]
    items = scale_ref.shape[0]
    width = 2 * LANES
    weight = jnp.concatenate([shard[:, items:] for shard in shard_refs], axis=0)
    for start in range(0, items, width):
        cov = jnp.concatenate([shard[:, start : start + width] for shard in shard_refs], axis=0)
        prior_log = lax.dot_general(weight, cov, TN, precision=HIGHEST, preferred_element_type=F32).T
        scale_ref[start : start + width, :] = jnp.exp(prior_log) / rate_ref[start : start + width, :]


def last_kernel(shards, spot_ref, theta_ref, marks_ref, table_ref, scale_ref, base_ref, *refs):
    shard_refs = refs[:shards]
    partial_ref, here_ref, keep_ref, send_ref, grad_ref, score_ref = refs[shards:]
    spot = spot_ref[2]
    theta = theta_ref[...]
    factors = theta.shape[1]
    theta_high, theta_both = split_theta(theta)
    total = jnp.zeros(theta.shape, F32)
    width = 2 * LANES
    for place in range(shards):
        block = spot ^ place
        here = pl.ds(pl.multiple_of(block * width, width), width)
        table = table_ref[here, :]
        marks = jnp.concatenate([marks_ref[2 * block], marks_ref[2 * block + 1]], axis=1)
        ratio_high, ratio_low, part = ascend_block(theta_high, theta_both, marks, table)
        total = total + part
        wide = dot(ratio_high, theta_both, TN)
        stats = table * (wide[:, :factors] + wide[:, factors:] + dot(ratio_low, theta_high, TN))
        (send_ref if place % 2 else keep_ref)[place // 2] = stats
        base = base_ref[here, :]
        if place == 0:
            here_ref[...] = base
        score = item_prior / shards - scale_ref[here, :] * (base / shards + step_weight * USER_RATIO * stats)
        score_ref[here, :] = jnp.concatenate(split(score), axis=1)
    partial_ref[...] = total
    rows = grad_ref.shape[1]
    group = 4
    items = score_ref.shape[0]
    for first in range(0, shards, group):
        cov = jnp.concatenate([shard[:, :items] for shard in shard_refs[first : first + group]], axis=0)
        cov_high, cov_low = split(cov)
        wide = dot(cov_high, score_ref[...], NN)
        grad = wide[:, :factors] + wide[:, factors:] + dot(cov_low, score_ref[:, :factors], NN)
        for place in range(group):
            grad_ref[spot ^ (first + place)] = grad[place * rows : (place + 1) * rows]


def halve_kernel(held_ref, recv_ref, keep_ref, send_ref):
    for place in range(held_ref.shape[0]):
        target = send_ref if place % 2 else keep_ref
        target[place // 2] = held_ref[place] + recv_ref[place]


def close_kernel(held_ref, recv_ref, base_ref, new_ref):
    new_ref[...] = base_ref[...] + step_weight * USER_RATIO * (held_ref[0] + recv_ref[0])


def update_kernel(activity_shape, recv_ref, theta_ref, activity_ref, totals_ref, active_ref, next_ref, send_ref):
    total = jnp.sum(recv_ref[...], axis=0)
    shapes = user_prior + theta_ref[...] * total
    rates = activity_shape / activity_ref[...] + totals_ref[...]
    active = activity_base + jnp.sum(shapes / rates, axis=1, keepdims=True)
    active_ref[...] = jnp.broadcast_to(active, shapes.shape)
    theta = exp_digamma_over(shapes, rates)
    next_ref[...] = theta
    send_ref[...] = jnp.broadcast_to(theta[None], send_ref.shape)


def join_kernel(grad_ref, partial_ref, send_ref):
    y_size, rows, _ = send_ref.shape
    grad = jnp.sum(grad_ref[...], axis=0)
    users = partial_ref.shape[0] // y_size
    for y in range(y_size):
        send_ref[y, :users, :] = partial_ref[y * users : (y + 1) * users, :]
        send_ref[y, users:, :] = grad


def fan_kernel(users, recv_ref, send_ref):
    z_size, rows, _ = send_ref.shape
    total = jnp.sum(recv_ref[...], axis=0)
    for z in range(z_size):
        send_ref[z, :users, :] = total[z * users : (z + 1) * users, :]
        send_ref[z, users:, :] = total[z_size * users :, :]


def finish_kernel(
    activity_shape, root, recv_ref, theta_ref, activity_ref, totals_ref, shapes_ref, rates_ref, active_ref, grad_ref
):
    total = jnp.sum(recv_ref[...], axis=0)
    users = shapes_ref.shape[0]
    shapes = user_prior + theta_ref[...] * total[:users]
    rates = activity_shape / activity_ref[...] + totals_ref[...]
    shapes_ref[...] = shapes
    rates_ref[...] = rates
    active = activity_base + jnp.sum(shapes / rates, axis=1, keepdims=True)
    eye = lax.broadcasted_iota(jnp.int32, shapes.shape, 0) == lax.broadcasted_iota(jnp.int32, shapes.shape, 1)
    row = jnp.sum(jnp.where(eye, active, 0.0), axis=0, keepdims=True)
    active_ref[...] = row[:, :users]
    grad_ref[...] = total[users:] / root


def shards(
    item_ids,
    clicks,
    block_counts,
    user_shape0,
    user_rate0,
    item_shape,
    item_rate,
    beta_totals,
    covariates,
    cov_weight,
):
    y_size, z_size = lax.axis_size("y"), lax.axis_size("z")
    owners = y_size * z_size
    item_rows, factors = item_shape.shape
    users_here, blocks, block_width = item_ids.shape
    cov_rows = covariates.shape[0]
    slot_rows = users_here * blocks
    highs = item_rows // LANES
    user_axes, item_axes = ("y", "z"), ("x", "core")
    split_count = lax.axis_size(item_axes)
    share_rows = item_rows // split_count
    everyone = owners * users_here
    activity_shape = activity_prior + factors * user_prior

    def exchange(array, axes):
        return lax.all_to_all(array, axes, split_axis=0, concat_axis=0, tiled=True)

    spot = jnp.stack([lax.axis_index("y"), lax.axis_index("z"), lax.axis_index(item_axes)]).astype(jnp.int32)
    totals = beta_totals[None, :]
    smem = pl.BlockSpec(memory_space=pltpu.SMEM)
    vmem = pl.BlockSpec(memory_space=pltpu.VMEM)
    hbm = pl.BlockSpec(memory_space=pl.ANY)
    small = shape_of(users_here, factors)
    share = shape_of(share_rows, factors)
    send, theta, active, own = kernel_call(
        functools.partial(prep_kernel, owners),
        (off_chip(owners, 16, LANES), small, small, off_chip(cov_rows, item_rows + factors)),
        in_specs=[hbm] * 7,
        scratch_shapes=[
            pltpu.SMEM((users_here,), jnp.int32),
            pltpu.VMEM((slot_rows, block_width), jnp.int32),
            pltpu.VMEM((slot_rows, block_width), jnp.int32),
            pltpu.VMEM((users_here, factors), F32),
            pltpu.VMEM((users_here, factors), F32),
            pltpu.SemaphoreType.DMA((7,)),
        ],
    )(
        away(block_counts),
        away(item_ids.reshape(slot_rows, block_width)),
        away(clicks.reshape(slot_rows, block_width)),
        away(user_shape0),
        away(user_rate0),
        away(covariates),
        away(cov_weight),
    )
    recv = exchange(send, user_axes)
    table, base = kernel_call(table_kernel, (on_chip(item_rows, factors), off_chip(item_rows, factors)))(
        item_shape, item_rate
    )
    table = stay(table)

    def swap(array, distance):
        axis, bit = ("core", 1) if distance == 1 else ("x", distance // 2)
        return lax.ppermute(array, axis, [(place, place ^ bit) for place in range(lax.axis_size(axis))])

    shards = [None] * split_count
    shards[0] = own
    for distance in (1, 2, 6, 4):
        shards[distance] = swap(own, distance)
    for distance in (2, 6, 4):
        shards[distance + 1] = swap(shards[distance], 1)

    marks, partial = kernel_call(
        build_kernel, (on_chip(highs, everyone, LANES), shape_of(everyone, factors))
    )(recv, table)
    marks = stay(marks)
    awaited = ()
    for iteration in range(ITERS - 1):
        parts = exchange(partial.reshape(owners, users_here, factors), user_axes)
        active, theta, spread = kernel_call(
            behind(functools.partial(update_kernel, activity_shape), 4, len(awaited)),
            (small, small, shape_of(owners, users_here, factors)),
            in_specs=[vmem] * 4 + [hbm] * len(awaited),
        )(parts, theta, active, totals, *awaited)
        theta_all = exchange(spread, user_axes).reshape(everyone, factors)
        if iteration == 0:
            awaited = [away(shards[place]) for place in (2, 6)]
            partial = kernel_call(
                behind(ascend_kernel, 3, len(awaited)),
                shape_of(everyone, factors),
                in_specs=[vmem] * 3 + [hbm] * len(awaited),
            )(theta_all, marks, table, *awaited)
            awaited = [away(shards[place]) for place in ()]
        else:
            scale = kernel_call(
                behind(functools.partial(scale_kernel, split_count), split_count + 1),
                off_chip(item_rows, factors),
                in_specs=[vmem] * (split_count + 1) + [hbm],
            )(*[away(shard) for shard in shards], away(item_rate), away(spread))
    half = split_count // 2
    partial, base, held, moved, grad = kernel_call(
        functools.partial(last_kernel, split_count),
        (
            shape_of(everyone, factors),
            shape_of(share_rows, factors),
            off_chip(half, share_rows, factors),
            off_chip(half, share_rows, factors),
            off_chip(split_count, cov_rows, factors),
        ),
        in_specs=[smem] + [vmem] * (5 + split_count),
        scratch_shapes=[pltpu.VMEM((item_rows, 2 * factors), BF16)],
    )(spot, theta_all, marks, table, away(scale), away(base), *[away(shard) for shard in shards])
    held = away(held)

    def halve(held, moved, distance):
        half = held.shape[0] // 2
        return kernel_call(halve_kernel, (shape_of(half, share_rows, factors),) * 2)(held, swap(moved, distance))

    grad = exchange(grad, item_axes)
    held, moved = halve(held, moved, 1)
    both = kernel_call(
        behind(join_kernel, 2), off_chip(y_size, z_size * users_here + cov_rows, factors), in_specs=[vmem, vmem, hbm]
    )(grad, partial, moved)
    both = exchange(both, ("y",))
    held, moved = halve(held, moved, 2)
    both = kernel_call(
        behind(functools.partial(fan_kernel, users_here), 1),
        off_chip(z_size, users_here + cov_rows, factors),
        in_specs=[vmem, hbm],
    )(both, moved)
    both = exchange(both, ("z",))
    new_shape = kernel_call(close_kernel, share)(held, swap(moved, 4), base)
    user_shape, user_rate, active, cov_grad = kernel_call(
        functools.partial(finish_kernel, activity_shape, math.sqrt(item_rows * owners)),
        (small, small, shape_of(1, users_here), shape_of(cov_rows, factors)),
    )(both, theta, active, totals)
    return (user_shape, user_rate, active.reshape(users_here), new_shape, cov_grad)


def solution(mesh):
    fine = Mesh(mesh.devices.reshape(4, 8, 4, 2), ("y", "z", "x", "core"))
    users, items = ("y", "z"), ("x", "core")
    both = users + items
    return jax.shard_map(
        shards,
        mesh=fine,
        in_specs=(
            P(both, None, None),
            P(both, None, None),
            P(both),
            P(both, None),
            P(both, None),
            P(users, None),
            P(users, None),
            P(),
            P(items, users),
            P(items, None),
        ),
        out_specs=(
            P(both, None),
            P(both, None),
            P(both),
            P(both, None),
            P(items, None),
        ),
        check_vma=False,
    )
```

```python
import functools
import math

import jax
import jax.numpy as jnp
from jax import lax
from jax.experimental import pallas as pl
from jax.experimental.pallas import tpu as pltpu
from jax.sharding import Mesh
from jax.sharding import PartitionSpec as P

ITERS = 3
USER_RATIO = 4

user_prior = 0.3
activity_prior = 0.3
activity_base = 1.0
item_prior = 0.3
step_weight = 0.5

F32 = jnp.float32
BF16 = jnp.bfloat16
HIGHEST = lax.Precision.HIGHEST
NT = (((1,), (1,)), ((), ()))
NN = (((1,), (0,)), ((), ()))
TN = (((0,), (0,)), ((), ()))
LANES = 128
VMEM_LIMIT = 32 * 1024 * 1024


def exp_digamma_over(x, rate):
    pair = x * (x + 5.0)
    low = pair + 4.0
    high = pair + 6.0
    steps = (2.0 * x + 5.0) * (low * high + pair * (low + high)) / (pair * low * high)
    y = x + 6.0
    inv = 1.0 / y
    sq = inv * inv
    tail = 0.5 * inv + sq * (1.0 / 12.0 - sq * (1.0 / 120.0 - sq * (1.0 / 252.0)))
    return y * jnp.exp(-steps - tail) / rate


def kernel_call(kernel, out_shape, **specs):
    return pl.pallas_call(
        kernel,
        out_shape=out_shape,
        compiler_params=pltpu.CompilerParams(vmem_limit_bytes=VMEM_LIMIT),
        **specs,
    )


def behind(kernel, inputs, awaited=1):
    def wrapped(*refs):
        kernel(*refs[:inputs], *refs[inputs + awaited :])

    return wrapped


def shape_of(*dims):
    return jax.ShapeDtypeStruct(dims, F32)


def on_chip(*dims):
    return pltpu.VMEM(dims, F32)


def off_chip(*dims):
    return pltpu.HBM(dims, F32)


def stay(array):
    return pltpu.with_memory_space_constraint(array, pltpu.VMEM)


def away(array):
    return pltpu.with_memory_space_constraint(array, pltpu.HBM)


def split(x):
    high = x.astype(BF16)
    return high, (x - high.astype(F32)).astype(BF16)


def dot(left, right, dims):
    return lax.dot_general(left, right, dims, preferred_element_type=F32)


def prep_kernel(
    owners,
    counts_hbm,
    ids_hbm,
    clicks_hbm,
    shape_hbm,
    rate_hbm,
    cov_hbm,
    weight_hbm,
    send_ref,
    theta_ref,
    active_ref,
    own_ref,
    counts_ref,
    ids_ref,
    clicks_ref,
    shape_ref,
    rate_ref,
    sems,
):
    copies = [
        pltpu.make_async_copy(source, target, sems.at[place])
        for place, (source, target) in enumerate(
            (
                (counts_hbm, counts_ref),
                (ids_hbm, ids_ref),
                (clicks_hbm, clicks_ref),
                (shape_hbm, shape_ref),
                (rate_hbm, rate_ref),
            )
        )
    ]
    items = cov_hbm.shape[1]
    pack = [
        pltpu.make_async_copy(cov_hbm, own_ref.at[:, pl.ds(0, items)], sems.at[len(copies)]),
        pltpu.make_async_copy(
            weight_hbm, own_ref.at[:, pl.ds(items, weight_hbm.shape[1])], sems.at[len(copies) + 1]
        ),
    ]
    for copy in copies + pack:
        copy.start()
    for copy in copies:
        copy.wait()
    rows = ids_ref.shape[0]
    blocks = 8
    width = 2 * LANES
    capacity = rows * LANES // owners
    before = (
        lax.broadcasted_iota(jnp.int32, (width, width), 0)
        < lax.broadcasted_iota(jnp.int32, (width, width), 1)
    )
    before = jnp.where(before, 1.0, 0.0).astype(BF16)
    owner_iota = lax.broadcasted_iota(jnp.int32, (owners, width), 0)
    rank_iota = lax.broadcasted_iota(jnp.int32, (capacity, width), 0).astype(F32)
    chunks = rows // 2
    ids_of, marks_of = [], []
    for chunk in range(chunks):
        ids = jnp.concatenate(
            [ids_ref[2 * chunk : 2 * chunk + 1, :], ids_ref[2 * chunk + 1 : 2 * chunk + 2, :]], axis=1
        )
        ids_of.append(ids)
        marks_of.append(jnp.where(owner_iota == (ids >> 11), 1.0, 0.0))
    earlier_of = dot(jnp.concatenate([marks.astype(BF16) for marks in marks_of], axis=0), before, NN)
    carry = jnp.zeros((owners, 1), F32)
    lists = jnp.zeros((4 * owners, capacity), F32)
    for chunk in range(chunks):
        user = 2 * chunk // blocks
        ids, marks = ids_of[chunk], marks_of[chunk]
        weights = []
        for row in (2 * chunk, 2 * chunk + 1):
            live = jnp.where(row % blocks < counts_ref[user], 1.0, 0.0)
            weights.append(clicks_ref[row : row + 1, :].astype(F32) * live)
        weight = jnp.concatenate(weights, axis=1)
        earlier = earlier_of[chunk * owners : (chunk + 1) * owners]
        rank = jnp.sum(marks * (earlier + carry), axis=0, keepdims=True)
        carry = carry + (earlier[:, width - 1 :] + marks[:, width - 1 :])
        place = jnp.where(rank_iota == rank, 1.0, 0.0).astype(BF16)
        high = ((ids >> 7) & 15).astype(F32)
        low = (ids & 127).astype(F32)
        payload = jnp.concatenate(
            [marks * high, marks * low, marks * float(user), marks * weight], axis=0
        ).astype(BF16)
        lists = lists + lax.dot_general(payload, place, NT, preferred_element_type=F32)
    theta = exp_digamma_over(shape_ref[...], rate_ref[...])
    active = activity_base + jnp.sum(shape_ref[...] / rate_ref[...], axis=1, keepdims=True)
    theta_ref[...] = theta
    active_ref[...] = jnp.broadcast_to(active, theta.shape)
    item_line = lists[:owners] * float(LANES) + lists[owners : 2 * owners]
    lines = (item_line, lists[2 * owners : 3 * owners], lists[3 * owners :])
    for owner in range(owners):
        for part in range(3):
            line = lines[part][owner : owner + 1, :]
            send_ref[owner, 2 * part : 2 * part + 1, :] = line[:, :LANES]
            send_ref[owner, 2 * part + 1 : 2 * part + 2, :] = line[:, LANES:]
        send_ref[owner, 6:8, :] = jnp.zeros((2, LANES), F32)
        send_ref[owner, 8:16, :] = theta
    for copy in pack:
        copy.wait()


def table_kernel(shape_ref, rate_ref, table_ref, base_ref):
    shapes = shape_ref[...]
    table_ref[...] = exp_digamma_over(shapes, rate_ref[...])
    base_ref[...] = (1.0 - step_weight) * shapes + step_weight * item_prior


def widen(table):
    table_high, table_low = split(table)
    twice = jnp.concatenate([table_high, table_high], axis=1)
    return table_high, table_low, twice, jnp.concatenate([table_high, table_low], axis=1)


def ascend_block(theta_high, theta_both, marks, table):
    factors = table.shape[1]
    table_high, table_low, twice, both = widen(table)
    share = dot(theta_both, twice, NT) + dot(theta_high, table_low, NT)
    ratio_high, ratio_low = split(marks / share)
    wide = dot(ratio_high, both, NN)
    part = wide[:, :factors] + wide[:, factors:] + dot(ratio_low, table_high, NN)
    return ratio_high, ratio_low, part


def split_theta(theta):
    theta_high, theta_low = split(theta)
    return theta_high, jnp.concatenate([theta_high, theta_low], axis=1)


def ascend(theta, marks_ref, table_ref):
    theta_high, theta_both = split_theta(theta)
    total = jnp.zeros(theta.shape, F32)
    width = 2 * LANES
    for pair in range(marks_ref.shape[0] // 2):
        marks = jnp.concatenate([marks_ref[2 * pair], marks_ref[2 * pair + 1]], axis=1)
        table = table_ref[pair * width : (pair + 1) * width, :]
        total = total + ascend_block(theta_high, theta_both, marks, table)[2]
    return total


def build_kernel(recv_ref, table_ref, marks_ref, partial_ref):
    owners = recv_ref.shape[0]
    highs = marks_ref.shape[0]
    line_iota = lax.broadcasted_iota(jnp.int32, (LANES, 2 * LANES), 0).astype(F32)

    def wide(source, part):
        return jnp.concatenate(
            [recv_ref[source, 2 * part : 2 * part + 1, :], recv_ref[source, 2 * part + 1 : 2 * part + 2, :]],
            axis=1,
        )

    for source in range(owners):
        item = wide(source, 0).astype(jnp.int32)
        low = (item & (LANES - 1)).astype(F32)
        high = (item >> 7).astype(F32) * 8.0 + wide(source, 1)
        left = jnp.where(line_iota == high, wide(source, 2), 0.0).astype(BF16)
        right = jnp.where(line_iota == low, 1.0, 0.0).astype(BF16)
        tile = dot(left, right, NT)
        for high in range(highs):
            marks_ref[high, 8 * source : 8 * source + 8, :] = tile[8 * high : 8 * high + 8, :]
    theta = jnp.concatenate([recv_ref[source, 8:16, :] for source in range(owners)], axis=0)
    partial_ref[...] = ascend(theta, marks_ref, table_ref)


def ascend_kernel(theta_ref, marks_ref, table_ref, partial_ref):
    partial_ref[...] = ascend(theta_ref[...], marks_ref, table_ref)


def scale_kernel(shards, *refs):
    shard_refs = refs[:shards]
    rate_ref, scale_ref = refs[shards:]
    items = scale_ref.shape[0]
    width = 2 * LANES
    weight = jnp.concatenate([shard[:, items:] for shard in shard_refs], axis=0)
    for start in range(0, items, width):
        cov = jnp.concatenate([shard[:, start : start + width] for shard in shard_refs], axis=0)
        prior_log = lax.dot_general(weight, cov, TN, precision=HIGHEST, preferred_element_type=F32).T
        scale_ref[start : start + width, :] = jnp.exp(prior_log) / rate_ref[start : start + width, :]


def last_kernel(shards, spot_ref, theta_ref, marks_ref, table_ref, scale_ref, base_ref, *refs):
    shard_refs = refs[:shards]
    partial_ref, here_ref, keep_ref, send_ref, grad_ref, score_ref = refs[shards:]
    spot = spot_ref[2]
    theta = theta_ref[...]
    factors = theta.shape[1]
    theta_high, theta_both = split_theta(theta)
    total = jnp.zeros(theta.shape, F32)
    width = 2 * LANES
    for place in range(shards):
        block = spot ^ place
        here = pl.ds(pl.multiple_of(block * width, width), width)
        table = table_ref[here, :]
        marks = jnp.concatenate([marks_ref[2 * block], marks_ref[2 * block + 1]], axis=1)
        ratio_high, ratio_low, part = ascend_block(theta_high, theta_both, marks, table)
        total = total + part
        wide = dot(ratio_high, theta_both, TN)
        stats = table * (wide[:, :factors] + wide[:, factors:] + dot(ratio_low, theta_high, TN))
        (send_ref if place % 2 else keep_ref)[place // 2] = stats
        base = base_ref[here, :]
        if place == 0:
            here_ref[...] = base
        score = item_prior / shards - scale_ref[here, :] * (base / shards + step_weight * USER_RATIO * stats)
        score_ref[here, :] = jnp.concatenate(split(score), axis=1)
    partial_ref[...] = total
    rows = grad_ref.shape[1]
    group = 4
    items = score_ref.shape[0]
    for first in range(0, shards, group):
        cov = jnp.concatenate([shard[:, :items] for shard in shard_refs[first : first + group]], axis=0)
        cov_high, cov_low = split(cov)
        wide = dot(cov_high, score_ref[...], NN)
        grad = wide[:, :factors] + wide[:, factors:] + dot(cov_low, score_ref[:, :factors], NN)
        for place in range(group):
            grad_ref[spot ^ (first + place)] = grad[place * rows : (place + 1) * rows]


def halve_kernel(held_ref, recv_ref, keep_ref, send_ref):
    for place in range(held_ref.shape[0]):
        target = send_ref if place % 2 else keep_ref
        target[place // 2] = held_ref[place] + recv_ref[place]


def close_kernel(held_ref, recv_ref, base_ref, new_ref):
    new_ref[...] = base_ref[...] + step_weight * USER_RATIO * (held_ref[0] + recv_ref[0])


def update_kernel(activity_shape, recv_ref, theta_ref, activity_ref, totals_ref, active_ref, next_ref, send_ref):
    total = jnp.sum(recv_ref[...], axis=0)
    shapes = user_prior + theta_ref[...] * total
    rates = activity_shape / activity_ref[...] + totals_ref[...]
    active = activity_base + jnp.sum(shapes / rates, axis=1, keepdims=True)
    active_ref[...] = jnp.broadcast_to(active, shapes.shape)
    theta = exp_digamma_over(shapes, rates)
    next_ref[...] = theta
    send_ref[...] = jnp.broadcast_to(theta[None], send_ref.shape)


def join_kernel(grad_ref, partial_ref, send_ref):
    y_size, rows, _ = send_ref.shape
    grad = jnp.sum(grad_ref[...], axis=0)
    users = partial_ref.shape[0] // y_size
    for y in range(y_size):
        send_ref[y, :users, :] = partial_ref[y * users : (y + 1) * users, :]
        send_ref[y, users:, :] = grad


def fan_kernel(users, recv_ref, send_ref):
    z_size, rows, _ = send_ref.shape
    total = jnp.sum(recv_ref[...], axis=0)
    for z in range(z_size):
        send_ref[z, :users, :] = total[z * users : (z + 1) * users, :]
        send_ref[z, users:, :] = total[z_size * users :, :]


def finish_kernel(
    activity_shape, root, recv_ref, theta_ref, activity_ref, totals_ref, shapes_ref, rates_ref, active_ref, grad_ref
):
    total = jnp.sum(recv_ref[...], axis=0)
    users = shapes_ref.shape[0]
    shapes = user_prior + theta_ref[...] * total[:users]
    rates = activity_shape / activity_ref[...] + totals_ref[...]
    shapes_ref[...] = shapes
    rates_ref[...] = rates
    active = activity_base + jnp.sum(shapes / rates, axis=1, keepdims=True)
    eye = lax.broadcasted_iota(jnp.int32, shapes.shape, 0) == lax.broadcasted_iota(jnp.int32, shapes.shape, 1)
    row = jnp.sum(jnp.where(eye, active, 0.0), axis=0, keepdims=True)
    active_ref[...] = row[:, :users]
    grad_ref[...] = total[users:] / root


def shards(
    item_ids,
    clicks,
    block_counts,
    user_shape0,
    user_rate0,
    item_shape,
    item_rate,
    beta_totals,
    covariates,
    cov_weight,
):
    y_size, z_size = lax.axis_size("y"), lax.axis_size("z")
    owners = y_size * z_size
    item_rows, factors = item_shape.shape
    users_here, blocks, block_width = item_ids.shape
    cov_rows = covariates.shape[0]
    slot_rows = users_here * blocks
    highs = item_rows // LANES
    user_axes, item_axes = ("y", "z"), ("x", "core")
    split_count = lax.axis_size(item_axes)
    share_rows = item_rows // split_count
    everyone = owners * users_here
    activity_shape = activity_prior + factors * user_prior

    def exchange(array, axes):
        return lax.all_to_all(array, axes, split_axis=0, concat_axis=0, tiled=True)

    spot = jnp.stack([lax.axis_index("y"), lax.axis_index("z"), lax.axis_index(item_axes)]).astype(jnp.int32)
    totals = beta_totals[None, :]
    smem = pl.BlockSpec(memory_space=pltpu.SMEM)
    vmem = pl.BlockSpec(memory_space=pltpu.VMEM)
    hbm = pl.BlockSpec(memory_space=pl.ANY)
    small = shape_of(users_here, factors)
    share = shape_of(share_rows, factors)
    send, theta, active, own = kernel_call(
        functools.partial(prep_kernel, owners),
        (off_chip(owners, 16, LANES), small, small, off_chip(cov_rows, item_rows + factors)),
        in_specs=[hbm] * 7,
        scratch_shapes=[
            pltpu.SMEM((users_here,), jnp.int32),
            pltpu.VMEM((slot_rows, block_width), jnp.int32),
            pltpu.VMEM((slot_rows, block_width), jnp.int32),
            pltpu.VMEM((users_here, factors), F32),
            pltpu.VMEM((users_here, factors), F32),
            pltpu.SemaphoreType.DMA((7,)),
        ],
    )(
        away(block_counts),
        away(item_ids.reshape(slot_rows, block_width)),
        away(clicks.reshape(slot_rows, block_width)),
        away(user_shape0),
        away(user_rate0),
        away(covariates),
        away(cov_weight),
    )
    recv = exchange(send, user_axes)
    table, base = kernel_call(table_kernel, (on_chip(item_rows, factors), off_chip(item_rows, factors)))(
        item_shape, item_rate
    )
    table = stay(table)

    def swap(array, distance):
        axis, bit = ("core", 1) if distance == 1 else ("x", distance // 2)
        return lax.ppermute(array, axis, [(place, place ^ bit) for place in range(lax.axis_size(axis))])

    shards = [None] * split_count
    shards[0] = own
    for distance in (1, 2, 6, 4):
        shards[distance] = swap(own, distance)
    for distance in (2, 6, 4):
        shards[distance + 1] = swap(shards[distance], 1)

    marks, partial = kernel_call(
        build_kernel, (on_chip(highs, everyone, LANES), shape_of(everyone, factors))
    )(recv, table)
    marks = stay(marks)
    awaited = ()
    for iteration in range(ITERS - 1):
        parts = exchange(partial.reshape(owners, users_here, factors), user_axes)
        active, theta, spread = kernel_call(
            behind(functools.partial(update_kernel, activity_shape), 4, len(awaited)),
            (small, small, shape_of(owners, users_here, factors)),
            in_specs=[vmem] * 4 + [hbm] * len(awaited),
        )(parts, theta, active, totals, *awaited)
        theta_all = exchange(spread, user_axes).reshape(everyone, factors)
        if iteration == 0:
            awaited = [away(shards[place]) for place in (2, 6)]
            partial = kernel_call(
                behind(ascend_kernel, 3, len(awaited)),
                shape_of(everyone, factors),
                in_specs=[vmem] * 3 + [hbm] * len(awaited),
            )(theta_all, marks, table, *awaited)
            awaited = [away(shards[place]) for place in ()]
        else:
            scale = kernel_call(
                behind(functools.partial(scale_kernel, split_count), split_count + 1),
                off_chip(item_rows, factors),
                in_specs=[vmem] * (split_count + 1) + [hbm],
            )(*[away(shard) for shard in shards], away(item_rate), away(spread))
    half = split_count // 2
    partial, base, held, moved, grad = kernel_call(
        functools.partial(last_kernel, split_count),
        (
            shape_of(everyone, factors),
            shape_of(share_rows, factors),
            off_chip(half, share_rows, factors),
            off_chip(half, share_rows, factors),
            off_chip(split_count, cov_rows, factors),
        ),
        in_specs=[smem] + [vmem] * (5 + split_count),
        scratch_shapes=[pltpu.VMEM((item_rows, 2 * factors), BF16)],
    )(spot, theta_all, marks, table, away(scale), away(base), *[away(shard) for shard in shards])
    held = away(held)

    def halve(held, moved, *awaited):
        half = held.shape[0] // 2
        return kernel_call(
            behind(halve_kernel, 2, len(awaited)),
            (shape_of(half, share_rows, factors),) * 2,
            in_specs=[vmem] * 2 + [hbm] * len(awaited),
        )(held, moved, *awaited)

    grad = exchange(grad, item_axes)
    held, moved = halve(held, swap(moved, 1))
    both = kernel_call(
        behind(join_kernel, 2), shape_of(y_size, z_size * users_here + cov_rows, factors), in_specs=[vmem, vmem, hbm]
    )(grad, partial, moved)
    both = exchange(both, ("y",))
    moved = swap(moved, 2)
    both = kernel_call(
        behind(functools.partial(fan_kernel, users_here), 1),
        off_chip(z_size, users_here + cov_rows, factors),
        in_specs=[vmem, hbm],
    )(both, moved)
    held, moved = halve(held, moved, away(both))
    both = exchange(both, ("z",))
    new_shape = kernel_call(close_kernel, share)(held, swap(moved, 4), base)
    user_shape, user_rate, active, cov_grad = kernel_call(
        functools.partial(finish_kernel, activity_shape, math.sqrt(item_rows * owners)),
        (small, small, shape_of(1, users_here), shape_of(cov_rows, factors)),
    )(both, theta, active, totals)
    return (user_shape, user_rate, active.reshape(users_here), new_shape, cov_grad)


def solution(mesh):
    fine = Mesh(mesh.devices.reshape(4, 8, 4, 2), ("y", "z", "x", "core"))
    users, items = ("y", "z"), ("x", "core")
    both = users + items
    return jax.shard_map(
        shards,
        mesh=fine,
        in_specs=(
            P(both, None, None),
            P(both, None, None),
            P(both),
            P(both, None),
            P(both, None),
            P(users, None),
            P(users, None),
            P(),
            P(items, users),
            P(items, None),
        ),
        out_specs=(
            P(both, None),
            P(both, None),
            P(both),
            P(both, None),
            P(items, None),
        ),
        check_vma=False,
    )
```

```python
import functools
import math

import jax
import jax.numpy as jnp
from jax import lax
from jax.experimental import pallas as pl
from jax.experimental.pallas import tpu as pltpu
from jax.sharding import Mesh
from jax.sharding import PartitionSpec as P

ITERS = 3
USER_RATIO = 4

user_prior = 0.3
activity_prior = 0.3
activity_base = 1.0
item_prior = 0.3
step_weight = 0.5

F32 = jnp.float32
BF16 = jnp.bfloat16
HIGHEST = lax.Precision.HIGHEST
NT = (((1,), (1,)), ((), ()))
NN = (((1,), (0,)), ((), ()))
TN = (((0,), (0,)), ((), ()))
LANES = 128
VMEM_LIMIT = 32 * 1024 * 1024


def exp_digamma_over(x, rate):
    pair = x * (x + 5.0)
    low = pair + 4.0
    high = pair + 6.0
    steps = (2.0 * x + 5.0) * (low * high + pair * (low + high)) / (pair * low * high)
    y = x + 6.0
    inv = 1.0 / y
    sq = inv * inv
    tail = 0.5 * inv + sq * (1.0 / 12.0 - sq * (1.0 / 120.0 - sq * (1.0 / 252.0)))
    return y * jnp.exp(-steps - tail) / rate


def kernel_call(kernel, out_shape, **specs):
    return pl.pallas_call(
        kernel,
        out_shape=out_shape,
        compiler_params=pltpu.CompilerParams(vmem_limit_bytes=VMEM_LIMIT),
        **specs,
    )


def behind(kernel, inputs, awaited=1):
    def wrapped(*refs):
        kernel(*refs[:inputs], *refs[inputs + awaited :])

    return wrapped


def shape_of(*dims):
    return jax.ShapeDtypeStruct(dims, F32)


def on_chip(*dims):
    return pltpu.VMEM(dims, F32)


def off_chip(*dims):
    return pltpu.HBM(dims, F32)


def stay(array):
    return pltpu.with_memory_space_constraint(array, pltpu.VMEM)


def away(array):
    return pltpu.with_memory_space_constraint(array, pltpu.HBM)


def split(x):
    high = x.astype(BF16)
    return high, (x - high.astype(F32)).astype(BF16)


def dot(left, right, dims):
    return lax.dot_general(left, right, dims, preferred_element_type=F32)


def prep_kernel(
    owners,
    counts_hbm,
    ids_hbm,
    clicks_hbm,
    shape_hbm,
    rate_hbm,
    cov_hbm,
    weight_hbm,
    send_ref,
    theta_ref,
    active_ref,
    own_ref,
    counts_ref,
    ids_ref,
    clicks_ref,
    shape_ref,
    rate_ref,
    sems,
):
    copies = [
        pltpu.make_async_copy(source, target, sems.at[place])
        for place, (source, target) in enumerate(
            (
                (counts_hbm, counts_ref),
                (ids_hbm, ids_ref),
                (clicks_hbm, clicks_ref),
                (shape_hbm, shape_ref),
                (rate_hbm, rate_ref),
            )
        )
    ]
    items = cov_hbm.shape[1]
    pack = [
        pltpu.make_async_copy(cov_hbm, own_ref.at[:, pl.ds(0, items)], sems.at[len(copies)]),
        pltpu.make_async_copy(
            weight_hbm, own_ref.at[:, pl.ds(items, weight_hbm.shape[1])], sems.at[len(copies) + 1]
        ),
    ]
    for copy in copies + pack:
        copy.start()
    for copy in copies:
        copy.wait()
    rows = ids_ref.shape[0]
    blocks = 8
    width = 2 * LANES
    capacity = rows * LANES // owners
    before = (
        lax.broadcasted_iota(jnp.int32, (width, width), 0)
        < lax.broadcasted_iota(jnp.int32, (width, width), 1)
    )
    before = jnp.where(before, 1.0, 0.0).astype(BF16)
    owner_iota = lax.broadcasted_iota(jnp.int32, (owners, width), 0)
    rank_iota = lax.broadcasted_iota(jnp.int32, (capacity, width), 0).astype(F32)
    chunks = rows // 2
    ids_of, marks_of = [], []
    for chunk in range(chunks):
        ids = jnp.concatenate(
            [ids_ref[2 * chunk : 2 * chunk + 1, :], ids_ref[2 * chunk + 1 : 2 * chunk + 2, :]], axis=1
        )
        ids_of.append(ids)
        marks_of.append(jnp.where(owner_iota == (ids >> 11), 1.0, 0.0))
    earlier_of = dot(jnp.concatenate([marks.astype(BF16) for marks in marks_of], axis=0), before, NN)
    carry = jnp.zeros((owners, 1), F32)
    lists = jnp.zeros((4 * owners, capacity), F32)
    for chunk in range(chunks):
        user = 2 * chunk // blocks
        ids, marks = ids_of[chunk], marks_of[chunk]
        weights = []
        for row in (2 * chunk, 2 * chunk + 1):
            live = jnp.where(row % blocks < counts_ref[user], 1.0, 0.0)
            weights.append(clicks_ref[row : row + 1, :].astype(F32) * live)
        weight = jnp.concatenate(weights, axis=1)
        earlier = earlier_of[chunk * owners : (chunk + 1) * owners]
        rank = jnp.sum(marks * (earlier + carry), axis=0, keepdims=True)
        carry = carry + (earlier[:, width - 1 :] + marks[:, width - 1 :])
        place = jnp.where(rank_iota == rank, 1.0, 0.0).astype(BF16)
        high = ((ids >> 7) & 15).astype(F32)
        low = (ids & 127).astype(F32)
        payload = jnp.concatenate(
            [marks * high, marks * low, marks * float(user), marks * weight], axis=0
        ).astype(BF16)
        lists = lists + lax.dot_general(payload, place, NT, preferred_element_type=F32)
    theta = exp_digamma_over(shape_ref[...], rate_ref[...])
    active = activity_base + jnp.sum(shape_ref[...] / rate_ref[...], axis=1, keepdims=True)
    theta_ref[...] = theta
    active_ref[...] = jnp.broadcast_to(active, theta.shape)
    item_line = lists[:owners] * float(LANES) + lists[owners : 2 * owners]
    lines = (item_line, lists[2 * owners : 3 * owners], lists[3 * owners :])
    for owner in range(owners):
        for part in range(3):
            line = lines[part][owner : owner + 1, :]
            send_ref[owner, 2 * part : 2 * part + 1, :] = line[:, :LANES]
            send_ref[owner, 2 * part + 1 : 2 * part + 2, :] = line[:, LANES:]
        send_ref[owner, 6:8, :] = jnp.zeros((2, LANES), F32)
        send_ref[owner, 8:16, :] = theta
    for copy in pack:
        copy.wait()


def table_kernel(shape_ref, rate_ref, table_ref):
    table_ref[...] = exp_digamma_over(shape_ref[...], rate_ref[...])


def widen(table):
    table_high, table_low = split(table)
    twice = jnp.concatenate([table_high, table_high], axis=1)
    return table_high, table_low, twice, jnp.concatenate([table_high, table_low], axis=1)


def ascend_block(theta_high, theta_both, marks, table):
    factors = table.shape[1]
    table_high, table_low, twice, both = widen(table)
    share = dot(theta_both, twice, NT) + dot(theta_high, table_low, NT)
    ratio_high, ratio_low = split(marks / share)
    wide = dot(ratio_high, both, NN)
    part = wide[:, :factors] + wide[:, factors:] + dot(ratio_low, table_high, NN)
    return ratio_high, ratio_low, part


def split_theta(theta):
    theta_high, theta_low = split(theta)
    return theta_high, jnp.concatenate([theta_high, theta_low], axis=1)


def ascend(theta, marks_ref, table_ref):
    theta_high, theta_both = split_theta(theta)
    total = jnp.zeros(theta.shape, F32)
    width = 2 * LANES
    for pair in range(marks_ref.shape[0] // 2):
        marks = jnp.concatenate([marks_ref[2 * pair], marks_ref[2 * pair + 1]], axis=1)
        table = table_ref[pair * width : (pair + 1) * width, :]
        total = total + ascend_block(theta_high, theta_both, marks, table)[2]
    return total


def build_kernel(recv_ref, table_ref, marks_ref, partial_ref):
    owners = recv_ref.shape[0]
    highs = marks_ref.shape[0]
    line_iota = lax.broadcasted_iota(jnp.int32, (LANES, 2 * LANES), 0).astype(F32)

    def wide(source, part):
        return jnp.concatenate(
            [recv_ref[source, 2 * part : 2 * part + 1, :], recv_ref[source, 2 * part + 1 : 2 * part + 2, :]],
            axis=1,
        )

    for source in range(owners):
        item = wide(source, 0).astype(jnp.int32)
        low = (item & (LANES - 1)).astype(F32)
        high = (item >> 7).astype(F32) * 8.0 + wide(source, 1)
        left = jnp.where(line_iota == high, wide(source, 2), 0.0).astype(BF16)
        right = jnp.where(line_iota == low, 1.0, 0.0).astype(BF16)
        tile = dot(left, right, NT)
        for high in range(highs):
            marks_ref[high, 8 * source : 8 * source + 8, :] = tile[8 * high : 8 * high + 8, :]
    theta = jnp.concatenate([recv_ref[source, 8:16, :] for source in range(owners)], axis=0)
    partial_ref[...] = ascend(theta, marks_ref, table_ref)


def ascend_kernel(theta_ref, marks_ref, table_ref, partial_ref):
    partial_ref[...] = ascend(theta_ref[...], marks_ref, table_ref)


def scale_kernel(shards, *refs):
    shard_refs = refs[:shards]
    rate_ref, scale_ref = refs[shards:]
    items = scale_ref.shape[0]
    width = 2 * LANES
    weight = jnp.concatenate([shard[:, items:] for shard in shard_refs], axis=0)
    for start in range(0, items, width):
        cov = jnp.concatenate([shard[:, start : start + width] for shard in shard_refs], axis=0)
        prior_log = lax.dot_general(weight, cov, TN, precision=HIGHEST, preferred_element_type=F32).T
        scale_ref[start : start + width, :] = jnp.exp(prior_log) / rate_ref[start : start + width, :]


def last_kernel(shards, spot_ref, theta_ref, marks_ref, table_ref, scale_ref, shape_ref, *refs):
    shard_refs = refs[:shards]
    partial_ref, here_ref, keep_ref, send_ref, grad_ref, score_ref = refs[shards:]
    spot = spot_ref[2]
    theta = theta_ref[...]
    factors = theta.shape[1]
    theta_high, theta_both = split_theta(theta)
    total = jnp.zeros(theta.shape, F32)
    width = 2 * LANES
    for place in range(shards):
        block = spot ^ place
        here = pl.ds(pl.multiple_of(block * width, width), width)
        table = table_ref[here, :]
        marks = jnp.concatenate([marks_ref[2 * block], marks_ref[2 * block + 1]], axis=1)
        ratio_high, ratio_low, part = ascend_block(theta_high, theta_both, marks, table)
        total = total + part
        wide = dot(ratio_high, theta_both, TN)
        stats = table * (wide[:, :factors] + wide[:, factors:] + dot(ratio_low, theta_high, TN))
        (send_ref if place % 2 else keep_ref)[place // 2] = stats
        base = (1.0 - step_weight) * shape_ref[here, :] + step_weight * item_prior
        if place == 0:
            here_ref[...] = base
        score = item_prior / shards - scale_ref[here, :] * (base / shards + step_weight * USER_RATIO * stats)
        score_ref[here, :] = jnp.concatenate(split(score), axis=1)
    partial_ref[...] = total
    rows = grad_ref.shape[1]
    group = shards
    items = score_ref.shape[0]
    for first in range(0, shards, group):
        cov = jnp.concatenate([shard[:, :items] for shard in shard_refs[first : first + group]], axis=0)
        cov_high, cov_low = split(cov)
        wide = dot(cov_high, score_ref[...], NN)
        grad = wide[:, :factors] + wide[:, factors:] + dot(cov_low, score_ref[:, :factors], NN)
        for place in range(group):
            grad_ref[spot ^ (first + place)] = grad[place * rows : (place + 1) * rows]


def halve_kernel(held_ref, recv_ref, keep_ref, send_ref):
    for place in range(held_ref.shape[0]):
        target = send_ref if place % 2 else keep_ref
        target[place // 2] = held_ref[place] + recv_ref[place]


def close_kernel(held_ref, recv_ref, base_ref, new_ref):
    new_ref[...] = base_ref[...] + step_weight * USER_RATIO * (held_ref[0] + recv_ref[0])


def update_kernel(activity_shape, recv_ref, theta_ref, activity_ref, totals_ref, active_ref, next_ref, send_ref):
    total = jnp.sum(recv_ref[...], axis=0)
    shapes = user_prior + theta_ref[...] * total
    rates = activity_shape / activity_ref[...] + totals_ref[...]
    active = activity_base + jnp.sum(shapes / rates, axis=1, keepdims=True)
    active_ref[...] = jnp.broadcast_to(active, shapes.shape)
    theta = exp_digamma_over(shapes, rates)
    next_ref[...] = theta
    send_ref[...] = jnp.broadcast_to(theta[None], send_ref.shape)


def join_kernel(grad_ref, partial_ref, send_ref):
    y_size, rows, _ = send_ref.shape
    grad = jnp.sum(grad_ref[...], axis=0)
    users = partial_ref.shape[0] // y_size
    for y in range(y_size):
        send_ref[y, :users, :] = partial_ref[y * users : (y + 1) * users, :]
        send_ref[y, users:, :] = grad


def fan_kernel(users, recv_ref, send_ref):
    z_size, rows, _ = send_ref.shape
    total = jnp.sum(recv_ref[...], axis=0)
    for z in range(z_size):
        send_ref[z, :users, :] = total[z * users : (z + 1) * users, :]
        send_ref[z, users:, :] = total[z_size * users :, :]


def finish_kernel(
    activity_shape, root, recv_ref, theta_ref, activity_ref, totals_ref, shapes_ref, rates_ref, active_ref, grad_ref
):
    total = jnp.sum(recv_ref[...], axis=0)
    users = shapes_ref.shape[0]
    shapes = user_prior + theta_ref[...] * total[:users]
    rates = activity_shape / activity_ref[...] + totals_ref[...]
    shapes_ref[...] = shapes
    rates_ref[...] = rates
    active = activity_base + jnp.sum(shapes / rates, axis=1, keepdims=True)
    eye = lax.broadcasted_iota(jnp.int32, shapes.shape, 0) == lax.broadcasted_iota(jnp.int32, shapes.shape, 1)
    row = jnp.sum(jnp.where(eye, active, 0.0), axis=0, keepdims=True)
    active_ref[...] = row[:, :users]
    grad_ref[...] = total[users:] / root


def shards(
    item_ids,
    clicks,
    block_counts,
    user_shape0,
    user_rate0,
    item_shape,
    item_rate,
    beta_totals,
    covariates,
    cov_weight,
):
    y_size, z_size = lax.axis_size("y"), lax.axis_size("z")
    owners = y_size * z_size
    item_rows, factors = item_shape.shape
    users_here, blocks, block_width = item_ids.shape
    cov_rows = covariates.shape[0]
    slot_rows = users_here * blocks
    highs = item_rows // LANES
    user_axes, item_axes = ("y", "z"), ("x", "core")
    split_count = lax.axis_size(item_axes)
    share_rows = item_rows // split_count
    everyone = owners * users_here
    activity_shape = activity_prior + factors * user_prior

    def exchange(array, axes):
        return lax.all_to_all(array, axes, split_axis=0, concat_axis=0, tiled=True)

    spot = jnp.stack([lax.axis_index("y"), lax.axis_index("z"), lax.axis_index(item_axes)]).astype(jnp.int32)
    totals = beta_totals[None, :]
    smem = pl.BlockSpec(memory_space=pltpu.SMEM)
    vmem = pl.BlockSpec(memory_space=pltpu.VMEM)
    hbm = pl.BlockSpec(memory_space=pl.ANY)
    small = shape_of(users_here, factors)
    share = shape_of(share_rows, factors)
    send, theta, active, own = kernel_call(
        functools.partial(prep_kernel, owners),
        (off_chip(owners, 16, LANES), small, small, off_chip(cov_rows, item_rows + factors)),
        in_specs=[hbm] * 7,
        scratch_shapes=[
            pltpu.SMEM((users_here,), jnp.int32),
            pltpu.VMEM((slot_rows, block_width), jnp.int32),
            pltpu.VMEM((slot_rows, block_width), jnp.int32),
            pltpu.VMEM((users_here, factors), F32),
            pltpu.VMEM((users_here, factors), F32),
            pltpu.SemaphoreType.DMA((7,)),
        ],
    )(
        away(block_counts),
        away(item_ids.reshape(slot_rows, block_width)),
        away(clicks.reshape(slot_rows, block_width)),
        away(user_shape0),
        away(user_rate0),
        away(covariates),
        away(cov_weight),
    )
    recv = exchange(send, user_axes)
    table = kernel_call(table_kernel, on_chip(item_rows, factors))(item_shape, item_rate)
    table = stay(table)

    def swap(array, distance):
        axis, bit = ("core", 1) if distance == 1 else ("x", distance // 2)
        return lax.ppermute(array, axis, [(place, place ^ bit) for place in range(lax.axis_size(axis))])

    shards = [None] * split_count
    shards[0] = own
    for distance in (1, 2, 6, 4):
        shards[distance] = swap(own, distance)
    for distance in (2, 6, 4):
        shards[distance + 1] = swap(shards[distance], 1)

    marks, partial = kernel_call(
        build_kernel, (on_chip(highs, everyone, LANES), shape_of(everyone, factors))
    )(recv, table)
    marks = stay(marks)
    awaited = ()
    for iteration in range(ITERS - 1):
        parts = exchange(partial.reshape(owners, users_here, factors), user_axes)
        active, theta, spread = kernel_call(
            behind(functools.partial(update_kernel, activity_shape), 4, len(awaited)),
            (small, small, shape_of(owners, users_here, factors)),
            in_specs=[vmem] * 4 + [hbm] * len(awaited),
        )(parts, theta, active, totals, *awaited)
        theta_all = exchange(spread, user_axes).reshape(everyone, factors)
        if iteration == 0:
            awaited = [away(shards[place]) for place in (2, 6)]
            partial = kernel_call(
                behind(ascend_kernel, 3, len(awaited)),
                shape_of(everyone, factors),
                in_specs=[vmem] * 3 + [hbm] * len(awaited),
            )(theta_all, marks, table, *awaited)
            awaited = [away(shards[place]) for place in ()]
        else:
            scale = kernel_call(
                behind(functools.partial(scale_kernel, split_count), split_count + 1),
                off_chip(item_rows, factors),
                in_specs=[vmem] * (split_count + 1) + [hbm],
            )(*[away(shard) for shard in shards], away(item_rate), away(spread))
    half = split_count // 2
    partial, base, held, moved, grad = kernel_call(
        functools.partial(last_kernel, split_count),
        (
            shape_of(everyone, factors),
            shape_of(share_rows, factors),
            off_chip(half, share_rows, factors),
            off_chip(half, share_rows, factors),
            off_chip(split_count, cov_rows, factors),
        ),
        in_specs=[smem] + [vmem] * (5 + split_count),
        scratch_shapes=[pltpu.VMEM((item_rows, 2 * factors), BF16)],
    )(spot, theta_all, marks, table, away(scale), away(item_shape), *[away(shard) for shard in shards])
    held = away(held)

    def halve(held, moved, *awaited):
        half = held.shape[0] // 2
        return kernel_call(
            behind(halve_kernel, 2, len(awaited)),
            (shape_of(half, share_rows, factors),) * 2,
            in_specs=[vmem] * 2 + [hbm] * len(awaited),
        )(held, moved, *awaited)

    grad = exchange(grad, item_axes)
    held, moved = halve(held, swap(moved, 1))
    both = kernel_call(
        behind(join_kernel, 2), shape_of(y_size, z_size * users_here + cov_rows, factors), in_specs=[vmem, vmem, hbm]
    )(grad, partial, moved)
    both = exchange(both, ("y",))
    moved = swap(moved, 2)
    both = kernel_call(
        behind(functools.partial(fan_kernel, users_here), 1),
        off_chip(z_size, users_here + cov_rows, factors),
        in_specs=[vmem, hbm],
    )(both, moved)
    held, moved = halve(held, moved, away(both))
    both = exchange(both, ("z",))
    new_shape = kernel_call(close_kernel, share)(held, swap(moved, 4), base)
    user_shape, user_rate, active, cov_grad = kernel_call(
        functools.partial(finish_kernel, activity_shape, math.sqrt(item_rows * owners)),
        (small, small, shape_of(1, users_here), shape_of(cov_rows, factors)),
    )(both, theta, active, totals)
    return (user_shape, user_rate, active.reshape(users_here), new_shape, cov_grad)


def solution(mesh):
    fine = Mesh(mesh.devices.reshape(4, 8, 4, 2), ("y", "z", "x", "core"))
    users, items = ("y", "z"), ("x", "core")
    both = users + items
    return jax.shard_map(
        shards,
        mesh=fine,
        in_specs=(
            P(both, None, None),
            P(both, None, None),
            P(both),
            P(both, None),
            P(both, None),
            P(users, None),
            P(users, None),
            P(),
            P(items, users),
            P(items, None),
        ),
        out_specs=(
            P(both, None),
            P(both, None),
            P(both),
            P(both, None),
            P(items, None),
        ),
        check_vma=False,
    )
```
